32 devices in a mesh: dp: 8 (over z, x), seq: 4 (over y, core).
Axes of the slice: x: 2, y: 2, z: 4, core: 2. Of those that a mesh axis runs over, the one named last changes fastest.
Arguments:
- tokens: bfloat16 [88, 360, 768], P('dp', 'seq'), may hold values from -6 to 6
- key_mask: int32 [88, 360], P('dp'), may hold values from 0 to 1, as said below
- row_split: int32 [88, 4], P('dp'), may hold values from 4 to 5, as said below
- group_tags: int32 [88], P('dp'), may hold values from 0 to 8, as said below
- norm1_gain: bfloat16 [768], replicated, may hold values from 0.5 to 1.5
- norm1_shift: bfloat16 [768], replicated, may hold values from -1.796875 to 1.796875
- qkv_weight: bfloat16 [768, 2304], replicated, may hold values from -0.21875 to 0.21875
- query_bias: bfloat16 [768], replicated, may hold values from -1.796875 to 1.796875
- value_bias: bfloat16 [768], replicated, may hold values from -1.796875 to 1.796875
- out_weight: bfloat16 [768, 768], replicated, may hold values from -0.875 to 0.875
- out_bias: bfloat16 [768], replicated, may hold values from -1.796875 to 1.796875
- norm2_gain: bfloat16 [768], replicated, may hold values from 0.5 to 1.5
- norm2_shift: bfloat16 [768], replicated, may hold values from -1.796875 to 1.796875
- fc1_weight: bfloat16 [768, 3072], replicated, may hold values from -0.21875 to 0.21875
- fc1_bias: bfloat16 [3072], replicated, may hold values from -1.796875 to 1.796875
- fc2_weight: bfloat16 [3072, 768], replicated, may hold values from -0.109375 to 0.109375
- fc2_bias: bfloat16 [768], replicated, may hold values from -1.796875 to 1.796875
- out_cotangent: bfloat16 [88, 360, 768], P('dp', 'seq'), may hold values from -6 to 6
Outputs:
- output: bfloat16 [88, 360, 768], P('dp', 'seq')
- input_grad: bfloat16 [88, 360, 768], P('dp', 'seq')
- norm1_gain_grad: float32 [768], P(('dp', 'seq'))
- norm1_shift_grad: float32 [768], P(('dp', 'seq'))
- qkv_weight_grad: float32 [768, 2304], P(None, ('dp', 'seq'))
- query_bias_grad: float32 [768], P(('dp', 'seq'))
- value_bias_grad: float32 [768], P(('dp', 'seq'))
- out_weight_grad: float32 [768, 768], P(None, ('dp', 'seq'))
- out_bias_grad: float32 [768], P(('dp', 'seq'))
- norm2_gain_grad: float32 [768], P(('dp', 'seq'))
- norm2_shift_grad: float32 [768], P(('dp', 'seq'))
- fc1_weight_grad: float32 [768, 3072], P(None, ('dp', 'seq'))
- fc1_bias_grad: float32 [3072], P(('dp', 'seq'))
- fc2_weight_grad: float32 [3072, 768], P(None, ('dp', 'seq'))
- fc2_bias_grad: float32 [768], P(('dp', 'seq'))
The draws below stay inside these ranges and needn't reach their ends.
Inputs may be any that keep to these rules, and one draw needn't show every extreme that they name: `row_split`: each image's rows sum to 18; every index of seq holds 4 or one more rows, and which indices hold one more differs from image to image. key_mask is 0 on every slot beyond an index's live rows; the first slot of every index of seq is 1 for every image. `group_tags`: the image slots on index g of dp carry tag g or 8; the number of tagged slots differs from index to index, and in every draw one index has all 11 slots tagged.
All inputs are finite; a program needn't handle non-finite values.
Results may differ from the reference program's by a relative error of at most 0.015.
Values may be sent and summed in bfloat16 or wider, within the bound.
No kernel may reach another device: no remote copies, remote signals or barrier semaphores. Data moves between devices by JAX's collectives and lax.ppermute only.
A program may use at most 192 MiB of HBM per device.

```python
import jax
import jax.numpy as jnp
from jax import lax

D = 768
HEADS = 12
FF = 3072
GRID = 18
IMG_DEV = 11
SLOTS = 90
KEYS = 360
IMAGES = 88
N_DP = 8
N_SEQ = 4


def split_rows(key):
    base_rows = GRID // N_SEQ
    extra_rows = GRID % N_SEQ
    image_keys = jax.random.split(key, IMAGES)

    def one_order(image_key):
        return jax.random.permutation(image_key, N_SEQ)
    orders = jax.vmap(one_order)(image_keys)
    return (base_rows + (orders < extra_rows).astype(jnp.int32)).astype(jnp.int32)


def draw_row_split(key, part):
    rows_each = split_rows(key)
    return rows_each


def draw_key_mask(key, part):
    rows_each = split_rows(key)
    key = jax.random.fold_in(key, 5)
    slot_index = jnp.arange(KEYS, dtype=jnp.int32)
    slot_local = slot_index % SLOTS
    rows_at = rows_each[:, slot_index // SLOTS]
    inside = slot_local[None, :] < rows_at * GRID
    chosen = jax.random.randint(key, (IMAGES, KEYS), 0, 4) > 0
    kept = chosen | (slot_local == 0)[None, :]
    return (inside & kept).astype(jnp.int32)


def draw_group_tags(key, part):
    key = jax.random.fold_in(key, 9)
    count_key, full_key, order_key = jax.random.split(key, 3)
    least = max(1, IMG_DEV // 4)
    device = jnp.arange(N_DP, dtype=jnp.int32)
    counts = jax.random.randint(count_key, (N_DP,), least, IMG_DEV + 1)
    full_slot = jax.random.randint(full_key, (), 0, N_DP)
    counts = jnp.where(device == (full_slot + 1) % N_DP, least, counts)
    counts = jnp.where(device == full_slot, IMG_DEV, counts)

    def one_order(device_key):
        return jax.random.permutation(device_key, IMG_DEV)
    orders = jax.vmap(one_order)(jax.random.split(order_key, N_DP))
    tagged = jnp.where(orders < counts[:, None], device[:, None], N_DP)
    return tagged.reshape(IMAGES).astype(jnp.int32)


def block_scale(rng, dims, pieces, smallest, high):
    def one(dim, parts):
        steps = jax.random.uniform(jax.random.fold_in(jax.random.fold_in(rng, 6), dim), (parts,), jnp.float32, smallest / len(pieces), high / len(pieces))
        return jnp.repeat(jnp.exp(steps), dims[dim] // parts).reshape((-1,) + (1,) * (len(dims) - dim - 1))

    loudness = one(*pieces[0])
    for cut in pieces[1:]:
        loudness = loudness * one(*cut)
    return loudness


def noise(own_key, shape, scale, bound, pieces=(), held_as=jnp.bfloat16):
    result = scale * jax.random.normal(own_key, shape, jnp.float32)
    if pieces:
        result = result * block_scale(own_key, shape, pieces, -0.22, 0.18)
    return jnp.clip(result, -bound, bound).astype(held_as)


def setup_inputs(seed: int = 0) -> dict:
    key_of = jax.random.split(jax.random.key(seed), 19)
    return {
        "tokens": noise(key_of[0], (IMAGES, KEYS, D), 1.0, 6.0, ((0, 8), (1, 4))),
        "key_mask": draw_key_mask(jax.random.fold_in(key_of[18], 71), 0),
        "row_split": draw_row_split(jax.random.fold_in(key_of[18], 71), 0),
        "group_tags": draw_group_tags(jax.random.fold_in(key_of[18], 71), 0),
        "norm1_gain": jnp.clip(1.0 + 0.1 * jax.random.normal(key_of[4], (D,), jnp.float32), 0.5, 1.5).astype(jnp.bfloat16),
        "norm1_shift": noise(key_of[5], (D,), 0.3, 1.796875),
        "qkv_weight": noise(key_of[6], (D, 3 * D), D ** -0.5, 0.21875),
        "query_bias": noise(key_of[7], (D,), 0.3, 1.796875),
        "value_bias": noise(key_of[8], (D,), 0.3, 1.796875),
        "out_weight": noise(key_of[9], (D, D), (D // 16) ** -0.5, 0.875),
        "out_bias": noise(key_of[10], (D,), 0.3, 1.796875),
        "norm2_gain": jnp.clip(1.0 + 0.1 * jax.random.normal(key_of[11], (D,), jnp.float32), 0.5, 1.5).astype(jnp.bfloat16),
        "norm2_shift": noise(key_of[12], (D,), 0.3, 1.796875),
        "fc1_weight": noise(key_of[13], (D, FF), D ** -0.5, 0.21875),
        "fc1_bias": noise(key_of[14], (FF,), 0.3, 1.796875),
        "fc2_weight": noise(key_of[15], (FF, D), FF ** -0.5, 0.109375),
        "fc2_bias": noise(key_of[16], (D,), 0.3, 1.796875),
        "out_cotangent": noise(key_of[17], (IMAGES, KEYS, D), 1.0, 6.0, ((0, 8), (1, 4))),
    }


EPS = 1e-06
NEG = -1e+30
HIGH = lax.Precision.HIGHEST

@jax.custom_vjp
def low(v):
    return lax.optimization_barrier(v.astype(jnp.bfloat16)).astype(jnp.float32)

@jax.custom_vjp
def low_back(v):
    return v

def low_keep(v):
    return (low(v), None)

def low_pass(kept, grad):
    return (grad,)

def back_keep(v):
    return (v, None)

def back_low(kept, grad):
    return (low(grad),)
low.defvjp(low_keep, low_pass)
low_back.defvjp(back_keep, back_low)

def norm_rows(values, gain, shift):
    row_mean = lax.optimization_barrier(jnp.mean(values, -1, keepdims=True))
    centered = values - row_mean
    variance = lax.optimization_barrier(jnp.mean(centered * centered, -1, keepdims=True))
    return centered * lax.rsqrt(variance + EPS) * gain + shift

def matmul(first, second):
    return jnp.einsum('bsd,de->bse', first, second, precision=HIGH)

def block_forward(params, inputs, key_valid, row_live):
    norm1_gain, norm1_shift, qkv_weight, query_bias, value_bias, out_weight, out_bias, norm2_gain, norm2_shift, fc1_weight, fc1_bias, fc2_weight, fc2_bias = params
    blocks, length, width = inputs.shape
    head_dim = width // HEADS
    normed = low(norm_rows(inputs, norm1_gain, norm1_shift))
    projected = matmul(normed, qkv_weight)
    queries = low(low_back(projected[..., :width] + query_bias))
    keys_all = low(low_back(projected[..., width:2 * width]))
    values = low(low_back(projected[..., 2 * width:] + value_bias))
    query_heads = queries.reshape(blocks, length, HEADS, head_dim)
    key_heads = keys_all.reshape(blocks, length, HEADS, head_dim)
    value_heads = values.reshape(blocks, length, HEADS, head_dim)
    scores = jnp.einsum('bqhe,bkhe->bhqk', query_heads, key_heads, precision=HIGH) * head_dim ** (-0.5)
    scores = low_back(scores)
    valid = key_valid[:, None, None, :]
    row_top = lax.optimization_barrier(jnp.max(jnp.where(valid, scores, NEG), -1, keepdims=True))
    exp_terms = jnp.where(valid, jnp.exp(scores - row_top), 0.0)
    weights_low = low(exp_terms / lax.optimization_barrier(jnp.sum(exp_terms, -1, keepdims=True)))
    mixed = jnp.einsum('bhqk,bkhe->bqhe', weights_low, value_heads, precision=HIGH)
    mixed = low(low_back(mixed.reshape(blocks, length, width)))
    attended = low_back(matmul(mixed, out_weight) + out_bias)
    hidden = inputs + row_live[..., None] * attended
    normed2 = low(norm_rows(hidden, norm2_gain, norm2_shift))
    expanded = low_back(matmul(normed2, fc1_weight) + fc1_bias)
    activated = low(low_back(jax.nn.gelu(expanded, approximate=False)))
    reduced = low_back(matmul(activated, fc2_weight) + fc2_bias)
    return hidden + row_live[..., None] * reduced

def reference(tokens, key_mask, row_split, group_tags, norm1_gain, norm1_shift, qkv_weight, query_bias, value_bias, out_weight, out_bias, norm2_gain, norm2_shift, fc1_weight, fc1_bias, fc2_weight, fc2_bias, out_cotangent):
    slot_index = jnp.arange(KEYS, dtype=jnp.int32)
    slot_rank = slot_index // SLOTS
    slot_local = slot_index % SLOTS
    rows_here = row_split[:, slot_rank]
    row_live = ((slot_local[None, :] < rows_here * GRID) & (group_tags < N_DP)[:, None]).astype(jnp.float32)
    key_valid = key_mask > 0
    params = tuple((weight_arg.astype(jnp.float32) for weight_arg in (norm1_gain, norm1_shift, qkv_weight, query_bias, value_bias, out_weight, out_bias, norm2_gain, norm2_shift, fc1_weight, fc1_bias, fc2_weight, fc2_bias)))

    def forward_all(inputs, params):

        def one_block(block_args):
            return block_forward(params, block_args[0], block_args[1], block_args[2])
        shaped = (inputs.reshape(N_DP, IMG_DEV, KEYS, D), key_valid.reshape(N_DP, IMG_DEV, KEYS), row_live.reshape(N_DP, IMG_DEV, KEYS))
        return lax.map(jax.checkpoint(one_block), shaped).reshape(IMAGES, KEYS, D)
    output, pullback = jax.vjp(forward_all, tokens.astype(jnp.float32), params)
    input_grad, grads = pullback(out_cotangent.astype(jnp.float32))
    return (output.astype(jnp.bfloat16), input_grad.astype(jnp.bfloat16), grads[0], grads[1], grads[2], grads[3], grads[4], grads[5], grads[6], grads[7], grads[8], grads[9], grads[10], grads[11], grads[12])
```

```python
import functools

import jax
import jax.numpy as jnp
from jax import lax
from jax.experimental import pallas as pl
from jax.experimental.pallas import tpu as pltpu
from jax.sharding import PartitionSpec as P

HEADS = 12
GRID = 18
EPS = 1e-06
NEG = -1e30
F32 = jnp.float32
BF16 = jnp.bfloat16
VMEM_LIMIT = 60 * 1024 * 1024
CHUNK = 256


def round_up(n, to):
    return -(-n // to) * to


class Rows:
    def __init__(self, ranks, slots):
        base, extra = GRID // ranks, GRID % ranks
        self.lens = [min(slots, (base + 1) * GRID)] * extra + [base * GRID] * (ranks - extra)
        self.extra = extra
        self.ranks = ranks
        self.slots = slots
        self.offs = []
        at = 0
        for n in self.lens:
            self.offs.append(at)
            at += round_up(n, 8)
        self.rows = round_up(at, 16)
        self.keys = round_up(self.rows, 128)
        self.piece = round_up(slots, 16)
        self.spare = round_up(max(o + round_up(n, 16) for o, n in zip(self.offs, self.lens)), 8) - self.rows
        self.spare = max(self.spare, 0)

    def is_row(self, index):
        hit = None
        for off, n in zip(self.offs, self.lens):
            one = (index >= off) & (index < off + n)
            hit = one if hit is None else hit | one
        return hit


def dot(a, b):
    return lax.dot_general(a, b, (((1,), (0,)), ((), ())), preferred_element_type=F32)


def dot_nt(a, b):
    return lax.dot_general(a, b, (((1,), (1,)), ((), ())), preferred_element_type=F32)


def dot_tn(a, b):
    return lax.dot_general(a, b, (((0,), (0,)), ((), ())), preferred_element_type=F32)


def params(n=0):
    return pltpu.CompilerParams(
        vmem_limit_bytes=VMEM_LIMIT, dimension_semantics=("arbitrary",) * n if n else None
    )


def unpack(lay, stage, scal_ref, base, to_ref, start):
    width = to_ref.shape[1]
    for i, (off, n) in enumerate(zip(lay.offs, lay.lens)):
        full = round_up(n, 8)
        if full > n:
            to_ref[start + off + full - 8 : start + off + full, :] = jnp.zeros((8, width), F32)
        piece = stage[scal_ref[base + i]].astype(F32)
        to_ref[start + off : start + off + n, :] = piece[:n]
    last = lay.offs[-1] + round_up(lay.lens[-1], 8)
    if lay.rows > last:
        to_ref[start + last : start + lay.rows, :] = jnp.zeros((lay.rows - last, width), F32)


def repack(lay, from_ref, start, scal_ref, base, out_ref, lead):
    for i, (off, n) in enumerate(zip(lay.offs, lay.lens)):
        full = round_up(n, 16)
        rows = from_ref[start + off : start + off + full, :].astype(BF16)
        out_ref[(*lead, scal_ref[base + i], slice(0, full), slice(None))] = rows


def live_column(lay, tag):
    index = lax.broadcasted_iota(jnp.int32, (lay.rows, 1), 0)
    return jnp.where(lay.is_row(index), tag, 0).astype(F32)


def normalise(x):
    mean = jnp.mean(x, -1, keepdims=True)
    centered = x - mean
    rstd = lax.rsqrt(jnp.mean(centered * centered, -1, keepdims=True) + EPS)
    return centered * rstd, rstd


def half_masks():
    lane = lax.broadcasted_iota(jnp.int32, (1, 128), 1)
    return [(lane < 64).astype(BF16), (lane >= 64).astype(BF16)]


def attention_forward(
    lay,
    alias,
    scal_ref,
    p0,
    p1,
    p2,
    p3,
    mask_ref,
    vec_ref,
    bias_ref,
    wqkv_ref,
    wout_ref,
    *refs,
):
    hid_ref, x_ref, normed_ref, mixed_ref, qkv_ref, prob_ref, stage, xs = refs[4 if alias else 0 :]
    width = wout_ref.shape[0]
    rows, keys = lay.rows, lay.keys
    for j, piece in enumerate((p0, p1, p2, p3)):
        stage[j] = piece[0]
    unpack(lay, stage, scal_ref, 0, xs, 0)
    x = xs[...]
    x_ref[0] = x.astype(BF16)
    xhat, _ = normalise(x)
    normed_ref[0] = (xhat * vec_ref[0:1] + vec_ref[1:2]).astype(BF16)
    normed = normed_ref[0]
    for c in range(0, 3 * width, CHUNK):
        part = dot(normed, wqkv_ref[:, c : c + CHUNK]) + bias_ref[:, c : c + CHUNK]
        if c < width:
            part = part * 0.125
        qkv_ref[0:rows, c : c + CHUNK] = part.astype(BF16)
    if keys > rows:
        qkv_ref[rows:keys, :] = jnp.zeros((keys - rows, 3 * width), BF16)
    masks = half_masks()

    def pair(p):
        at = pl.multiple_of(p * 128, 128)
        q = qkv_ref[0:rows, pl.ds(at, 128)]
        k = qkv_ref[:, pl.ds(pl.multiple_of(width + at, 128), 128)]
        v = qkv_ref[:, pl.ds(pl.multiple_of(2 * width + at, 128), 128)]
        total = None
        for h in (0, 1):
            s = dot_nt(q, k * masks[h]) + mask_ref[...]
            e = jnp.exp(s - jnp.max(s, -1, keepdims=True))
            prob = (e * (1.0 / jnp.sum(e, -1, keepdims=True))).astype(BF16)
            prob_ref[2 * p + h] = prob
            part = dot(prob, v * masks[h])
            total = part if total is None else total + part
        mixed_ref[0, :, pl.ds(at, 128)] = total.astype(BF16)

    pl.loop(0, width // 128, unroll=2)(pair)
    attended = dot(mixed_ref[0], wout_ref[...]) + vec_ref[2:3]
    hid_ref[0] = xs[...] + live_column(lay, scal_ref[lay.ranks]) * attended


def feed_forward(
    lay,
    per,
    steps,
    scal_ref,
    hid_ref,
    c0,
    c1,
    c2,
    c3,
    w1_ref,
    b1_ref,
    w2_ref,
    vec_ref,
    out_ref,
    gh_ref,
    ga_ref,
    dw1_ref,
    dw2_ref,
    db1_ref,
    dvec_ref,
    stage,
    grad,
    n2,
    gr,
    grt,
    red,
    gn,
    act,
    gexp,
):
    step = pl.program_id(0)
    rows = lay.rows
    each = lay.ranks + 1

    @pl.when(step == 0)
    def _():
        total = None
        for k in range(per):
            block = slice(k * rows, (k + 1) * rows)
            for j, piece in enumerate((c0, c1, c2, c3)):
                stage[j] = piece[k]
            unpack(lay, stage, scal_ref, k * each, grad, k * rows)
            live = live_column(lay, scal_ref[k * each + lay.ranks])
            reduced = (live * grad[block, :]).astype(BF16)
            gr[block, :] = reduced
            wide = reduced.astype(F32)
            grt[:, block] = wide.T.astype(BF16)
            total = jnp.sum(wide, 0, keepdims=True) + (0.0 if total is None else total)
            xhat, _ = normalise(hid_ref[k])
            n2[block, :] = (xhat * vec_ref[0:1] + vec_ref[1:2]).astype(BF16)
        dvec_ref[...] = jnp.zeros_like(dvec_ref)
        dvec_ref[3:4] = total
        red[...] = jnp.zeros_like(red)
        gn[...] = jnp.zeros_like(gn)

    total = None
    for k in range(per):
        block = slice(k * rows, (k + 1) * rows)
        expanded = dot(n2[block, :], w1_ref[...]) + b1_ref[...]
        cdf = 0.5 * (1.0 + lax.erf(expanded * 0.7071067811865476))
        slope = cdf + expanded * (jnp.exp(-0.5 * expanded * expanded) * 0.3989422804014327)
        act[block, :] = (expanded * cdf).astype(BF16)
        grad_active = dot_nt(gr[block, :], w2_ref[...])
        grad_exp = (grad_active * slope).astype(BF16)
        gexp[block, :] = grad_exp
        total = jnp.sum(grad_exp.astype(F32), 0, keepdims=True) + (0.0 if total is None else total)
        red[block, :] += dot(act[block, :], w2_ref[...])
        gn[block, :] += dot_nt(gexp[block, :], w1_ref[...])
    db1_ref[...] = total
    dw1_ref[...] = dot_tn(gexp[...], n2[...]).astype(BF16)
    dw2_ref[...] = dot(grt[...], act[...]).astype(BF16)

    @pl.when(step == steps - 1)
    def _():
        for k in range(per):
            block = slice(k * rows, (k + 1) * rows)
            live = live_column(lay, scal_ref[k * each + lay.ranks])
            hidden = hid_ref[k]
            red[block, :] = hidden + live * (red[block, :] + vec_ref[2:3])
            xhat, rstd = normalise(hidden)
            grad_n2 = gn[block, :]
            dvec_ref[0:1] += jnp.sum(grad_n2 * xhat, 0, keepdims=True)
            dvec_ref[1:2] += jnp.sum(grad_n2, 0, keepdims=True)
            scaled = grad_n2 * vec_ref[0:1]
            row = scaled - jnp.mean(scaled, -1, keepdims=True)
            row = row - xhat * jnp.mean(scaled * xhat, -1, keepdims=True)
            grad_hidden = grad[block, :] + rstd * row
            gh_ref[k] = grad_hidden
            attended = (live * grad_hidden).astype(BF16)
            ga_ref[k] = attended
            dvec_ref[2:3] += jnp.sum(attended.astype(F32), 0, keepdims=True)
        for k in range(per):
            repack(lay, red, k * rows, scal_ref, k * each, out_ref, (k,))


def attention_backward(
    lay,
    alias,
    scal_ref,
    ga_ref,
    gh_ref,
    x_ref,
    qkv_ref,
    prob_ref,
    vec_ref,
    wqkv_ref,
    wout_ref,
    *refs,
):
    ig_ref, gp_ref, dvec_ref, gm_ref, res = refs[1 if alias else 0 :]
    width = wout_ref.shape[0]
    rows = lay.rows
    gm_ref[...] = dot_nt(ga_ref[0], wout_ref[...]).astype(BF16)
    masks = half_masks()

    def pair(p):
        at = pl.multiple_of(p * 128, 128)
        at_k = pl.multiple_of(width + at, 128)
        at_v = pl.multiple_of(2 * width + at, 128)
        q = qkv_ref[0:rows, pl.ds(at, 128)]
        k = qkv_ref[:, pl.ds(at_k, 128)]
        v = qkv_ref[:, pl.ds(at_v, 128)]
        gm = gm_ref[:, pl.ds(at, 128)]
        dq = dk = dv = None
        for h in (0, 1):
            prob = prob_ref[2 * p + h]
            weights = prob.astype(F32)
            gw = dot_nt(gm, v * masks[h])
            delta = jnp.sum(weights * gw, -1, keepdims=True)
            ds = (weights * (gw - delta)).astype(BF16)
            parts = dot(ds, k * masks[h]), dot_tn(ds, q * masks[h]), dot_tn(prob, gm * masks[h])
            if h == 0:
                dq, dk, dv = parts
            else:
                dq, dk, dv = dq + parts[0], dk + parts[1], dv + parts[2]
        gp_ref[0, :, pl.ds(at, 128)] = (dq * 0.125).astype(BF16)
        gp_ref[0, :, pl.ds(at_k, 128)] = dk[:rows].astype(BF16)
        gp_ref[0, :, pl.ds(at_v, 128)] = dv[:rows].astype(BF16)

    pl.loop(0, width // 128, unroll=2)(pair)
    dvec_ref[...] = jnp.zeros_like(dvec_ref)
    dvec_ref[2:3] = jnp.sum(gp_ref[0, :, 0:width].astype(F32), 0, keepdims=True)
    dvec_ref[3:4] = jnp.sum(gp_ref[0, :, 2 * width :].astype(F32), 0, keepdims=True)
    grad_normed = dot_nt(gp_ref[0], wqkv_ref[...])
    xhat, rstd = normalise(x_ref[0].astype(F32))
    dvec_ref[0:1] = jnp.sum(grad_normed * xhat, 0, keepdims=True)
    dvec_ref[1:2] = jnp.sum(grad_normed, 0, keepdims=True)
    scaled = grad_normed * vec_ref[0:1]
    row = scaled - jnp.mean(scaled, -1, keepdims=True)
    row = row - xhat * jnp.mean(scaled * xhat, -1, keepdims=True)
    res[0:rows] = gh_ref[0] + rstd * row
    repack(lay, res, 0, scal_ref, 0, ig_ref, ())


def outer_sum(a_ref, b_ref, out_ref):
    out_ref[...] = dot_tn(a_ref[...], b_ref[...]).astype(BF16)


def weight_sum(a, b, block):
    rows, n = a.shape
    m = b.shape[1]
    return pl.pallas_call(
        outer_sum,
        grid=(n // block,),
        in_specs=[
            pl.BlockSpec((rows, block), lambda i: (0, i)),
            pl.BlockSpec((rows, m), lambda i: (0, 0)),
        ],
        out_specs=pl.BlockSpec((block, m), lambda i: (i, 0)),
        out_shape=jax.ShapeDtypeStruct((n, m), BF16),
        compiler_params=params(1),
        cost_estimate=pl.CostEstimate(
            flops=2 * rows * n * m, bytes_accessed=2 * (rows * (n + m) + n * m), transcendentals=0
        ),
    )(a, b)


def whole(shape):
    return pl.BlockSpec(shape, lambda i: (0,) * len(shape))


def at_image(k, shape):
    return pl.BlockSpec((1, *shape[1:]), lambda i: (k,) + (0,) * (len(shape) - 1))


SMEM = pl.BlockSpec(memory_space=pltpu.SMEM)
HBM = pl.BlockSpec(memory_space=pl.ANY)


class Exchange:
    def __init__(self, n_dp, n_seq):
        self.sizes = (n_dp, n_seq)
        self.bits = []
        for axis, size in (("dp", n_dp), ("seq", n_seq)):
            mask = size // 2
            while mask:
                self.bits.append((axis, mask))
                mask //= 2
        self.n_seq = n_seq

    def order(self, kind):
        names = list(range(len(self.bits)))
        if len(names) != 5:
            return names[::-1]
        z1, z0, x, y, core = names
        return {
            "xyz": [core, x, y, z0, z1],
            "yxz": [core, y, x, z0, z1],
            "zxy": [core, z0, x, z1, y],
            "xzy": [core, x, z0, z1, y],
            "yzx": [core, y, z0, z1, x],
        }[kind]

    def scatter_sum(self, terms, kind, keep=None):
        held = terms.reshape((2,) * len(self.bits) + terms.shape[2:])
        left = list(range(len(self.bits)))
        for bit in self.order(kind):
            axis, mask = self.bits[bit]
            dim = left.index(bit)
            mine = (lax.axis_index(axis) // mask) % 2
            size = self.sizes[0] if axis == "dp" else self.sizes[1]
            other = lax.dynamic_index_in_dim(held, 1 - mine, dim, keepdims=False)
            own = lax.dynamic_index_in_dim(held, mine, dim, keepdims=False)
            got = lax.ppermute(other, axis, [(i, i ^ mask) for i in range(size)])
            left.remove(bit)
            held = own.astype(F32) + got.astype(F32)
            if left:
                held = held.astype(terms.dtype)
        return held


def per_device(
    tokens,
    key_mask,
    row_split,
    group_tags,
    norm1_gain,
    norm1_shift,
    qkv_weight,
    query_bias,
    value_bias,
    out_weight,
    out_bias,
    norm2_gain,
    norm2_shift,
    fc1_weight,
    fc1_bias,
    fc2_weight,
    fc2_bias,
    out_cotangent,
):
    images, slots, width = tokens.shape
    hidden_width = fc1_weight.shape[1]
    n_seq = lax.axis_size("seq")
    n_dp = lax.axis_size("dp")
    rank = lax.axis_index("seq")
    lay = Rows(n_seq, slots)
    per = -(-images // n_seq)
    rows, keys = lay.rows, lay.keys

    def swap(value, j):
        return lax.ppermute(value, "seq", [(i, i ^ j) for i in range(n_seq)])

    def rows_of(array, owner, k):
        return lax.dynamic_slice_in_dim(array, jnp.minimum(owner * per + k, images - 1), 1, 0)

    def bring(array, k):
        return [rows_of(array, rank, k)] + [
            swap(rows_of(array, rank ^ j, k), j) for j in range(1, n_seq)
        ]

    number = rank * per + jnp.arange(per)
    pick = (jnp.minimum(number, images - 1)[:, None] == jnp.arange(images)[None, :]).astype(jnp.int32)
    split_own = jnp.sum(pick[:, :, None] * row_split[None], 1)
    tag_own = jnp.sum(pick * group_tags[None], 1)
    counts = ((tag_own < n_dp) & (number < images)).astype(jnp.int32)
    long = (split_own > GRID // n_seq).astype(jnp.int32)
    earlier = jnp.tril(jnp.ones((n_seq, n_seq), jnp.int32), -1)
    long_before = jnp.sum(long[:, None, :] * earlier[None], -1)
    short_before = jnp.sum((1 - long)[:, None, :] * earlier[None], -1)
    place = jnp.where(long == 1, long_before, lay.extra + short_before)
    hits = (place[:, None, :] == jnp.arange(n_seq)[None, :, None]).astype(jnp.int32)
    source = jnp.sum(hits * jnp.arange(n_seq)[None, None, :], -1)
    scal = jnp.concatenate([source ^ rank, counts[:, None]], 1)
    mask_own = jnp.sum(pick[:, :, None] * key_mask[None], 1).reshape(per, 1, n_seq, slots)
    mask_seg = jnp.sum(hits[..., None] * mask_own, 2)
    mask_rows = []
    for i, n in enumerate(lay.lens):
        end = lay.offs[i + 1] if i + 1 < n_seq else keys
        mask_rows.append(jnp.pad(mask_seg[:, i, :n], ((0, 0), (0, end - lay.offs[i] - n))))
    mask_row = jnp.where(jnp.concatenate(mask_rows, 1) > 0, 0.0, NEG).astype(F32)

    vec1 = jnp.stack([norm1_gain, norm1_shift, out_bias]).astype(F32)
    vec2 = jnp.stack([norm2_gain, norm2_shift, fc2_bias]).astype(F32)
    bias = jnp.concatenate([query_bias, jnp.zeros_like(query_bias), value_bias]).astype(F32)[None]

    kept = []
    chain = None
    for k in range(per):
        pieces = bring(tokens, k)
        shapes = [
            jax.ShapeDtypeStruct((per, rows, width), F32),
            jax.ShapeDtypeStruct((per, rows, width), BF16),
            jax.ShapeDtypeStruct((per, rows, width), BF16),
            jax.ShapeDtypeStruct((per, rows, width), BF16),
            jax.ShapeDtypeStruct((keys, 3 * width), BF16),
            jax.ShapeDtypeStruct((HEADS, rows, keys), BF16),
        ]
        args = [scal[k], *pieces, mask_row[k][None], vec1, bias, qkv_weight, out_weight]
        specs = [SMEM] + [whole(a.shape) for a in args[1:]]
        aliases = {}
        if chain is not None:
            aliases = {len(args) + i: i for i in range(4)}
            args += chain
            specs += [HBM] * 4
        got = pl.pallas_call(
            functools.partial(attention_forward, lay, chain is not None),
            grid=(1,),
            in_specs=specs,
            out_specs=[at_image(k, s.shape) for s in shapes[:4]] + [whole(s.shape) for s in shapes[4:]],
            out_shape=shapes,
            scratch_shapes=[
                pltpu.VMEM((n_seq, slots, width), BF16),
                pltpu.VMEM((rows, width), F32),
            ],
            input_output_aliases=aliases,
            compiler_params=params(1),
            cost_estimate=pl.CostEstimate(
                flops=int(8e9), bytes_accessed=int(12e6), transcendentals=HEADS * rows * keys
            ),
        )(*args)
        chain = list(got[:4])
        kept.append(got[4:])
    hidden, x_all, normed_all, mixed_all = chain

    cot = []
    for j in range(n_seq):
        mine = jnp.concatenate([rows_of(out_cotangent, rank ^ j, k) for k in range(per)], 0)
        cot.append(mine if j == 0 else swap(mine, j))
    steps = hidden_width // CHUNK
    all_rows = per * rows
    shapes = [
        jax.ShapeDtypeStruct((per, n_seq, lay.piece, width), BF16),
        jax.ShapeDtypeStruct((per, rows, width), F32),
        jax.ShapeDtypeStruct((per, rows, width), BF16),
        jax.ShapeDtypeStruct((hidden_width, width), BF16),
        jax.ShapeDtypeStruct((width, hidden_width), BF16),
        jax.ShapeDtypeStruct((1, hidden_width), F32),
        jax.ShapeDtypeStruct((8, width), F32),
    ]
    out_pieces, grad_hidden, grad_att, dw1, dw2, db1, dvec2 = pl.pallas_call(
        functools.partial(feed_forward, lay, per, steps),
        grid=(steps,),
        in_specs=[
            SMEM,
            whole((per, rows, width)),
            *[whole((per, slots, width))] * n_seq,
            pl.BlockSpec((width, CHUNK), lambda i: (0, i)),
            pl.BlockSpec((1, CHUNK), lambda i: (0, i)),
            pl.BlockSpec((CHUNK, width), lambda i: (i, 0)),
            whole(vec2.shape),
        ],
        out_specs=[
            whole(shapes[0].shape),
            whole(shapes[1].shape),
            whole(shapes[2].shape),
            pl.BlockSpec((CHUNK, width), lambda i: (i, 0)),
            pl.BlockSpec((width, CHUNK), lambda i: (0, i)),
            pl.BlockSpec((1, CHUNK), lambda i: (0, i)),
            whole((8, width)),
        ],
        out_shape=shapes,
        scratch_shapes=[
            pltpu.VMEM((n_seq, slots, width), BF16),
            pltpu.VMEM((all_rows, width), F32),
            pltpu.VMEM((all_rows, width), BF16),
            pltpu.VMEM((all_rows, width), BF16),
            pltpu.VMEM((width, all_rows), BF16),
            pltpu.VMEM((all_rows + lay.spare, width), F32),
            pltpu.VMEM((all_rows, width), F32),
            pltpu.VMEM((all_rows, CHUNK), BF16),
            pltpu.VMEM((all_rows, CHUNK), BF16),
        ],
        compiler_params=params(1),
        cost_estimate=pl.CostEstimate(
            flops=12 * all_rows * width * hidden_width,
            bytes_accessed=int(30e6),
            transcendentals=2 * all_rows * hidden_width,
        ),
    )(scal.reshape(-1), hidden, *cot, fc1_weight, fc1_bias.astype(F32)[None], fc2_weight, vec2)

    ex = Exchange(n_dp, n_seq)

    def by_device(array):
        return array.reshape(n_dp, n_seq, array.shape[0] // (n_dp * n_seq), *array.shape[1:])

    fc2_sum = ex.scatter_sum(by_device(dw2), "xyz")
    fc1_sum = ex.scatter_sum(by_device(dw1), "yxz")
    dwo = weight_sum(grad_att.reshape(all_rows, width), mixed_all.reshape(all_rows, width), 256)
    out_sum = ex.scatter_sum(by_device(dwo), "zxy")

    chain = None
    grad_pieces = []
    dvec1 = 0.0
    for k in range(per):
        shapes = [
            jax.ShapeDtypeStruct((n_seq, lay.piece, width), BF16),
            jax.ShapeDtypeStruct((per, rows, 3 * width), BF16),
            jax.ShapeDtypeStruct((8, width), F32),
        ]
        args = [scal[k], grad_att, grad_hidden, x_all, *kept[k], vec1, qkv_weight, out_weight]
        specs = [SMEM] + [at_image(k, a.shape) for a in args[1:4]] + [whole(a.shape) for a in args[4:]]
        aliases = {}
        if chain is not None:
            aliases = {len(args): 1}
            args.append(chain)
            specs.append(HBM)
        pieces, chain, dvec = pl.pallas_call(
            functools.partial(attention_backward, lay, chain is not None),
            grid=(1,),
            in_specs=specs,
            out_specs=[whole(shapes[0].shape), at_image(k, shapes[1].shape), whole(shapes[2].shape)],
            out_shape=shapes,
            scratch_shapes=[
                pltpu.VMEM((rows, width), BF16),
                pltpu.VMEM((rows + lay.spare, width), F32),
            ],
            input_output_aliases=aliases,
            compiler_params=params(1),
            cost_estimate=pl.CostEstimate(
                flops=int(10e9), bytes_accessed=int(15e6), transcendentals=0
            ),
        )(*args)
        grad_pieces.append(pieces)
        dvec1 = dvec1 + dvec
    gp_all = chain.reshape(all_rows, 3 * width)
    dwqkv = weight_sum(gp_all, normed_all.reshape(all_rows, width), 256)
    third = by_device(dwqkv)
    cut = third.shape[2] // 3
    qkv_sum = jnp.concatenate(
        [
            ex.scatter_sum(third[:, :, i * cut : (i + 1) * cut], kind)
            for i, kind in enumerate(("xyz", "yzx", "zxy"))
        ],
        0,
    )

    vectors = [dvec1[0], dvec1[1], dvec1[2], dvec1[3], dvec2[2], dvec2[0], dvec2[1], dvec2[3], db1[0]]
    part = width // (n_dp * n_seq)
    small = jnp.concatenate([by_device(v) for v in vectors], -1)
    small_sum = ex.scatter_sum(small, "xyz")
    small_out = [small_sum[i * part : (i + 1) * part] for i in range(8)] + [small_sum[8 * part :]]

    live = jnp.arange(slots)[None, :] < (
        jnp.sum(jnp.where(jnp.arange(n_seq)[None, :] == rank, row_split, 0), 1) * GRID
    )[:, None]
    live = live[..., None]

    def home(pieces, passed):
        got = [[p[0] if j == 0 else swap(p[j], j) for j in range(n_seq)] for p in pieces]
        parts = []
        for owner in range(n_seq):
            for k in range(per):
                if owner * per + k < images:
                    parts.append(lax.select_n(rank ^ owner, *[got[k][j] for j in range(n_seq)])[:slots])
        return jnp.where(live, jnp.stack(parts), passed)

    output = home([out_pieces[k] for k in range(per)], tokens)
    input_grad = home(grad_pieces, out_cotangent)
    return (
        output,
        input_grad,
        small_out[0],
        small_out[1],
        qkv_sum.T,
        small_out[2],
        small_out[3],
        out_sum.T,
        small_out[4],
        small_out[5],
        small_out[6],
        fc1_sum.T,
        small_out[8],
        fc2_sum.T,
        small_out[7],
    )


def solution(mesh):
    rows = P("dp", "seq", None)
    split = P(("dp", "seq"))
    columns = P(None, ("dp", "seq"))
    return jax.shard_map(
        per_device,
        mesh=mesh,
        in_specs=(rows, P("dp", None), P("dp", None), P("dp")) + (P(),) * 13 + (rows,),
        out_specs=(
            rows,
            rows,
            split,
            split,
            columns,
            split,
            split,
            columns,
            split,
            split,
            split,
            columns,
            split,
            columns,
            split,
        ),
        check_vma=False,
    )
```

```python
import functools

import jax
import jax.numpy as jnp
from jax import lax
from jax.experimental import pallas as pl
from jax.experimental.pallas import tpu as pltpu
from jax.sharding import PartitionSpec as P

HEADS = 12
GRID = 18
EPS = 1e-06
NEG = -1e30
F32 = jnp.float32
BF16 = jnp.bfloat16
VMEM_LIMIT = 60 * 1024 * 1024
CHUNK = 768
GROUP = 256
EARLY_LANES = 256
LATE_LANES = 128

BITS = {"core": ("seq", 1), "y": ("seq", 2), "x": ("dp", 1), "z0": ("dp", 2), "z1": ("dp", 4)}
FC1_ORDER = ("x", "z0", "y", "z1")
FC2_ORDER = ("z0", "x", "z1", "y")
OUT_ORDER = ("y", "x", "z0", "z1")
QKV_ORDERS = (("x", "y", "z0", "z1"), ("z0", "x", "z1", "y"))
QKV_CUTS = (0, 40, 72)
SMEM = pl.BlockSpec(memory_space=pltpu.SMEM)
HBM = pl.BlockSpec(memory_space=pl.ANY)


def round_up(n, to):
    return -(-n // to) * to


class Rows:
    def __init__(self, ranks, slots):
        base, extra = GRID // ranks, GRID % ranks
        self.lens = [min(slots, (base + 1) * GRID)] * extra + [base * GRID] * (ranks - extra)
        self.extra = extra
        self.ranks = ranks
        self.slots = slots
        self.offs = []
        at = 0
        for n in self.lens:
            self.offs.append(at)
            at += round_up(n, 8)
        self.rows = round_up(at, 16)
        self.keys = round_up(self.rows, 128)
        self.piece = round_up(slots, 16)
        end = max(o + round_up(n, 16) for o, n in zip(self.offs, self.lens))
        self.spare = max(round_up(end, 8) - self.rows, 0)
        self.scalars = ranks + 1

    def is_row(self, index):
        hit = None
        for off, n in zip(self.offs, self.lens):
            one = (index >= off) & (index < off + n)
            hit = one if hit is None else hit | one
        return hit


def dot(a, b):
    return lax.dot_general(a, b, (((1,), (0,)), ((), ())), preferred_element_type=F32)


def dot_nt(a, b):
    return lax.dot_general(a, b, (((1,), (1,)), ((), ())), preferred_element_type=F32)


def dot_tn(a, b):
    return lax.dot_general(a, b, (((0,), (0,)), ((), ())), preferred_element_type=F32)


def params():
    return pltpu.CompilerParams(vmem_limit_bytes=VMEM_LIMIT)


def cost(flops, moved, exps=0):
    return pl.CostEstimate(flops=int(flops) // 16, bytes_accessed=int(moved) // 16, transcendentals=int(exps) // 16)


def whole(shape):
    return pl.BlockSpec(shape, lambda *i: (0,) * len(shape))


def shaped(shape, dtype):
    return jax.ShapeDtypeStruct(shape, dtype)


def unpack(lay, stage, scal_ref, base, to_ref):
    width = to_ref.shape[1]
    for i, (off, n) in enumerate(zip(lay.offs, lay.lens)):
        full = round_up(n, 8)
        if full > n:
            to_ref[off + full - 8 : off + full, :] = jnp.zeros((8, width), F32)
        piece = stage[scal_ref[base + i]].astype(F32)
        to_ref[off : off + n, :] = piece[:n]
    last = lay.offs[-1] + round_up(lay.lens[-1], 8)
    if lay.rows > last:
        to_ref[last : lay.rows, :] = jnp.zeros((lay.rows - last, width), F32)


def repack(lay, from_ref, start, scal_ref, base, stage):
    for i, (off, n) in enumerate(zip(lay.offs, lay.lens)):
        full = round_up(n, 16)
        stage[scal_ref[base + i], 0:full, :] = from_ref[start + off : start + off + full, :].astype(BF16)


def live_column(lay, tag):
    index = lax.broadcasted_iota(jnp.int32, (lay.rows, 1), 0)
    return jnp.where(lay.is_row(index), tag, 0).astype(F32)


def normalise(x):
    mean = jnp.mean(x, -1, keepdims=True)
    centered = x - mean
    rstd = lax.rsqrt(jnp.mean(centered * centered, -1, keepdims=True) + EPS)
    return centered * rstd, rstd


def norm_backward(grad, gain, xhat, rstd):
    scaled = grad * gain
    row = scaled - jnp.mean(scaled, -1, keepdims=True)
    return rstd * (row - xhat * jnp.mean(scaled * xhat, -1, keepdims=True))


def half_masks():
    lane = lax.broadcasted_iota(jnp.int32, (1, 128), 1)
    return [(lane < 64).astype(BF16), (lane >= 64).astype(BF16)]


def keep_and_send(core, even, odd):
    mine = core == 0
    return jnp.where(mine, even, odd).astype(BF16), jnp.where(mine, odd, even).astype(BF16)


def spread(vectors, lanes):
    total, at = 0.0, 0
    for v in vectors:
        n = v.shape[1]
        each = n // 32
        dest = lax.broadcasted_iota(jnp.int32, (32, n), 0) * each
        lane = lax.broadcasted_iota(jnp.int32, (32, n), 1)
        chosen = jnp.where((lane >= dest) & (lane < dest + each), v, 0.0).astype(BF16)
        source = lax.broadcasted_iota(jnp.int32, (n, lanes), 0)
        part = ((source.astype(F32) + 0.5) * (1.0 / each)).astype(jnp.int32)
        target = lax.broadcasted_iota(jnp.int32, (n, lanes), 1)
        pick = (source - part * each == target - at).astype(F32).astype(BF16)
        total = total + dot(chosen, pick)
        at += each
    return total


def with_vectors(rows, packed, d, width):
    lanes = packed.shape[1]
    vec = jnp.broadcast_to(packed[d : d + 1, :], (8, lanes))
    return jnp.concatenate([rows, jnp.concatenate([vec, jnp.zeros((8, width - lanes), F32)], 1)], 0)


def place_of(order, dp, y):
    bits = {"x": dp % 2, "z0": dp // 2 % 2, "z1": dp // 4, "y": y}
    return tuple(bits[name] for name in order)


def attention_forward(lay, first, linked, scal_ref, p0, p1, p2, p3, mask_ref, vec_ref, bias_ref, wq, wk, wv, wo, *refs):
    outs = refs[7:] if linked else refs
    hid_ref, x_ref, normed_ref, mixed_ref, n2_ref, qkv_ref, prob_ref, stage, xs = outs
    rows, keys = lay.rows, lay.keys
    image, group = pl.program_id(0), pl.program_id(1)
    base = (first + image) * lay.scalars

    @pl.when(group == 0)
    def _():
        for j, piece in enumerate((p0, p1, p2, p3)):
            stage[j] = piece[0]
        unpack(lay, stage, scal_ref, base, xs)
        x = xs[...]
        x_ref[0] = x.astype(BF16)
        xhat, _ = normalise(x)
        normed_ref[0] = (xhat * vec_ref[0:1] + vec_ref[1:2]).astype(BF16)

    normed = normed_ref[0]
    qkv = []
    for j, weight in enumerate((wq, wk, wv)):
        part = dot(normed, weight[...]) + bias_ref[j : j + 1, :]
        if j == 0:
            part = part * 0.125
        part = part.astype(BF16)
        if j and keys > rows:
            part = jnp.concatenate([part, jnp.zeros((keys - rows, GROUP), BF16)], 0)
        qkv_ref[0, j, 0 : part.shape[0], :] = part
    if keys > rows:
        qkv_ref[0, 0, rows:keys, :] = jnp.zeros((keys - rows, GROUP), BF16)
    masks = half_masks()
    for p in range(GROUP // 128):
        lanes = slice(p * 128, (p + 1) * 128)
        q = qkv_ref[0, 0, 0:rows, lanes]
        k = qkv_ref[0, 1, :, lanes]
        v = qkv_ref[0, 2, :, lanes]
        total = None
        for h in (0, 1):
            s = dot_nt(q, k * masks[h]) + mask_ref[0]
            e = jnp.exp(s - jnp.max(s, -1, keepdims=True))
            prob = (e * (1.0 / jnp.sum(e, -1, keepdims=True))).astype(BF16)
            prob_ref[0, 2 * p + h] = prob
            part = dot(prob, v * masks[h])
            total = part if total is None else total + part
        at = pl.multiple_of(group * GROUP + p * 128, 128)
        mixed_ref[0, :, pl.ds(at, 128)] = total.astype(BF16)

    @pl.when(group == pl.num_programs(1) - 1)
    def _():
        attended = dot(mixed_ref[0], wo[...]) + vec_ref[2:3]
        hidden = xs[...] + live_column(lay, scal_ref[base + lay.ranks]) * attended
        hid_ref[0] = hidden
        xhat, _ = normalise(hidden)
        n2_ref[0] = (xhat * vec_ref[3:4] + vec_ref[4:5]).astype(BF16)


def call_forward(lay, first, count, per, scal, pieces, mask_row, vecs, bias, qkv_weight, out_weight, chain):
    rows, keys = lay.rows, lay.keys
    width = out_weight.shape[0]
    groups = width // GROUP
    shapes = [
        shaped((per, rows, width), F32),
        shaped((per, rows, width), BF16),
        shaped((per, rows, width), BF16),
        shaped((per, rows, width), BF16),
        shaped((per, rows, width), BF16),
        shaped((per, 3, keys, width), BF16),
        shaped((per, HEADS, rows, keys), BF16),
    ]
    args = [scal, *pieces, mask_row, vecs, bias, qkv_weight, qkv_weight, qkv_weight, out_weight]
    specs = (
        [SMEM]
        + [pl.BlockSpec((1, lay.slots, width), lambda i, g: (i, 0, 0))] * len(pieces)
        + [pl.BlockSpec((1, 1, keys), lambda i, g: (first + i, 0, 0)), whole(vecs.shape)]
        + [pl.BlockSpec((3, GROUP), lambda i, g: (0, g))]
        + [pl.BlockSpec((width, GROUP), functools.partial(lambda j, i, g: (0, j * groups + g), j)) for j in range(3)]
        + [whole(out_weight.shape)]
    )
    aliases = {}
    if chain is not None:
        aliases = {len(args) + i: i for i in range(7)}
        args += chain
        specs += [HBM] * 7
    return list(
        pl.pallas_call(
            functools.partial(attention_forward, lay, first, chain is not None),
            grid=(count, groups),
            in_specs=specs,
            out_specs=[pl.BlockSpec((1, rows, width), lambda i, g: (first + i, 0, 0))] * 5
            + [
                pl.BlockSpec((1, 3, keys, GROUP), lambda i, g: (first + i, 0, 0, g)),
                pl.BlockSpec((1, HEADS // groups, rows, keys), lambda i, g: (first + i, g, 0, 0)),
            ],
            out_shape=shapes,
            scratch_shapes=[pltpu.VMEM((lay.ranks, lay.slots, width), BF16), pltpu.VMEM((rows, width), F32)],
            input_output_aliases=aliases,
            compiler_params=params(),
            cost_estimate=cost(8e9 * count, 12e6 * count, HEADS * rows * keys * count),
        )(*args)
    )


def feed_forward(lay, per, fast, scal_ref, hid_hbm, c0, c1, c2, c3, n2_ref, w1_ref, b1_ref, w2_ref, vec_ref, *refs):
    out_refs = refs[: lay.ranks]
    ga_ref, db1_ref, dvec_ref, *dw = refs[lay.ranks : -11]
    stage, back, cot, gr, grt, red, gn, act, gexp, hid, sem = refs[-11:]
    step = pl.program_id(0)
    last = pl.num_programs(0) - 1
    rows = lay.rows
    fetch = pltpu.make_async_copy(hid_hbm, hid, sem)

    @pl.when(step == 0)
    def _():
        fetch.start()
        total = None
        for k in range(per):
            block = slice(k * rows, (k + 1) * rows)
            for j, piece in enumerate((c0, c1, c2, c3)):
                stage[j] = piece[k]
            unpack(lay, stage, scal_ref, k * lay.scalars, cot)
            wide = live_column(lay, scal_ref[k * lay.scalars + lay.ranks]) * cot[...]
            gr[block, :] = wide.astype(BF16)
            grt[:, block] = wide.T.astype(BF16)
            total = jnp.sum(wide, 0, keepdims=True) + (0.0 if total is None else total)
        dvec_ref[...] = jnp.zeros_like(dvec_ref)
        dvec_ref[3:4] = total
        red[...] = jnp.zeros_like(red)
        gn[...] = jnp.zeros_like(gn)

    total = None
    for k in range(per):
        block = slice(k * rows, (k + 1) * rows)
        expanded = dot(n2_ref[block, :], w1_ref[...]) + b1_ref[...]
        cdf = 0.5 * (1.0 + lax.erf(expanded * 0.7071067811865476))
        slope = cdf + expanded * (jnp.exp(-0.5 * expanded * expanded) * 0.3989422804014327)
        act[block, :] = (expanded * cdf).astype(BF16)
        grad_active = dot_nt(gr[block, :], w2_ref[...])
        grad_exp = (grad_active * slope).astype(BF16)
        gexp[block, :] = grad_exp
        total = jnp.sum(grad_exp.astype(F32), 0, keepdims=True) + (0.0 if total is None else total)
        red[block, :] += dot(act[block, :], w2_ref[...])
        gn[block, :] += dot_nt(gexp[block, :], w1_ref[...])
    db1_ref[...] = total
    sums1 = dot_tn(gexp[...], n2_ref[...])
    sums2 = dot(grt[...], act[...])
    if fast:
        core = scal_ref[per * lay.scalars]
        own1, send1, own2, send2 = dw
        n = CHUNK // 8
        for i in range(2):
            for y in range(2):
                at = (i * 4 + y * 2) * n
                place = place_of(FC1_ORDER, i, y)
                own1[place], send1[place] = keep_and_send(core, sums1[at : at + n], sums1[at + n : at + 2 * n])
        n = sums2.shape[0] // 32
        for dp in range(8):
            for y in range(2):
                at = (dp * 4 + y * 2) * n
                place = place_of(FC2_ORDER, dp, y)
                own2[place], send2[place] = keep_and_send(core, sums2[at : at + n], sums2[at + n : at + 2 * n])
    else:
        dw[0][...] = sums1.astype(BF16)
        dw[1][...] = sums2.astype(BF16)

    @pl.when(step == last)
    def _():
        fetch.wait()
        for k in range(per):
            block = slice(k * rows, (k + 1) * rows)
            live = live_column(lay, scal_ref[k * lay.scalars + lay.ranks])
            hidden = hid[k]
            red[block, :] = hidden + live * (red[block, :] + vec_ref[5:6])
            xhat, rstd = normalise(hidden)
            grad = gn[block, :]
            dvec_ref[0:1] += jnp.sum(grad * xhat, 0, keepdims=True)
            dvec_ref[1:2] += jnp.sum(grad, 0, keepdims=True)
            row = norm_backward(grad, vec_ref[3:4], xhat, rstd)
            attended = (live * (gr[block, :].astype(F32) + row)).astype(BF16)
            ga_ref[k] = attended
            dvec_ref[2:3] += jnp.sum(attended.astype(F32), 0, keepdims=True)
        for k in range(per):
            repack(lay, red, k * rows, scal_ref, k * lay.scalars, back)
            for j, out_ref in enumerate(out_refs):
                out_ref[k] = back[j]


def call_feed(lay, per, fast, scal, hidden, cot, n2, w1, b1, w2, vecs):
    width, inner = w1.shape
    rows = per * lay.rows
    shapes = [shaped((per, lay.piece, width), BF16)] * lay.ranks + [
        shaped((per, lay.rows, width), BF16),
        shaped((1, inner), F32),
        shaped((8, width), F32),
    ]
    specs = [whole((per, lay.piece, width))] * lay.ranks + [
        whole((per, lay.rows, width)),
        pl.BlockSpec((1, CHUNK), lambda i: (0, i)),
        whole((8, width)),
    ]
    if fast:
        def where(i):
            at = {"x": 0, "y": 0, "z0": i % 2, "z1": i // 2}
            return tuple(at[name] for name in FC1_ORDER) + (0, 0)

        block = tuple(2 if name in ("x", "y") else 1 for name in FC1_ORDER) + (inner // 32, width)
        shapes += [shaped((2, 2, 2, 2, inner // 32, width), BF16)] * 2
        specs += [pl.BlockSpec(block, where)] * 2
        n = width // 32
        shapes += [shaped((2, 2, 2, 2, n, inner), BF16)] * 2
        specs += [pl.BlockSpec((2, 2, 2, 2, n, CHUNK), lambda i: (0, 0, 0, 0, 0, i))] * 2
    else:
        shapes += [shaped((inner, width), BF16), shaped((width, inner), BF16)]
        specs += [pl.BlockSpec((CHUNK, width), lambda i: (i, 0)), pl.BlockSpec((width, CHUNK), lambda i: (0, i))]
    once = pl.Buffered(1)
    return pl.pallas_call(
        functools.partial(feed_forward, lay, per, fast),
        grid=(inner // CHUNK,),
        in_specs=[
            SMEM,
            HBM,
            *[pl.BlockSpec(c.shape, lambda i: (0, 0, 0), pipeline_mode=once) for c in cot],
            pl.BlockSpec(n2.shape, lambda i: (0, 0), pipeline_mode=once),
            pl.BlockSpec((width, CHUNK), lambda i: (0, i)),
            pl.BlockSpec((1, CHUNK), lambda i: (0, i)),
            pl.BlockSpec((CHUNK, width), lambda i: (i, 0)),
            whole(vecs.shape),
        ],
        out_specs=specs,
        out_shape=shapes,
        scratch_shapes=[
            pltpu.VMEM((lay.ranks, lay.slots, width), BF16),
            pltpu.VMEM((lay.ranks, lay.piece, width), BF16),
            pltpu.VMEM((lay.rows, width), F32),
            pltpu.VMEM((rows, width), BF16),
            pltpu.VMEM((width, rows), BF16),
            pltpu.VMEM((rows + lay.spare, width), F32),
            pltpu.VMEM((rows, width), F32),
            pltpu.VMEM((rows, CHUNK), BF16),
            pltpu.VMEM((rows, CHUNK), BF16),
            pltpu.VMEM((per, lay.rows, width), F32),
            pltpu.SemaphoreType.DMA,
        ],
        compiler_params=params(),
        cost_estimate=cost(12 * rows * width * inner, 30e6, 2 * rows * inner),
    )(scal, hidden, *cot, n2, w1, b1, w2, vecs)


def out_sums(fast, core_ref, ga_ref, mixed_ref, dvec_ref, db1_ref, *refs):
    width = mixed_ref.shape[1]
    sums = dot_tn(ga_ref[...], mixed_ref[...])
    if not fast:
        refs[0][...] = sums.astype(BF16)
        return
    own_ref, send_ref = refs
    n = width // 32
    parts = [dvec_ref[2:3], dvec_ref[0:1], dvec_ref[1:2], dvec_ref[3:4], db1_ref[...]]
    packed = spread(parts, EARLY_LANES)
    for dp in range(8):
        for y in range(2):
            d = dp * 4 + y * 2
            even, odd = [
                with_vectors(sums[e * n : (e + 1) * n], packed, e, width) for e in (d, d + 1)
            ]
            place = place_of(OUT_ORDER, dp, y)
            own_ref[place], send_ref[place] = keep_and_send(core_ref[0], even, odd)


def call_out_sums(fast, core, ga, mixed, dvec, db1):
    rows, width = ga.shape
    shapes = [shaped((2, 2, 2, 2, width // 32 + 8, width), BF16)] * 2 if fast else [shaped((width, width), BF16)]
    args = [core, ga, mixed, dvec, db1]
    return pl.pallas_call(
        functools.partial(out_sums, fast),
        grid=(1,),
        in_specs=[SMEM] + [whole(a.shape) for a in args[1:]],
        out_specs=[whole(s.shape) for s in shapes],
        out_shape=shapes,
        compiler_params=params(),
        cost_estimate=cost(2 * rows * width * width, 6e6),
    )(*args)


def qkv_sums(per, fast, core_ref, gp_ref, normed_ref, *refs):
    _, _, rows, width = gp_ref.shape
    dvecs = refs[:per]
    sums = dot_tn(gp_ref[...].reshape(per * rows, width), normed_ref[...])
    if not fast:
        refs[per][...] = sums.astype(BF16)
        return
    own_refs, send_refs, held = refs[per : per + 2], refs[per + 2 : per + 4], refs[-1]
    step = pl.program_id(0)
    held[pl.ds(pl.multiple_of(step * width, width), width), :] = sums

    @pl.when(step == pl.num_programs(0) - 1)
    def _():
        vec = dvecs[0][...]
        for more in dvecs[1:]:
            vec = vec + more[...]
        packed = spread([vec[i : i + 1] for i in range(4)], LATE_LANES)
        each = 3 * width // 32
        for dp in range(8):
            for y in range(2):
                d = dp * 4 + y * 2
                for i, order in enumerate(QKV_ORDERS):
                    lo, hi = QKV_CUTS[i : i + 2]
                    even, odd = [held[e * each + lo : e * each + hi, :] for e in (d, d + 1)]
                    if i == 1:
                        even, odd = [
                            with_vectors(v, packed, e, width) for v, e in ((even, d), (odd, d + 1))
                        ]
                    place = place_of(order, dp, y)
                    own_refs[i][place], send_refs[i][place] = keep_and_send(core_ref[0], even, odd)


def call_qkv_sums(fast, core, gp, normed, dvecs):
    per, _, rows, width = gp.shape
    if fast:
        heights = (QKV_CUTS[1], QKV_CUTS[2] - QKV_CUTS[1] + 8)
        shapes = [shaped((2, 2, 2, 2, n, width), BF16) for n in heights] * 2
        specs = [whole(s.shape) for s in shapes]
        scratch = [pltpu.VMEM((3 * width, width), F32)]
    else:
        shapes = [shaped((3 * width, width), BF16)]
        specs = [pl.BlockSpec((width, width), lambda i: (i, 0))]
        scratch = []
    return pl.pallas_call(
        functools.partial(qkv_sums, per, fast),
        grid=(3,),
        in_specs=[SMEM, pl.BlockSpec((per, 1, rows, width), lambda i: (0, i, 0, 0)), whole(normed.shape)]
        + [whole(d.shape) for d in dvecs],
        out_specs=specs,
        out_shape=shapes,
        scratch_shapes=scratch,
        compiler_params=params(),
        cost_estimate=cost(6 * per * rows * width * width, 10e6),
    )(core, gp, normed, *dvecs)


def attention_backward(lay, k, linked, scal_ref, ga_ref, qkv_ref, prob_ref, x_ref, vec_ref, wo_ref, wq, wk, wv, *refs):
    gp_ref, *ig_refs, dvec_ref, gn, res, back = refs[linked:]
    rows = lay.rows
    group = pl.program_id(0)
    grad_mixed = dot_nt(ga_ref[0], wo_ref[...]).astype(BF16)
    masks = half_masks()

    @pl.when(group == 0)
    def _():
        dvec_ref[...] = jnp.zeros_like(dvec_ref)
        gn[...] = jnp.zeros_like(gn)

    for p in range(GROUP // 128):
        lanes = slice(p * 128, (p + 1) * 128)
        q = qkv_ref[0, 0, 0:rows, lanes]
        key = qkv_ref[0, 1, :, lanes]
        v = qkv_ref[0, 2, :, lanes]
        gm = grad_mixed[:, lanes]
        dq = dk = dv = 0.0
        for h in (0, 1):
            prob = prob_ref[0, 2 * p + h]
            weights = prob.astype(F32)
            gw = dot_nt(gm, v * masks[h])
            delta = jnp.sum(weights * gw, -1, keepdims=True)
            ds = (weights * (gw - delta)).astype(BF16)
            dq = dq + dot(ds, key * masks[h])
            dk = dk + dot_tn(ds, q * masks[h])
            dv = dv + dot_tn(prob, gm * masks[h])
        dq, dk, dv = (dq * 0.125).astype(BF16), dk[:rows].astype(BF16), dv[:rows].astype(BF16)
        gp_ref[0, 0, :, lanes] = dq
        gp_ref[0, 1, :, lanes] = dk
        gp_ref[0, 2, :, lanes] = dv
        at = pl.multiple_of(group * GROUP + p * 128, 128)
        dvec_ref[2:3, pl.ds(at, 128)] = jnp.sum(dq.astype(F32), 0, keepdims=True)
        dvec_ref[3:4, pl.ds(at, 128)] = jnp.sum(dv.astype(F32), 0, keepdims=True)
    gn[...] += sum(dot_nt(gp_ref[0, j], w[...]) for j, w in enumerate((wq, wk, wv)))

    @pl.when(group == pl.num_programs(0) - 1)
    def _():
        grad = gn[...]
        xhat, rstd = normalise(x_ref[0].astype(F32))
        dvec_ref[0:1] = jnp.sum(grad * xhat, 0, keepdims=True)
        dvec_ref[1:2] = jnp.sum(grad, 0, keepdims=True)
        res[0:rows] = ga_ref[0].astype(F32) + norm_backward(grad, vec_ref[0:1], xhat, rstd)
        repack(lay, res, 0, scal_ref, k * lay.scalars, back)
        for j, ig_ref in enumerate(ig_refs):
            ig_ref[0] = back[j]


def call_backward(lay, k, per, scal, ga, qkv, prob, x, vecs, out_weight, qkv_weight, chain):
    rows, keys = lay.rows, lay.keys
    width = out_weight.shape[0]
    groups = width // GROUP
    alone = k == per - 1
    one = pl.BlockSpec((1, rows, width), lambda g: (k, 0, 0))
    args = [scal, ga, qkv, prob, x, vecs, out_weight, qkv_weight, qkv_weight, qkv_weight]
    specs = [
        SMEM,
        one,
        pl.BlockSpec((1, 3, keys, GROUP), lambda g: (k, 0, 0, g)),
        pl.BlockSpec((1, HEADS // groups, rows, keys), lambda g: (k, g, 0, 0)),
        one,
        whole(vecs.shape),
        pl.BlockSpec((GROUP, width), lambda g: (g, 0)),
    ] + [pl.BlockSpec((width, GROUP), functools.partial(lambda j, g: (0, j * groups + g), j)) for j in range(3)]
    aliases = {}
    if chain is not None:
        count = 1 if alone else len(chain)
        aliases = {len(args) + i: i for i in range(count)}
        args += chain[:count]
        specs += [HBM] * count
    return pl.pallas_call(
        functools.partial(attention_backward, lay, k, len(args) - 10),
        grid=(groups,),
        in_specs=specs,
        out_specs=[
            pl.BlockSpec((1, 3, rows, GROUP), lambda g: (k, 0, 0, g)),
            *[pl.BlockSpec((1, lay.piece, width), lambda g: (0 if alone else k, 0, 0))] * lay.ranks,
            whole((8, width)),
        ],
        out_shape=[
            shaped((per, 3, rows, width), BF16),
            *[shaped((1 if alone else per - 1, lay.piece, width), BF16)] * lay.ranks,
            shaped((8, width), F32),
        ],
        scratch_shapes=[
            pltpu.VMEM((rows, width), F32),
            pltpu.VMEM((rows + lay.spare, width), F32),
            pltpu.VMEM((lay.ranks, lay.piece, width), BF16),
        ],
        input_output_aliases=aliases,
        compiler_params=params(),
        cost_estimate=cost(10e9, 10e6),
    )(*args)


def assemble(per, ranks, scal_ref, *refs):
    *got, passed_ref, out_ref = refs
    images, slots, width = out_ref.shape
    row = lax.broadcasted_iota(jnp.int32, (slots, width), 0)
    first = 0
    for b in range(0, len(got), ranks):
        for j, piece in enumerate(got[b : b + ranks]):
            for k in range(piece.shape[0]):
                image = (scal_ref[images] ^ j) * per + first + k

                @pl.when(image < images)
                def _():
                    worked = piece[k][:slots].astype(F32)
                    kept = passed_ref[image].astype(F32)
                    out_ref[image] = jnp.where(row < scal_ref[image], worked, kept).astype(BF16)

        first += got[b].shape[0]


def call_assemble(per, ranks, home_scal, got, passed):
    args = [home_scal, *got, passed]
    return pl.pallas_call(
        functools.partial(assemble, per, ranks),
        grid=(1,),
        in_specs=[SMEM] + [whole(a.shape) for a in args[1:]],
        out_specs=whole(passed.shape),
        out_shape=shaped(passed.shape, BF16),
        compiler_params=params(),
        cost_estimate=cost(0, 5e6),
    )(*args)


class Part:
    def __init__(self, own, send, order, at=None):
        self.own, self.send, self.order = own, send, ["core", *order]
        self.got = self.sent = None
        self.at = at


def exchange(parts):
    for p in parts:
        if p.send is None:
            continue
        axis, weight = BITS[p.order[0]]
        size = lax.axis_size(axis)
        p.got = lax.ppermute(p.send, axis, [(i, i ^ weight) for i in range(size)])
        p.sent, p.send = p.send, None


def add_and_split(counts, mine_ref, *refs):
    n = len(counts)
    for i in range(n):
        own, got, keep, send = refs[2 * i], refs[2 * i + 1], refs[2 * n + 2 * i], refs[2 * n + 2 * i + 1]
        mine = mine_ref[i]
        keep[...] = (own[mine].astype(F32) + got[mine].astype(F32)).astype(BF16)
        send[...] = (own[1 - mine].astype(F32) + got[1 - mine].astype(F32)).astype(BF16)


def combine(parts):
    parts = [p for p in parts if p.got is not None]
    last = [p for p in parts if len(p.order) == 1]
    for p in last:
        p.own = p.own.astype(F32) + p.got.astype(F32)
        p.got = p.send = None
        p.order = []
    parts = [p for p in parts if p.order]
    if not parts:
        return
    views = []
    for p in parts:
        shape = p.own.shape
        flat = (2, 2 ** (len(p.order) - 2), *shape[-2:])
        if p.at is not None:
            flat = (shape[0], *flat)
        views.append((p.own.reshape(flat), p.got.reshape(flat)))
    size = sum(4 * v[0].size for v in views)
    steps = min(4 if size > 12e6 else 2 if size > 3e6 else 1, *(v[0].shape[-3] for v in views))
    ins, outs, shapes, args, mine = [], [], [], [], []
    for p, (own, got) in zip(parts, views):
        many, n, width = own.shape[-3:]
        block = (2, many // steps, n, width)
        if p.at is None:
            ins += [pl.BlockSpec(block, lambda i: (0, i, 0, 0))] * 2
        else:
            ins += [pl.BlockSpec((None, *block), functools.partial(lambda a, i: (a, 0, i, 0, 0), p.at))] * 2
        outs += [pl.BlockSpec(block[1:], lambda i: (i, 0, 0))] * 2
        shapes += [shaped((many, n, width), BF16)] * 2
        args += [own, got]
        axis, weight = BITS[p.order[1]]
        mine.append((lax.axis_index(axis) // weight) % 2)
    moved = sum(3 * a.size for a in args)
    res = pl.pallas_call(
        functools.partial(add_and_split, [None] * len(parts)),
        grid=(steps,),
        in_specs=[SMEM] + ins,
        out_specs=outs,
        out_shape=shapes,
        compiler_params=params(),
        cost_estimate=cost(0, moved),
    )(jnp.stack(mine), *args)
    for i, p in enumerate(parts):
        shape = (*[2] * (len(p.order) - 2), *p.own.shape[-2:])
        p.at = None
        p.own, p.send = res[2 * i].reshape(shape), res[2 * i + 1].reshape(shape)
        p.got = None
        p.order.pop(0)


def wait(values, parts):
    live = [p for p in parts if p.got is not None]
    values, gots = lax.optimization_barrier((values, [p.got for p in live]))
    for p, g in zip(live, gots):
        p.got = g
    return values


def after(values, parts):
    return lax.optimization_barrier((values, [p.sent for p in parts if p.sent is not None]))[0]


def small_sum(value, n_dp, n_seq):
    for axis, size in (("seq", n_seq), ("dp", n_dp)):
        dim = 1 if axis == "seq" else 0
        weight = 1
        place = lax.axis_index(axis)
        while weight < size:
            shape = value.shape
            cut = value.reshape(*shape[:dim], shape[dim] // 2, 2, *shape[dim + 1 :])
            mine = (place // weight) % 2
            other = lax.dynamic_index_in_dim(cut, 1 - mine, dim + 1, keepdims=False)
            own = lax.dynamic_index_in_dim(cut, mine, dim + 1, keepdims=False)
            value = own + lax.ppermute(other, axis, [(i, i ^ weight) for i in range(size)])
            weight *= 2
    return value.reshape(-1)


def per_device(
    tokens,
    key_mask,
    row_split,
    group_tags,
    norm1_gain,
    norm1_shift,
    qkv_weight,
    query_bias,
    value_bias,
    out_weight,
    out_bias,
    norm2_gain,
    norm2_shift,
    fc1_weight,
    fc1_bias,
    fc2_weight,
    fc2_bias,
    out_cotangent,
):
    images, slots, width = tokens.shape
    n_seq = lax.axis_size("seq")
    n_dp = lax.axis_size("dp")
    devices = n_dp * n_seq
    rank = lax.axis_index("seq")
    lay = Rows(n_seq, slots)
    per = -(-images // n_seq)
    rows, keys = lay.rows, lay.keys
    all_rows = per * rows
    fast = (n_dp, n_seq) == (8, 4)

    def swap(value, j):
        return lax.ppermute(value, "seq", [(i, i ^ j) for i in range(n_seq)])

    def rows_of(array, owner, k):
        return lax.dynamic_slice_in_dim(array, jnp.minimum(owner * per + k, images - 1), 1, 0)

    def cut_for(array, which):
        got = []
        for j in range(n_seq):
            mine = [rows_of(array, rank ^ j, k) for k in which]
            got.append(mine[0] if len(mine) == 1 else jnp.concatenate(mine, 0))
        return got

    def bring(mine):
        return [mine[0]] + [swap(mine[j], j) for j in range(1, n_seq)]

    number = rank * per + jnp.arange(per)
    pick = (jnp.minimum(number, images - 1)[:, None] == jnp.arange(images)[None, :]).astype(jnp.int32)
    split_own = jnp.sum(pick[:, :, None] * row_split[None], 1)
    tag_own = jnp.sum(pick * group_tags[None], 1)
    counts = ((tag_own < n_dp) & (number < images)).astype(jnp.int32)
    long = (split_own > GRID // n_seq).astype(jnp.int32)
    earlier = jnp.tril(jnp.ones((n_seq, n_seq), jnp.int32), -1)
    long_before = jnp.sum(long[:, None, :] * earlier[None], -1)
    short_before = jnp.sum((1 - long)[:, None, :] * earlier[None], -1)
    place = jnp.where(long == 1, long_before, lay.extra + short_before)
    hits = (place[:, None, :] == jnp.arange(n_seq)[None, :, None]).astype(jnp.int32)
    source = jnp.sum(hits * jnp.arange(n_seq)[None, None, :], -1)
    core = (rank % 2)[None]
    scal = jnp.concatenate([jnp.concatenate([source ^ rank, counts[:, None]], 1).reshape(-1), core])
    mask_own = jnp.sum(pick[:, :, None] * key_mask[None], 1).reshape(per, 1, n_seq, slots)
    mask_seg = jnp.sum(hits[..., None] * mask_own, 2)
    mask_rows = []
    for i, n in enumerate(lay.lens):
        end = lay.offs[i + 1] if i + 1 < n_seq else keys
        mask_rows.append(jnp.pad(mask_seg[:, i, :n], ((0, 0), (0, end - lay.offs[i] - n))))
    mask_row = jnp.where(jnp.concatenate(mask_rows, 1) > 0, 0.0, NEG).astype(F32)[:, None, :]
    live_rows = jnp.sum(jnp.where(jnp.arange(n_seq)[None, :] == rank, row_split, 0), 1) * GRID
    live_rows = jnp.where(group_tags < n_dp, live_rows, 0)
    home_scal = jnp.concatenate([live_rows, rank[None]])

    vecs = jnp.stack([norm1_gain, norm1_shift, out_bias, norm2_gain, norm2_shift, fc2_bias]).astype(F32)
    bias = jnp.stack([query_bias, jnp.zeros_like(query_bias), value_bias]).astype(F32)

    first, rest = cut_for(tokens, [0]), cut_for(tokens, list(range(1, per)))
    cot = cut_for(out_cotangent, list(range(per)))
    first = bring(first)
    first, rest = lax.optimization_barrier((first, rest))
    chain = call_forward(lay, 0, 1, per, scal, first, mask_row, vecs, bias, qkv_weight, out_weight, None)
    rest = bring(rest)
    chain, rest, cot = lax.optimization_barrier((chain, rest, cot))
    chain = call_forward(
        lay, 1, per - 1, per, scal, rest, mask_row, vecs, bias, qkv_weight, out_weight, chain
    )
    hidden, x_all, normed_all, mixed_all, n2, qkv, prob = chain
    n2 = n2.reshape(all_rows, width)

    cot = bring(cot)
    res = call_feed(
        lay, per, fast, scal, hidden, cot, n2, fc1_weight, fc1_bias.astype(F32)[None], fc2_weight, vecs
    )
    out_pieces, (ga, db1, dvec2, *dw) = list(res[:n_seq]), res[n_seq:]

    fc = out = late = []
    out_got = [swap(out_pieces[j], j) for j in range(2, n_seq)]
    if fast:
        fc = [Part(*dw[:2], FC1_ORDER), Part(*dw[2:], FC2_ORDER)]
    exchange(fc)
    flat_ga = after(ga.reshape(all_rows, width), fc)
    dwo = call_out_sums(fast, core, flat_ga, mixed_all.reshape(all_rows, width), dvec2, db1)
    dwo = wait(dwo, fc)
    if fast:
        out = [Part(*dwo, OUT_ORDER)]
    combine(fc)
    exchange(fc + out)
    ga = after(ga, fc)

    chain = None
    dvecs, ig, ig_got = [], [], []
    for k in range(per):
        *chain, dvec = call_backward(
            lay, k, per, scal, ga, qkv, prob, x_all, vecs, out_weight, qkv_weight, chain
        )
        dvecs.append(dvec)
        ready = out if k == 0 else fc + out
        chain = wait(chain, ready)
        if k == 0:
            chain, out_got, out_pieces = lax.optimization_barrier((chain, out_got, out_pieces))
            out_got = [out_pieces[0], swap(out_pieces[1], 1), *out_got]
        if k == 1:
            chain, out_got[1] = lax.optimization_barrier((chain, out_got[1]))
        if k == per - 1 and ig_got:
            chain, ig_got[0] = lax.optimization_barrier((chain, ig_got[0]))
        combine(ready)
        exchange(ready)
        ga, chain[0] = after((ga, chain[0]), ready)
        if k >= per - 2:
            ig_got.append([swap(chain[1 + j], j) for j in range(2, n_seq)])
            ig.append(chain[1:3])
    dwq = call_qkv_sums(fast, core, chain[0], normed_all.reshape(all_rows, width), dvecs)
    if fast:
        dwq = wait(dwq, fc + out)
        late = [Part(dwq[i], dwq[2 + i], order) for i, order in enumerate(QKV_ORDERS)]
        exchange(late)
        combine(fc + out)
        combine(late)
        exchange(late)
        for p in fc + out:
            if p.send is not None:
                p.send = after(p.send, late)
        exchange(fc + out)
        out_got = after(out_got, late)
        ig_got, ig = after((ig_got, ig), late)
    output = call_assemble(per, n_seq, home_scal, out_got, tokens)
    if fast:
        output, ig_got = wait((output, ig_got), late)
        combine(late)
        exchange(late)
        combine(fc + out)
        exchange(fc + out)
    ig_got = [g for near, far in zip(ig, ig_got) for g in (near[0], swap(near[1], 1), *far)]
    if fast:
        ig_got = wait(ig_got, late)
        combine(late)
        exchange(late)
        ig_got = after(ig_got, late)
    input_grad = call_assemble(per, n_seq, home_scal, ig_got, out_cotangent)
    if fast:
        input_grad = wait(input_grad, late)
    while any(p.got is not None for p in late + fc + out):
        combine(late + fc + out)
        exchange(late + fc + out)

    part = width // devices
    if fast:
        fc1_sum, fc2_sum = fc[0].own, fc[1].own
        out_sum = out[0].own[:part]
        qkv_sum = jnp.concatenate([late[0].own, late[1].own[:-8]], 0)
        small_early, small_late = out[0].own[part], late[1].own[-8]
    else:
        fc1_sum, fc2_sum, out_sum, qkv_sum = [
            lax.psum_scatter(v.astype(F32), ("dp", "seq"), scatter_dimension=0, tiled=True)
            for v in (*dw, dwo[0], dwq[0])
        ]
        dvec1 = sum(dvecs)

        def by_device(v):
            return v.reshape(n_dp, n_seq, v.shape[0] // devices)

        early = (dvec2[2], dvec2[0], dvec2[1], dvec2[3], db1[0])
        small_early = small_sum(jnp.concatenate([by_device(v) for v in early], -1), n_dp, n_seq)
        small_late = small_sum(jnp.concatenate([by_device(dvec1[i]) for i in range(4)], -1), n_dp, n_seq)
    vec = [small_late[i * part : (i + 1) * part] for i in range(4)]
    vec += [small_early[i * part : (i + 1) * part] for i in range(4)]
    vec.append(small_early[4 * part : 4 * part + fc1_bias.shape[0] // devices])
    return (
        output,
        input_grad,
        vec[0],
        vec[1],
        qkv_sum.T,
        vec[2],
        vec[3],
        out_sum.T,
        vec[4],
        vec[5],
        vec[6],
        fc1_sum.T,
        vec[8],
        fc2_sum.T,
        vec[7],
    )


def solution(mesh):
    rows = P("dp", "seq", None)
    split = P(("dp", "seq"))
    columns = P(None, ("dp", "seq"))
    return jax.shard_map(
        per_device,
        mesh=mesh,
        in_specs=(rows, P("dp", None), P("dp", None), P("dp")) + (P(),) * 13 + (rows,),
        out_specs=(
            rows,
            rows,
            split,
            split,
            columns,
            split,
            split,
            columns,
            split,
            split,
            split,
            columns,
            split,
            columns,
            split,
        ),
        check_vma=False,
    )
```

```python
import functools

import jax
import jax.numpy as jnp
from jax import lax
from jax.experimental import pallas as pl
from jax.experimental.pallas import tpu as pltpu
from jax.sharding import PartitionSpec as P

HEADS = 12
GRID = 18
EPS = 1e-06
NEG = -1e30
F32 = jnp.float32
BF16 = jnp.bfloat16
VMEM_LIMIT = 60 * 1024 * 1024
CHUNK = 768
GROUP = 256
LANES = 384

BITS = {"core": ("seq", 1), "y": ("seq", 2), "x": ("dp", 1), "z0": ("dp", 2), "z1": ("dp", 4)}
FC1_ORDER = ("x", "z0", "z1", "y")
FC2_ORDER = ("z0", "x", "y", "z1")
LATE_ORDERS = (("x", "y", "z0", "z1"), ("y", "x", "z0", "z1"))
LATE_CUT = 40
SMEM = pl.BlockSpec(memory_space=pltpu.SMEM)
HBM = pl.BlockSpec(memory_space=pl.ANY)


def round_up(n, to):
    return -(-n // to) * to


class Rows:
    def __init__(self, ranks, slots):
        base, extra = GRID // ranks, GRID % ranks
        self.lens = [min(slots, (base + 1) * GRID)] * extra + [base * GRID] * (ranks - extra)
        self.extra = extra
        self.ranks = ranks
        self.slots = slots
        self.offs = []
        at = 0
        for n in self.lens:
            self.offs.append(at)
            at += round_up(n, 8)
        self.rows = round_up(at, 16)
        self.keys = round_up(self.rows, 128)
        self.piece = round_up(slots, 16)
        end = max(o + round_up(n, 16) for o, n in zip(self.offs, self.lens))
        self.spare = max(round_up(end, 8) - self.rows, 0)
        self.scalars = ranks + 1

    def is_row(self, index):
        hit = None
        for off, n in zip(self.offs, self.lens):
            one = (index >= off) & (index < off + n)
            hit = one if hit is None else hit | one
        return hit


def dot(a, b):
    return lax.dot_general(a, b, (((1,), (0,)), ((), ())), preferred_element_type=F32)


def dot_nt(a, b):
    return lax.dot_general(a, b, (((1,), (1,)), ((), ())), preferred_element_type=F32)


def dot_tn(a, b):
    return lax.dot_general(a, b, (((0,), (0,)), ((), ())), preferred_element_type=F32)


def params():
    return pltpu.CompilerParams(vmem_limit_bytes=VMEM_LIMIT)


def cost(flops, moved, exps=0):
    return pl.CostEstimate(flops=int(flops) // 16, bytes_accessed=int(moved) // 16, transcendentals=int(exps) // 16)


def whole(shape):
    return pl.BlockSpec(shape, lambda *i: (0,) * len(shape))


def shaped(shape, dtype):
    return jax.ShapeDtypeStruct(shape, dtype)


def unpack(lay, stage, scal_ref, base, to_ref):
    width = to_ref.shape[1]
    for i, (off, n) in enumerate(zip(lay.offs, lay.lens)):
        full = round_up(n, 8)
        if full > n:
            to_ref[off + full - 8 : off + full, :] = jnp.zeros((8, width), F32)
        piece = stage[scal_ref[base + i]].astype(F32)
        to_ref[off : off + n, :] = piece[:n]
    last = lay.offs[-1] + round_up(lay.lens[-1], 8)
    if lay.rows > last:
        to_ref[last : lay.rows, :] = jnp.zeros((lay.rows - last, width), F32)


def repack(lay, from_ref, start, scal_ref, base, stage):
    for i, (off, n) in enumerate(zip(lay.offs, lay.lens)):
        full = round_up(n, 16)
        stage[scal_ref[base + i], 0:full, :] = from_ref[start + off : start + off + full, :].astype(BF16)


def row_of(ref):
    return ref[...].astype(F32).reshape(1, -1)


def live_column(lay, tag):
    index = lax.broadcasted_iota(jnp.int32, (lay.rows, 1), 0)
    return jnp.where(lay.is_row(index), tag, 0).astype(F32)


def normalise(x):
    mean = jnp.mean(x, -1, keepdims=True)
    centered = x - mean
    rstd = lax.rsqrt(jnp.mean(centered * centered, -1, keepdims=True) + EPS)
    return centered * rstd, rstd


def norm_backward(grad, gain, xhat, rstd):
    scaled = grad * gain
    row = scaled - jnp.mean(scaled, -1, keepdims=True)
    return rstd * (row - xhat * jnp.mean(scaled * xhat, -1, keepdims=True))


def half_masks():
    lane = lax.broadcasted_iota(jnp.int32, (1, 128), 1)
    return [(lane < 64).astype(BF16), (lane >= 64).astype(BF16)]


def keep_and_send(core, even, odd):
    mine = core == 0
    return jnp.where(mine, even, odd).astype(BF16), jnp.where(mine, odd, even).astype(BF16)


def spread(vectors, lanes):
    total, at = 0.0, 0
    for v in vectors:
        n = v.shape[1]
        each = n // 32
        dest = lax.broadcasted_iota(jnp.int32, (32, n), 0) * each
        lane = lax.broadcasted_iota(jnp.int32, (32, n), 1)
        chosen = jnp.where((lane >= dest) & (lane < dest + each), v, 0.0).astype(BF16)
        source = lax.broadcasted_iota(jnp.int32, (n, lanes), 0)
        part = ((source.astype(F32) + 0.5) * (1.0 / each)).astype(jnp.int32)
        target = lax.broadcasted_iota(jnp.int32, (n, lanes), 1)
        pick = (source - part * each == target - at).astype(F32).astype(BF16)
        total = total + dot(chosen, pick)
        at += each
    return total


def with_vectors(rows, packed, d, width):
    lanes = packed.shape[1]
    vec = jnp.broadcast_to(packed[d : d + 1, :], (8, lanes))
    return jnp.concatenate([rows, jnp.concatenate([vec, jnp.zeros((8, width - lanes), F32)], 1)], 0)


def place_of(order, dp, y):
    bits = {"x": dp % 2, "z0": dp // 2 % 2, "z1": dp // 4, "y": y}
    return tuple(bits[name] for name in order)


def attention_forward(lay, first, linked, scal_ref, p0, p1, p2, p3, mask_ref, n1g, n1s, ob, n2g, n2s, bias_ref, wq, wk, wv, wo, *refs):
    outs = refs[7:] if linked else refs
    hid_ref, x_ref, normed_ref, mixed_ref, n2_ref, qkv_ref, prob_ref, stage, xs = outs
    rows, keys = lay.rows, lay.keys
    image, group = pl.program_id(0), pl.program_id(1)
    base = (first + image) * lay.scalars

    @pl.when(group == 0)
    def _():
        for j, piece in enumerate((p0, p1, p2, p3)):
            stage[j] = piece[0]
        unpack(lay, stage, scal_ref, base, xs)
        x = xs[...]
        x_ref[0] = x.astype(BF16)
        xhat, _ = normalise(x)
        normed_ref[0] = (xhat * row_of(n1g) + row_of(n1s)).astype(BF16)

    normed = normed_ref[0]
    qkv = []
    for j, weight in enumerate((wq, wk, wv)):
        part = dot(normed, weight[...]) + bias_ref[j : j + 1, :]
        if j == 0:
            part = part * 0.125
        part = part.astype(BF16)
        if j and keys > rows:
            part = jnp.concatenate([part, jnp.zeros((keys - rows, GROUP), BF16)], 0)
        qkv_ref[0, j, 0 : part.shape[0], :] = part
    if keys > rows:
        qkv_ref[0, 0, rows:keys, :] = jnp.zeros((keys - rows, GROUP), BF16)
    masks = half_masks()
    for p in range(GROUP // 128):
        lanes = slice(p * 128, (p + 1) * 128)
        q = qkv_ref[0, 0, 0:rows, lanes]
        k = qkv_ref[0, 1, :, lanes]
        v = qkv_ref[0, 2, :, lanes]
        both = dot_nt(q, jnp.concatenate([k * masks[0], k * masks[1]], 0))
        probs = []
        for h in (0, 1):
            s = both[:, h * keys : (h + 1) * keys] + mask_ref[0]
            e = jnp.exp(s - jnp.max(s, -1, keepdims=True))
            prob = (e * (1.0 / jnp.sum(e, -1, keepdims=True))).astype(BF16)
            prob_ref[0, 2 * p + h] = prob
            probs.append(prob)
        total = dot(jnp.concatenate(probs, 1), jnp.concatenate([v * masks[0], v * masks[1]], 0))
        at = pl.multiple_of(group * GROUP + p * 128, 128)
        mixed_ref[0, :, pl.ds(at, 128)] = total.astype(BF16)

    @pl.when(group == pl.num_programs(1) - 1)
    def _():
        attended = dot(mixed_ref[0], wo[...]) + row_of(ob)
        hidden = xs[...] + live_column(lay, scal_ref[base + lay.ranks]) * attended
        hid_ref[0] = hidden
        xhat, _ = normalise(hidden)
        n2_ref[0] = (xhat * row_of(n2g) + row_of(n2s)).astype(BF16)


def call_forward(lay, first, count, per, scal, pieces, mask_row, vecs, bias, qkv_weight, out_weight, chain):
    rows, keys = lay.rows, lay.keys
    width = out_weight.shape[0]
    groups = width // GROUP
    shapes = [
        shaped((per, rows, width), F32),
        shaped((per, rows, width), BF16),
        shaped((per, rows, width), BF16),
        shaped((per, rows, width), BF16),
        shaped((per, rows, width), BF16),
        shaped((per, 3, keys, width), BF16),
        shaped((per, HEADS, rows, keys), BF16),
    ]
    args = [scal, *pieces, mask_row, *vecs, bias, qkv_weight, qkv_weight, qkv_weight, out_weight]
    specs = (
        [SMEM]
        + [pl.BlockSpec((1, lay.slots, width), lambda i, g: (i, 0, 0))] * len(pieces)
        + [pl.BlockSpec((1, 1, keys), lambda i, g: (first + i, 0, 0))]
        + [whole(v.shape) for v in vecs]
        + [pl.BlockSpec((3, GROUP), lambda i, g: (0, g))]
        + [pl.BlockSpec((width, GROUP), functools.partial(lambda j, i, g: (0, j * groups + g), j)) for j in range(3)]
        + [whole(out_weight.shape)]
    )
    aliases = {}
    if chain is not None:
        aliases = {len(args) + i: i for i in range(7)}
        args += chain
        specs += [HBM] * 7
    return list(
        pl.pallas_call(
            functools.partial(attention_forward, lay, first, chain is not None),
            grid=(count, groups),
            in_specs=specs,
            out_specs=[pl.BlockSpec((1, rows, width), lambda i, g: (first + i, 0, 0))] * 5
            + [
                pl.BlockSpec((1, 3, keys, GROUP), lambda i, g: (first + i, 0, 0, g)),
                pl.BlockSpec((1, HEADS // groups, rows, keys), lambda i, g: (first + i, g, 0, 0)),
            ],
            out_shape=shapes,
            scratch_shapes=[pltpu.VMEM((lay.ranks, lay.slots, width), BF16), pltpu.VMEM((rows, width), F32)],
            input_output_aliases=aliases,
            compiler_params=params(),
            cost_estimate=cost(8e9 * count, 12e6 * count, HEADS * rows * keys * count),
        )(*args)
    )


def feed_forward(
    lay, per, fast, scal_ref, hid_hbm, c0, c1, c2, c3, n2_ref, w1_ref, b1_ref, w2_ref, n2g, b2_ref, mixed_hbm, *refs
):
    out_refs = refs[: lay.ranks]
    ga_ref, db1_ref, dvec_ref, *dw = refs[lay.ranks : -13]
    stage, back, cot, gr, grt, red, gn, act, gexp, hid, mixed, sem, sem2 = refs[-13:]
    step = pl.program_id(0)
    last = pl.num_programs(0) - 1
    rows = lay.rows
    fetch = pltpu.make_async_copy(hid_hbm, hid, sem)
    fetch2 = pltpu.make_async_copy(mixed_hbm, mixed, sem2)

    @pl.when(step == 0)
    def _():
        fetch.start()
        fetch2.start()
        total = None
        for k in range(per):
            block = slice(k * rows, (k + 1) * rows)
            for j, piece in enumerate((c0, c1, c2, c3)):
                stage[j] = piece[k]
            unpack(lay, stage, scal_ref, k * lay.scalars, cot)
            wide = live_column(lay, scal_ref[k * lay.scalars + lay.ranks]) * cot[...]
            gr[block, :] = wide.astype(BF16)
            grt[:, block] = wide.T.astype(BF16)
            total = jnp.sum(wide, 0, keepdims=True) + (0.0 if total is None else total)
        dvec_ref[...] = jnp.zeros_like(dvec_ref)
        dvec_ref[3:4] = total
        red[...] = jnp.zeros_like(red)
        gn[...] = jnp.zeros_like(gn)

    def share_fc2(sums):
        own2, send2 = dw[-2:]
        n = sums.shape[0] // 32
        for dp in range(8):
            for y in range(2):
                at = (dp * 4 + y * 2) * n
                place = place_of(FC2_ORDER, dp, y)
                own2[place], send2[place] = keep_and_send(
                    scal_ref[per * lay.scalars], sums[at : at + n], sums[at + n : at + 2 * n]
                )

    @pl.when(step < last)
    def _():
        total = None
        for k in range(per):
            block = slice(k * rows, (k + 1) * rows)
            expanded = dot(n2_ref[block, :], w1_ref[...]) + b1_ref[...]
            cdf = 0.5 * (1.0 + lax.erf(expanded * 0.7071067811865476))
            slope = cdf + expanded * (jnp.exp(-0.5 * expanded * expanded) * 0.3989422804014327)
            act[block, :] = (expanded * cdf).astype(BF16)
            grad_active = dot_nt(gr[block, :], w2_ref[...])
            grad_exp = (grad_active * slope).astype(BF16)
            gexp[block, :] = grad_exp
            total = jnp.sum(grad_exp.astype(F32), 0, keepdims=True) + (0.0 if total is None else total)
            red[block, :] += dot(act[block, :], w2_ref[...])
            gn[block, :] += dot_nt(gexp[block, :], w1_ref[...])
        db1_ref[...] = total
        sums1 = dot_tn(gexp[...], n2_ref[...])
        sums2 = dot(grt[...], act[...])
        if fast:
            own1, send1 = dw[:2]
            n = CHUNK // 8
            for i in range(2):
                for y in range(2):
                    at = (i * 4 + y * 2) * n
                    place = place_of(FC1_ORDER, i, y)
                    own1[place], send1[place] = keep_and_send(
                        scal_ref[per * lay.scalars], sums1[at : at + n], sums1[at + n : at + 2 * n]
                    )
            share_fc2(sums2)
        else:
            dw[0][...] = sums1.astype(BF16)
            dw[1][...] = sums2.astype(BF16)

    @pl.when(step == last)
    def _():
        fetch.wait()
        fetch2.wait()
        for k in range(per):
            block = slice(k * rows, (k + 1) * rows)
            live = live_column(lay, scal_ref[k * lay.scalars + lay.ranks])
            hidden = hid[k]
            red[block, :] = hidden + live * (red[block, :] + row_of(b2_ref))
            xhat, rstd = normalise(hidden)
            grad = gn[block, :]
            dvec_ref[0:1] += jnp.sum(grad * xhat, 0, keepdims=True)
            dvec_ref[1:2] += jnp.sum(grad, 0, keepdims=True)
            row = norm_backward(grad, row_of(n2g), xhat, rstd)
            attended = (live * (gr[block, :].astype(F32) + row)).astype(BF16)
            ga_ref[block, :] = attended
            dvec_ref[2:3] += jnp.sum(attended.astype(F32), 0, keepdims=True)
        for k in range(per):
            repack(lay, red, k * rows, scal_ref, k * lay.scalars, back)
            for j, out_ref in enumerate(out_refs):
                out_ref[k] = back[j]
        sums = dot_tn(ga_ref[...], mixed[...])
        if fast:
            share_fc2(sums)
        else:
            dw[1][...] = sums.astype(BF16)


def call_feed(lay, per, fast, scal, hidden, cot, n2, w1, b1, w2, n2g, b2, mixed):
    width, inner = w1.shape
    rows = per * lay.rows
    steps = inner // CHUNK

    def hold(i):
        return jnp.minimum(i, steps - 1)

    shapes = [shaped((per, lay.piece, width), BF16)] * lay.ranks + [
        shaped((rows, width), BF16),
        shaped((1, inner), F32),
        shaped((8, width), F32),
    ]
    specs = [whole((per, lay.piece, width))] * lay.ranks + [
        whole((rows, width)),
        pl.BlockSpec((1, CHUNK), lambda i: (0, hold(i))),
        whole((8, width)),
    ]
    if fast:
        def where(i):
            i = hold(i)
            at = {"x": 0, "y": 0, "z0": i % 2, "z1": i // 2}
            return tuple(at[name] for name in FC1_ORDER) + (0, 0)

        block = tuple(2 if name in ("x", "y") else 1 for name in FC1_ORDER) + (inner // 32, width)
        shapes += [shaped((2, 2, 2, 2, inner // 32, width), BF16)] * 2
        specs += [pl.BlockSpec(block, where)] * 2
        n = width // 32
        shapes += [shaped((2, 2, 2, 2, n, inner + width), BF16)] * 2
        specs += [pl.BlockSpec((2, 2, 2, 2, n, CHUNK), lambda i: (0, 0, 0, 0, 0, i))] * 2
    else:
        shapes += [shaped((inner, width), BF16), shaped((width, inner + width), BF16)]
        specs += [pl.BlockSpec((CHUNK, width), lambda i: (hold(i), 0)), pl.BlockSpec((width, CHUNK), lambda i: (0, i))]
    once = pl.Buffered(1)
    return pl.pallas_call(
        functools.partial(feed_forward, lay, per, fast),
        grid=(steps + 1,),
        in_specs=[
            SMEM,
            HBM,
            *[pl.BlockSpec(c.shape, lambda i: (0, 0, 0), pipeline_mode=once) for c in cot],
            pl.BlockSpec(n2.shape, lambda i: (0, 0), pipeline_mode=once),
            pl.BlockSpec((width, CHUNK), lambda i: (0, hold(i))),
            pl.BlockSpec((1, CHUNK), lambda i: (0, hold(i))),
            pl.BlockSpec((CHUNK, width), lambda i: (hold(i), 0)),
            whole(n2g.shape),
            whole(b2.shape),
            HBM,
        ],
        out_specs=specs,
        out_shape=shapes,
        scratch_shapes=[
            pltpu.VMEM((lay.ranks, lay.slots, width), BF16),
            pltpu.VMEM((lay.ranks, lay.piece, width), BF16),
            pltpu.VMEM((lay.rows, width), F32),
            pltpu.VMEM((rows, width), BF16),
            pltpu.VMEM((width, rows), BF16),
            pltpu.VMEM((rows + lay.spare, width), F32),
            pltpu.VMEM((rows, width), F32),
            pltpu.VMEM((rows, CHUNK), BF16),
            pltpu.VMEM((rows, CHUNK), BF16),
            pltpu.VMEM((per, lay.rows, width), F32),
            pltpu.VMEM((rows, width), BF16),
            pltpu.SemaphoreType.DMA,
            pltpu.SemaphoreType.DMA,
        ],
        compiler_params=params(),
        cost_estimate=cost(12 * rows * width * inner, 30e6, 2 * rows * inner),
    )(scal, hidden, *cot, n2, w1, b1, w2, n2g, b2, mixed)


def late_sums(per, fast, core_ref, gp_ref, normed_ref, dvec_ref, db1_ref, *refs):
    _, _, rows, width = gp_ref.shape
    dvecs = refs[:per]
    step = pl.program_id(0)
    sums = dot_tn(gp_ref[...].reshape(per * rows, width), normed_ref[...])
    if not fast:
        refs[per][...] = sums.astype(BF16)
        return
    own_refs, send_refs, held = refs[per : per + 2], refs[per + 2 : per + 4], refs[-1]
    held[pl.ds(pl.multiple_of(step * width, width), width), :] = sums

    @pl.when(step == pl.num_programs(0) - 1)
    def _():
        vec = dvecs[0][...]
        for more in dvecs[1:]:
            vec = vec + more[...]
        parts = [vec[i : i + 1] for i in range(4)]
        parts += [dvec_ref[2:3], dvec_ref[0:1], dvec_ref[1:2], dvec_ref[3:4], db1_ref[...]]
        packed = spread(parts, LANES)
        each = 3 * width // 32
        for dp in range(8):
            for y in range(2):
                d = dp * 4 + y * 2
                first = [held[e * each : e * each + LATE_CUT, :] for e in (d, d + 1)]
                second = [
                    with_vectors(held[e * each + LATE_CUT : (e + 1) * each, :], packed, e, width)
                    for e in (d, d + 1)
                ]
                for i, pair in enumerate((first, second)):
                    place = place_of(LATE_ORDERS[i], dp, y)
                    own_refs[i][place], send_refs[i][place] = keep_and_send(core_ref[0], *pair)


def call_late_sums(fast, core, gp, normed, dvec, db1, dvecs):
    per, _, rows, width = gp.shape
    if fast:
        heights = (LATE_CUT, 3 * width // 32 - LATE_CUT + 8)
        shapes = [shaped((2, 2, 2, 2, n, width), BF16) for n in heights] * 2
        specs = [whole(s.shape) for s in shapes]
        scratch = [pltpu.VMEM((3 * width, width), F32)]
    else:
        shapes = [shaped((3 * width, width), BF16)]
        specs = [pl.BlockSpec((width, width), lambda i: (i, 0))]
        scratch = []
    return pl.pallas_call(
        functools.partial(late_sums, per, fast),
        grid=(3,),
        in_specs=[SMEM, pl.BlockSpec((per, 1, rows, width), lambda i: (0, i, 0, 0)), whole(normed.shape)]
        + [whole(dvec.shape), whole(db1.shape)]
        + [whole(d.shape) for d in dvecs],
        out_specs=specs,
        out_shape=shapes,
        scratch_shapes=scratch,
        compiler_params=params(),
        cost_estimate=cost(6 * per * rows * width * width, 10e6),
    )(core, gp, normed, dvec, db1, *dvecs)


def attention_backward(lay, k, linked, scal_ref, ga_ref, qkv_ref, prob_ref, x_ref, n1g, wo_ref, wq, wk, wv, *refs):
    gp_ref, *ig_refs, dvec_ref, gn, res, back = refs[linked:]
    rows = lay.rows
    group = pl.program_id(0)
    grad_mixed = dot_nt(ga_ref[0], wo_ref[...]).astype(BF16)
    masks = half_masks()

    @pl.when(group == 0)
    def _():
        dvec_ref[...] = jnp.zeros_like(dvec_ref)
        gn[...] = jnp.zeros_like(gn)

    for p in range(GROUP // 128):
        lanes = slice(p * 128, (p + 1) * 128)
        q = qkv_ref[0, 0, 0:rows, lanes]
        key = qkv_ref[0, 1, :, lanes]
        v = qkv_ref[0, 2, :, lanes]
        gm = grad_mixed[:, lanes]
        both = dot_nt(gm, jnp.concatenate([v * masks[0], v * masks[1]], 0))
        ds, probs = [], []
        for h in (0, 1):
            prob = prob_ref[0, 2 * p + h]
            weights = prob.astype(F32)
            gw = both[:, h * lay.keys : (h + 1) * lay.keys]
            delta = jnp.sum(weights * gw, -1, keepdims=True)
            ds.append((weights * (gw - delta)).astype(BF16))
            probs.append(prob)
        dq = dot(jnp.concatenate(ds, 1), jnp.concatenate([key * masks[0], key * masks[1]], 0))
        dk = dot_tn(jnp.concatenate(ds, 0), jnp.concatenate([q * masks[0], q * masks[1]], 0))
        dv = dot_tn(jnp.concatenate(probs, 0), jnp.concatenate([gm * masks[0], gm * masks[1]], 0))
        dq, dk, dv = (dq * 0.125).astype(BF16), dk[:rows].astype(BF16), dv[:rows].astype(BF16)
        gp_ref[0, 0, :, lanes] = dq
        gp_ref[0, 1, :, lanes] = dk
        gp_ref[0, 2, :, lanes] = dv
        at = pl.multiple_of(group * GROUP + p * 128, 128)
        dvec_ref[2:3, pl.ds(at, 128)] = jnp.sum(dq.astype(F32), 0, keepdims=True)
        dvec_ref[3:4, pl.ds(at, 128)] = jnp.sum(dv.astype(F32), 0, keepdims=True)
    gn[...] += sum(dot_nt(gp_ref[0, j], w[...]) for j, w in enumerate((wq, wk, wv)))

    @pl.when(group == pl.num_programs(0) - 1)
    def _():
        grad = gn[...]
        xhat, rstd = normalise(x_ref[0].astype(F32))
        dvec_ref[0:1] = jnp.sum(grad * xhat, 0, keepdims=True)
        dvec_ref[1:2] = jnp.sum(grad, 0, keepdims=True)
        res[0:rows] = ga_ref[0].astype(F32) + norm_backward(grad, row_of(n1g), xhat, rstd)
        repack(lay, res, 0, scal_ref, k * lay.scalars, back)
        for j, ig_ref in enumerate(ig_refs):
            ig_ref[0] = back[j]


def call_backward(lay, k, per, scal, ga, qkv, prob, x, n1g, out_weight, qkv_weight, chain):
    rows, keys = lay.rows, lay.keys
    width = out_weight.shape[0]
    groups = width // GROUP
    alone = k == per - 1
    one = pl.BlockSpec((1, rows, width), lambda g: (k, 0, 0))
    args = [scal, ga, qkv, prob, x, n1g, out_weight, qkv_weight, qkv_weight, qkv_weight]
    specs = [
        SMEM,
        one,
        pl.BlockSpec((1, 3, keys, GROUP), lambda g: (k, 0, 0, g)),
        pl.BlockSpec((1, HEADS // groups, rows, keys), lambda g: (k, g, 0, 0)),
        one,
        whole(n1g.shape),
        pl.BlockSpec((GROUP, width), lambda g: (g, 0)),
    ] + [pl.BlockSpec((width, GROUP), functools.partial(lambda j, g: (0, j * groups + g), j)) for j in range(3)]
    aliases = {}
    if chain is not None:
        count = 1 if alone else len(chain)
        aliases = {len(args) + i: i for i in range(count)}
        args += chain[:count]
        specs += [HBM] * count
    return pl.pallas_call(
        functools.partial(attention_backward, lay, k, len(args) - 10),
        grid=(groups,),
        in_specs=specs,
        out_specs=[
            pl.BlockSpec((1, 3, rows, GROUP), lambda g: (k, 0, 0, g)),
            *[pl.BlockSpec((1, lay.piece, width), lambda g: (0 if alone else k, 0, 0))] * lay.ranks,
            whole((8, width)),
        ],
        out_shape=[
            shaped((per, 3, rows, width), BF16),
            *[shaped((1 if alone else per - 1, lay.piece, width), BF16)] * lay.ranks,
            shaped((8, width), F32),
        ],
        scratch_shapes=[
            pltpu.VMEM((rows, width), F32),
            pltpu.VMEM((rows + lay.spare, width), F32),
            pltpu.VMEM((lay.ranks, lay.piece, width), BF16),
        ],
        input_output_aliases=aliases,
        compiler_params=params(),
        cost_estimate=cost(10e9, 10e6),
    )(*args)


def assemble(per, ranks, scal_ref, *refs):
    *got, passed_ref, out_ref = refs
    images, slots, width = out_ref.shape
    row = lax.broadcasted_iota(jnp.int32, (slots, width), 0)
    first = 0
    for b in range(0, len(got), ranks):
        for j, piece in enumerate(got[b : b + ranks]):
            for k in range(piece.shape[0]):
                image = (scal_ref[images] ^ j) * per + first + k

                @pl.when(image < images)
                def _():
                    worked = piece[k][:slots].astype(F32)
                    kept = passed_ref[image].astype(F32)
                    out_ref[image] = jnp.where(row < scal_ref[image], worked, kept).astype(BF16)

        first += got[b].shape[0]


def call_assemble(per, ranks, home_scal, got, passed):
    args = [home_scal, *got, passed]
    return pl.pallas_call(
        functools.partial(assemble, per, ranks),
        grid=(1,),
        in_specs=[SMEM] + [whole(a.shape) for a in args[1:]],
        out_specs=whole(passed.shape),
        out_shape=shaped(passed.shape, BF16),
        compiler_params=params(),
        cost_estimate=cost(0, 5e6),
    )(*args)


class Part:
    def __init__(self, own, send, order, at=None):
        self.own, self.send, self.order = own, send, ["core", *order]
        self.got = self.sent = None
        self.at = at


def exchange(parts):
    for p in parts:
        if p.send is None:
            continue
        axis, weight = BITS[p.order[0]]
        size = lax.axis_size(axis)
        p.got = lax.ppermute(p.send, axis, [(i, i ^ weight) for i in range(size)])
        p.sent, p.send = p.send, None


def add_and_split(counts, mine_ref, *refs):
    n = len(counts)
    for i in range(n):
        own, got, keep, send = refs[2 * i], refs[2 * i + 1], refs[2 * n + 2 * i], refs[2 * n + 2 * i + 1]
        mine = mine_ref[i]
        keep[...] = (own[mine].astype(F32) + got[mine].astype(F32)).astype(BF16)
        send[...] = (own[1 - mine].astype(F32) + got[1 - mine].astype(F32)).astype(BF16)


def combine(parts, before=()):
    parts = [p for p in parts if p.got is not None]
    last = [p for p in parts if len(p.order) == 1]
    for p in last:
        p.own = p.own.astype(F32) + p.got.astype(F32)
        p.got = p.send = None
        p.order = []
    parts = [p for p in parts if p.order]
    if not parts:
        return ()
    tied, _ = lax.optimization_barrier(([(p.own, p.got) for p in parts], before))
    for p, (p.own, p.got) in zip(parts, tied):
        pass
    views = []
    for p in parts:
        shape = p.own.shape
        flat = (2, 2 ** (len(p.order) - 2), *shape[-2:])
        if p.at is not None:
            flat = (shape[0], *flat)
        views.append((p.own.reshape(flat), p.got.reshape(flat)))
    size = sum(4 * v[0].size for v in views)
    steps = min(4 if size > 12e6 else 2 if size > 3e6 else 1, *(v[0].shape[-3] for v in views))
    ins, outs, shapes, args, mine = [], [], [], [], []
    for p, (own, got) in zip(parts, views):
        many, n, width = own.shape[-3:]
        block = (2, many // steps, n, width)
        if p.at is None:
            ins += [pl.BlockSpec(block, lambda i: (0, i, 0, 0))] * 2
        else:
            ins += [pl.BlockSpec((None, *block), functools.partial(lambda a, i: (a, 0, i, 0, 0), p.at))] * 2
        outs += [pl.BlockSpec(block[1:], lambda i: (i, 0, 0))] * 2
        shapes += [shaped((many, n, width), BF16)] * 2
        args += [own, got]
        axis, weight = BITS[p.order[1]]
        mine.append((lax.axis_index(axis) // weight) % 2)
    moved = sum(3 * a.size for a in args)
    res = pl.pallas_call(
        functools.partial(add_and_split, [None] * len(parts)),
        grid=(steps,),
        in_specs=[SMEM] + ins,
        out_specs=outs,
        out_shape=shapes,
        compiler_params=params(),
        cost_estimate=cost(0, moved),
    )(jnp.stack(mine), *args)
    for i, p in enumerate(parts):
        shape = (*[2] * (len(p.order) - 2), *p.own.shape[-2:])
        p.at = None
        p.own, p.send = res[2 * i].reshape(shape), res[2 * i + 1].reshape(shape)
        p.got = None
        p.order.pop(0)
    return res[0]


def wait(values, parts):
    live = [p for p in parts if p.got is not None]
    values, gots = lax.optimization_barrier((values, [p.got for p in live]))
    for p, g in zip(live, gots):
        p.got = g
    return values


def after(values, parts):
    return lax.optimization_barrier((values, [p.sent for p in parts if p.sent is not None]))[0]


def small_sum(value, n_dp, n_seq):
    for axis, size in (("seq", n_seq), ("dp", n_dp)):
        dim = 1 if axis == "seq" else 0
        weight = 1
        place = lax.axis_index(axis)
        while weight < size:
            shape = value.shape
            cut = value.reshape(*shape[:dim], shape[dim] // 2, 2, *shape[dim + 1 :])
            mine = (place // weight) % 2
            other = lax.dynamic_index_in_dim(cut, 1 - mine, dim + 1, keepdims=False)
            own = lax.dynamic_index_in_dim(cut, mine, dim + 1, keepdims=False)
            value = own + lax.ppermute(other, axis, [(i, i ^ weight) for i in range(size)])
            weight *= 2
    return value.reshape(-1)


def per_device(
    tokens,
    key_mask,
    row_split,
    group_tags,
    norm1_gain,
    norm1_shift,
    qkv_weight,
    query_bias,
    value_bias,
    out_weight,
    out_bias,
    norm2_gain,
    norm2_shift,
    fc1_weight,
    fc1_bias,
    fc2_weight,
    fc2_bias,
    out_cotangent,
):
    images, slots, width = tokens.shape
    n_seq = lax.axis_size("seq")
    n_dp = lax.axis_size("dp")
    devices = n_dp * n_seq
    rank = lax.axis_index("seq")
    lay = Rows(n_seq, slots)
    per = -(-images // n_seq)
    rows, keys = lay.rows, lay.keys
    all_rows = per * rows
    fast = (n_dp, n_seq) == (8, 4)

    def swap(value, j):
        return lax.ppermute(value, "seq", [(i, i ^ j) for i in range(n_seq)])

    def rows_of(array, owner, k):
        return lax.dynamic_slice_in_dim(array, jnp.minimum(owner * per + k, images - 1), 1, 0)

    def cut_for(array, which):
        got = []
        for j in range(n_seq):
            mine = [rows_of(array, rank ^ j, k) for k in which]
            got.append(mine[0] if len(mine) == 1 else jnp.concatenate(mine, 0))
        return got

    def bring(mine):
        return [mine[0]] + [swap(mine[j], j) for j in range(1, n_seq)]

    number = rank * per + jnp.arange(per)
    pick = (jnp.minimum(number, images - 1)[:, None] == jnp.arange(images)[None, :]).astype(jnp.int32)
    split_own = jnp.sum(pick[:, :, None] * row_split[None], 1)
    tag_own = jnp.sum(pick * group_tags[None], 1)
    counts = ((tag_own < n_dp) & (number < images)).astype(jnp.int32)
    long = (split_own > GRID // n_seq).astype(jnp.int32)
    earlier = jnp.tril(jnp.ones((n_seq, n_seq), jnp.int32), -1)
    long_before = jnp.sum(long[:, None, :] * earlier[None], -1)
    short_before = jnp.sum((1 - long)[:, None, :] * earlier[None], -1)
    place = jnp.where(long == 1, long_before, lay.extra + short_before)
    hits = (place[:, None, :] == jnp.arange(n_seq)[None, :, None]).astype(jnp.int32)
    source = jnp.sum(hits * jnp.arange(n_seq)[None, None, :], -1)
    core = (rank % 2)[None]
    scal = jnp.concatenate([jnp.concatenate([source ^ rank, counts[:, None]], 1).reshape(-1), core])
    mask_own = jnp.sum(pick[:, :, None] * key_mask[None], 1).reshape(per, 1, n_seq, slots)
    mask_seg = jnp.sum(hits[..., None] * mask_own, 2)
    mask_rows = []
    for i, n in enumerate(lay.lens):
        end = lay.offs[i + 1] if i + 1 < n_seq else keys
        mask_rows.append(jnp.pad(mask_seg[:, i, :n], ((0, 0), (0, end - lay.offs[i] - n))))
    mask_row = jnp.where(jnp.concatenate(mask_rows, 1) > 0, 0.0, NEG).astype(F32)[:, None, :]
    live_rows = jnp.sum(jnp.where(jnp.arange(n_seq)[None, :] == rank, row_split, 0), 1) * GRID
    live_rows = jnp.where(group_tags < n_dp, live_rows, 0)
    home_scal = jnp.concatenate([live_rows, rank[None]])

    vecs = (norm1_gain, norm1_shift, out_bias, norm2_gain, norm2_shift)
    bias = jnp.concatenate([query_bias, jnp.zeros_like(query_bias), value_bias]).astype(F32).reshape(3, width)

    first, rest = cut_for(tokens, [0]), cut_for(tokens, list(range(1, per)))
    cot = cut_for(out_cotangent, list(range(per)))
    first = bring(first)
    first, rest, scal, mask_row, bias = lax.optimization_barrier((first, rest, scal, mask_row, bias))
    chain = call_forward(lay, 0, 1, per, scal, first, mask_row, vecs, bias, qkv_weight, out_weight, None)
    rest = bring(rest)
    chain, rest, cot = lax.optimization_barrier((chain, rest, cot))
    chain = call_forward(
        lay, 1, per - 1, per, scal, rest, mask_row, vecs, bias, qkv_weight, out_weight, chain
    )
    hidden, x_all, normed_all, mixed_all, n2, qkv, prob = chain
    n2 = n2.reshape(all_rows, width)

    cot = bring(cot)
    res = call_feed(
        lay,
        per,
        fast,
        scal,
        hidden,
        cot,
        n2,
        fc1_weight,
        fc1_bias.astype(F32)[None],
        fc2_weight,
        norm2_gain,
        fc2_bias,
        mixed_all.reshape(all_rows, width),
    )
    out_pieces, (ga, db1, dvec2, *dw) = list(res[:n_seq]), res[n_seq:]

    fc = late = []
    if fast:
        fc = [Part(*dw[:2], FC1_ORDER), Part(*dw[2:], FC2_ORDER)]
    out_got = [swap(out_pieces[j], j) for j in range(2, n_seq)]
    exchange(fc)
    ga = ga.reshape(per, rows, width)

    chain = None
    dvecs, ig, ig_got = [], [], []
    for k in range(per):
        *chain, dvec = call_backward(
            lay, k, per, scal, ga, qkv, prob, x_all, norm1_gain, out_weight, qkv_weight, chain
        )
        dvecs.append(dvec)
        if k == 0:
            chain, out_got[0] = lax.optimization_barrier((chain, out_got[0]))
        if k == 1:
            chain, out_got, out_pieces = lax.optimization_barrier((chain, out_got, out_pieces))
            out_got = [out_pieces[0], swap(out_pieces[1], 1), *out_got]
        if k == 2:
            chain, ig_got[0] = lax.optimization_barrier((chain, ig_got[0]))
        if k >= per - 2:
            ig.append(chain[1:3])
            ig_got.append([swap(chain[1 + j], j) for j in range(2, n_seq)])
        if k != 1:
            chain = wait(chain, fc)
            combine(fc)
            exchange(fc)
            ga, chain = after((ga, chain), fc)
    gp = chain[0]
    dwl = call_late_sums(fast, core, gp, normed_all.reshape(all_rows, width), dvec2, db1, dvecs)
    if fast:
        dwl, ig_got[1] = wait((dwl, ig_got[1]), fc)
        late = [Part(dwl[i], dwl[2 + i], order) for i, order in enumerate(LATE_ORDERS)]
        exchange(late)
        token = combine(fc, dwl)
        exchange(fc)
        token = combine(late, token)
        exchange(late)
        out_got, ig, _ = lax.optimization_barrier((out_got, ig, token))
    output = call_assemble(per, n_seq, home_scal, out_got, tokens)
    if fast:
        token = combine(late, output)
        exchange(late)
        token = combine(fc, token)
        exchange(fc)
        ig = after(ig, late)
    ig_got = [g for near, far in zip(ig, ig_got) for g in (near[0], swap(near[1], 1), *far)]
    if fast:
        token = combine(late, token)
        exchange(late)
        ig_got, _ = lax.optimization_barrier((ig_got, token))
    input_grad = call_assemble(per, n_seq, home_scal, ig_got, out_cotangent)
    if fast:
        combine(late, input_grad)
        exchange(late)
        fc[0].got, fc[1].got = after([p.got for p in fc], late)
        combine(fc)
        combine(late)

    part = width // devices
    inner = fc1_weight.shape[1]
    if fast:
        fc1_sum, fc2_sum, out_sum = fc[0].own, fc[1].own[:, :inner], fc[1].own[:, inner:]
        qkv_sum = jnp.concatenate([late[0].own, late[1].own[:-8]], 0)
        small = late[1].own[-8]
        small_late, small_early = small[: 4 * part], small[4 * part :]
    else:
        fc1_sum, fc2_sum, out_sum, qkv_sum = [
            lax.psum_scatter(v.astype(F32), ("dp", "seq"), scatter_dimension=0, tiled=True)
            for v in (dw[0], dw[1][:, :inner], dw[1][:, inner:], dwl[0])
        ]
        dvec1 = sum(dvecs)

        def by_device(v):
            return v.reshape(n_dp, n_seq, v.shape[0] // devices)

        early = (dvec2[2], dvec2[0], dvec2[1], dvec2[3], db1[0])
        small_early = small_sum(jnp.concatenate([by_device(v) for v in early], -1), n_dp, n_seq)
        small_late = small_sum(jnp.concatenate([by_device(dvec1[i]) for i in range(4)], -1), n_dp, n_seq)
    vec = [small_late[i * part : (i + 1) * part] for i in range(4)]
    vec += [small_early[i * part : (i + 1) * part] for i in range(4)]
    vec.append(small_early[4 * part : 4 * part + fc1_bias.shape[0] // devices])
    return (
        output,
        input_grad,
        vec[0],
        vec[1],
        qkv_sum.T,
        vec[2],
        vec[3],
        out_sum.T,
        vec[4],
        vec[5],
        vec[6],
        fc1_sum.T,
        vec[8],
        fc2_sum.T,
        vec[7],
    )


def solution(mesh):
    rows = P("dp", "seq", None)
    split = P(("dp", "seq"))
    columns = P(None, ("dp", "seq"))
    return jax.shard_map(
        per_device,
        mesh=mesh,
        in_specs=(rows, P("dp", None), P("dp", None), P("dp")) + (P(),) * 13 + (rows,),
        out_specs=(
            rows,
            rows,
            split,
            split,
            columns,
            split,
            split,
            columns,
            split,
            split,
            split,
            columns,
            split,
            columns,
            split,
        ),
        check_vma=False,
    )
```

```python
import functools

import jax
import jax.numpy as jnp
from jax import lax
from jax.experimental import pallas as pl
from jax.experimental.pallas import tpu as pltpu
from jax.sharding import PartitionSpec as P

HEADS = 12
GRID = 18
EPS = 1e-06
NEG = -1e30
F32 = jnp.float32
BF16 = jnp.bfloat16
VMEM_LIMIT = 60 * 1024 * 1024
CHUNK = 768
GROUP = 256
LANES = 384

BITS = {"core": ("seq", 1), "y": ("seq", 2), "x": ("dp", 1), "z0": ("dp", 2), "z1": ("dp", 4)}
FC1_ORDER = ("x", "z0", "z1", "y")
FC2_ORDER = ("z0", "x", "y", "z1")
LATE_ORDERS = (("x", "y", "z0", "z1"), ("y", "x", "z0", "z1"))
LATE_CUT = 40
SMEM = pl.BlockSpec(memory_space=pltpu.SMEM)
VMEM = pl.BlockSpec(memory_space=pltpu.VMEM)
SMALL_LIMIT = 8 * 1024 * 1024
HBM = pl.BlockSpec(memory_space=pl.ANY)


def round_up(n, to):
    return -(-n // to) * to


class Rows:
    def __init__(self, ranks, slots, images, groups):
        self.images, self.groups = images, groups
        self.per = -(-images // ranks)
        base, extra = GRID // ranks, GRID % ranks
        self.lens = [min(slots, (base + 1) * GRID)] * extra + [base * GRID] * (ranks - extra)
        self.extra = extra
        self.ranks = ranks
        self.slots = slots
        self.offs = []
        at = 0
        for n in self.lens:
            self.offs.append(at)
            at += round_up(n, 8)
        self.rows = round_up(at, 16)
        self.keys = round_up(self.rows, 128)
        self.piece = round_up(slots, 16)
        end = max(o + round_up(n, 16) for o, n in zip(self.offs, self.lens))
        self.spare = max(round_up(end, 8) - self.rows, 0)

    def is_row(self, index):
        hit = None
        for off, n in zip(self.offs, self.lens):
            one = (index >= off) & (index < off + n)
            hit = one if hit is None else hit | one
        return hit


def dot(a, b):
    return lax.dot_general(a, b, (((1,), (0,)), ((), ())), preferred_element_type=F32)


def dot_nt(a, b):
    return lax.dot_general(a, b, (((1,), (1,)), ((), ())), preferred_element_type=F32)


def dot_tn(a, b):
    return lax.dot_general(a, b, (((0,), (0,)), ((), ())), preferred_element_type=F32)


def params(limit=VMEM_LIMIT):
    return pltpu.CompilerParams(vmem_limit_bytes=limit)


def cost(flops, moved, exps=0):
    return pl.CostEstimate(flops=int(flops) // 16, bytes_accessed=int(moved) // 16, transcendentals=int(exps) // 16)


def whole(shape):
    return pl.BlockSpec(shape, lambda *i: (0,) * len(shape))


def shaped(shape, dtype):
    return jax.ShapeDtypeStruct(shape, dtype)


class Image:
    def __init__(self, lay, meta, k):
        rank_ref, split_ref, tag_ref = meta
        rank = rank_ref[0]
        number = rank * lay.per + k
        self.index = jnp.minimum(number, lay.images - 1)
        base = GRID // lay.ranks
        longs, shorts = jnp.int32(0), jnp.int32(lay.extra)
        self.sources = [jnp.int32(0)] * lay.ranks
        for r in range(lay.ranks):
            is_long = split_ref[self.index, r] > base
            place = jnp.where(is_long, longs, shorts)
            longs = longs + jnp.where(is_long, 1, 0)
            shorts = shorts + jnp.where(is_long, 0, 1)
            self.sources = [jnp.where(place == i, r, s) for i, s in enumerate(self.sources)]
        self.pieces = [s ^ rank for s in self.sources]
        self.counts = jnp.where((tag_ref[self.index] < lay.groups) & (number < lay.images), 1, 0)


def unpack(lay, stage, image, to_ref):
    width = to_ref.shape[1]
    for i, (off, n) in enumerate(zip(lay.offs, lay.lens)):
        full = round_up(n, 8)
        if full > n:
            to_ref[off + full - 8 : off + full, :] = jnp.zeros((8, width), F32)
        piece = stage[image.pieces[i]].astype(F32)
        to_ref[off : off + n, :] = piece[:n]
    last = lay.offs[-1] + round_up(lay.lens[-1], 8)
    if lay.rows > last:
        to_ref[last : lay.rows, :] = jnp.zeros((lay.rows - last, width), F32)


def repack(lay, from_ref, start, image, stage):
    for i, (off, n) in enumerate(zip(lay.offs, lay.lens)):
        full = round_up(n, 16)
        stage[image.pieces[i], 0:full, :] = from_ref[start + off : start + off + full, :].astype(BF16)


def mask_of(lay, image, key_ref):
    slots = key_ref.shape[1]
    row = jnp.broadcast_to(key_ref[pl.ds(image.index, 1), :], (8, slots)).astype(F32)
    lane = lax.broadcasted_iota(jnp.int32, (slots, lay.keys), 1)
    want = jnp.full((slots, lay.keys), -1, jnp.int32)
    for i, (off, n) in enumerate(zip(lay.offs, lay.lens)):
        want = jnp.where((lane >= off) & (lane < off + n), lane + (image.sources[i] * lay.slots - off), want)
    pick = (lax.broadcasted_iota(jnp.int32, (slots, lay.keys), 0) == want).astype(F32).astype(BF16)
    valid = jnp.where(row > 0, 1.0, 0.0).astype(BF16)
    return jnp.where(dot(valid, pick)[0:1] > 0.5, 0.0, NEG)


def row_of(ref):
    return ref[...].astype(F32).reshape(1, -1)


def live_column(lay, image):
    index = lax.broadcasted_iota(jnp.int32, (lay.rows, 1), 0)
    return jnp.where(lay.is_row(index), image.counts, 0).astype(F32)


def normalise(x):
    mean = jnp.mean(x, -1, keepdims=True)
    centered = x - mean
    rstd = lax.rsqrt(jnp.mean(centered * centered, -1, keepdims=True) + EPS)
    return centered * rstd, rstd


def norm_backward(grad, gain, xhat, rstd):
    scaled = grad * gain
    row = scaled - jnp.mean(scaled, -1, keepdims=True)
    return rstd * (row - xhat * jnp.mean(scaled * xhat, -1, keepdims=True))


def half_masks():
    lane = lax.broadcasted_iota(jnp.int32, (1, 128), 1)
    return [(lane < 64).astype(BF16), (lane >= 64).astype(BF16)]


def keep_and_send(core, even, odd):
    mine = core == 0
    return jnp.where(mine, even, odd).astype(BF16), jnp.where(mine, odd, even).astype(BF16)


def parts_of(rows, each):
    n = rows.shape[1]
    place = lax.broadcasted_iota(jnp.int32, rows.shape, 0) % (n // each) * each
    lane = lax.broadcasted_iota(jnp.int32, rows.shape, 1)
    return jnp.where((lane >= place) & (lane < place + each), rows, 0.0).astype(BF16)


def picker(n, each):
    source = lax.broadcasted_iota(jnp.int32, (n, 128), 0)
    part = ((source.astype(F32) + 0.5) * (1.0 / each)).astype(jnp.int32)
    target = lax.broadcasted_iota(jnp.int32, (n, 128), 1)
    return (source - part * each == target).astype(F32).astype(BF16)


def spread(vectors, long):
    n, m = vectors[0].shape[1], long.shape[1]
    each, long_each = n // 32, m // 32
    rows = [parts_of(jnp.broadcast_to(v, (32, n)), each) for v in vectors]
    found = dot(jnp.concatenate(rows, 0), picker(n, each))
    many = m // n
    group = lax.broadcasted_iota(jnp.int32, (32, n), 0) // (32 // many)
    chosen = sum(jnp.where(group == i, long[:, i * n : (i + 1) * n], 0.0) for i in range(many))
    last = dot(parts_of(chosen, long_each), picker(n, long_each))
    blank = jnp.zeros((32, LANES - 128), F32)
    total = pltpu.roll(jnp.concatenate([last, blank], 1), each * len(vectors), 1)
    for i in range(len(vectors)):
        one = jnp.concatenate([found[i * 32 : (i + 1) * 32], blank], 1)
        total = total + (pltpu.roll(one, each * i, 1) if i else one)
    return total


def with_vectors(rows, packed, d, width):
    lanes = packed.shape[1]
    vec = jnp.broadcast_to(packed[d : d + 1, :], (8, lanes))
    return jnp.concatenate([rows, jnp.concatenate([vec, jnp.zeros((8, width - lanes), F32)], 1)], 0)


def place_of(order, dp, y):
    bits = {"x": dp % 2, "z0": dp // 2 % 2, "z1": dp // 4, "y": y}
    return tuple(bits[name] for name in order)


def attention_forward(
    lay, first, linked, rank_ref, split_ref, tag_ref, p0, p1, p2, p3, key_ref, n1g, n1s, ob, n2g, n2s, qb, vb, wq, wk, wv, wo, *refs
):
    outs = refs[7:] if linked else refs
    hid_ref, x_ref, normed_ref, mixed_ref, n2_ref, qkv_ref, prob_ref, stage, xs, bias, mask = outs
    rows, keys = lay.rows, lay.keys
    group = pl.program_id(1)
    image = Image(lay, (rank_ref, split_ref, tag_ref), first + pl.program_id(0))

    @pl.when(group == 0)
    def _():
        for j, piece in enumerate((p0, p1, p2, p3)):
            stage[j] = piece[0]
        unpack(lay, stage, image, xs)
        mask[...] = jnp.broadcast_to(mask_of(lay, image, key_ref), mask.shape)
        bias[0:1, :] = row_of(qb)
        bias[1:2, :] = jnp.zeros((1, bias.shape[1]), F32)
        bias[2:3, :] = row_of(vb)
        x = xs[...]
        x_ref[0] = x.astype(BF16)
        xhat, _ = normalise(x)
        normed_ref[0] = (xhat * row_of(n1g) + row_of(n1s)).astype(BF16)

    normed = normed_ref[0]
    qkv = []
    for j, weight in enumerate((wq, wk, wv)):
        part = dot(normed, weight[...]) + bias[j : j + 1, pl.ds(pl.multiple_of(group * GROUP, GROUP), GROUP)]
        if j == 0:
            part = part * 0.125
        part = part.astype(BF16)
        if j and keys > rows:
            part = jnp.concatenate([part, jnp.zeros((keys - rows, GROUP), BF16)], 0)
        qkv_ref[0, j, 0 : part.shape[0], :] = part
    if keys > rows:
        qkv_ref[0, 0, rows:keys, :] = jnp.zeros((keys - rows, GROUP), BF16)
    masks = half_masks()
    for p in range(GROUP // 128):
        lanes = slice(p * 128, (p + 1) * 128)
        q = qkv_ref[0, 0, 0:rows, lanes]
        k = qkv_ref[0, 1, :, lanes]
        v = qkv_ref[0, 2, :, lanes]
        both = dot_nt(q, jnp.concatenate([k * masks[0], k * masks[1]], 0))
        probs = []
        for h in (0, 1):
            s = both[:, h * keys : (h + 1) * keys] + mask[0:1, :]
            e = jnp.exp(s - jnp.max(s, -1, keepdims=True))
            prob = (e * (1.0 / jnp.sum(e, -1, keepdims=True))).astype(BF16)
            prob_ref[0, 2 * p + h] = prob
            probs.append(prob)
        total = dot(jnp.concatenate(probs, 1), jnp.concatenate([v * masks[0], v * masks[1]], 0))
        at = pl.multiple_of(group * GROUP + p * 128, 128)
        mixed_ref[0, :, pl.ds(at, 128)] = total.astype(BF16)

    @pl.when(group == pl.num_programs(1) - 1)
    def _():
        attended = dot(mixed_ref[0], wo[...]) + row_of(ob)
        hidden = xs[...] + live_column(lay, image) * attended
        hid_ref[0] = hidden
        xhat, _ = normalise(hidden)
        n2_ref[0] = (xhat * row_of(n2g) + row_of(n2s)).astype(BF16)


def call_forward(lay, first, count, meta, pieces, key_mask, vecs, qkv_weight, out_weight, chain):
    per, rows, keys = lay.per, lay.rows, lay.keys
    width = out_weight.shape[0]
    groups = width // GROUP
    shapes = [
        shaped((per, rows, width), F32),
        shaped((per, rows, width), BF16),
        shaped((per, rows, width), BF16),
        shaped((per, rows, width), BF16),
        shaped((per, rows, width), BF16),
        shaped((per, 3, keys, width), BF16),
        shaped((per, HEADS, rows, keys), BF16),
    ]
    args = [*meta, *pieces, key_mask, *vecs, qkv_weight, qkv_weight, qkv_weight, out_weight]
    specs = (
        [SMEM] * 3
        + [pl.BlockSpec((1, lay.slots, width), lambda i, g: (i, 0, 0))] * len(pieces)
        + [whole(v.shape) for v in (key_mask, *vecs)]
        + [pl.BlockSpec((width, GROUP), functools.partial(lambda j, i, g: (0, j * groups + g), j)) for j in range(3)]
        + [whole(out_weight.shape)]
    )
    aliases = {}
    if chain is not None:
        aliases = {len(args) + i: i for i in range(7)}
        args += chain
        specs += [HBM] * 7
    return list(
        pl.pallas_call(
            functools.partial(attention_forward, lay, first, chain is not None),
            grid=(count, groups),
            in_specs=specs,
            out_specs=[pl.BlockSpec((1, rows, width), lambda i, g: (first + i, 0, 0))] * 5
            + [
                pl.BlockSpec((1, 3, keys, GROUP), lambda i, g: (first + i, 0, 0, g)),
                pl.BlockSpec((1, HEADS // groups, rows, keys), lambda i, g: (first + i, g, 0, 0)),
            ],
            out_shape=shapes,
            scratch_shapes=[
                pltpu.VMEM((lay.ranks, lay.slots, width), BF16),
                pltpu.VMEM((rows, width), F32),
                pltpu.VMEM((8, width), F32),
                pltpu.VMEM((8, keys), F32),
            ],
            input_output_aliases=aliases,
            compiler_params=params(),
            cost_estimate=cost(8e9 * count, 12e6 * count, HEADS * rows * keys * count),
        )(*args)
    )


def feed_forward(
    lay, per, fast, rank_ref, split_ref, tag_ref, hid_hbm, c0, c1, c2, c3, n2_ref, w1_ref, b1_ref, w2_ref, n2g, b2_ref, mixed_hbm, *refs
):
    out_refs = refs[: lay.ranks]
    ga_ref, db1_ref, dvec_ref, *dw = refs[lay.ranks : -13]
    stage, back, cot, gr, grt, red, gn, act, gexp, hid, mixed, sem, sem2 = refs[-13:]
    step = pl.program_id(0)
    last = pl.num_programs(0) - 1
    rows = lay.rows
    meta = rank_ref, split_ref, tag_ref
    fetch = pltpu.make_async_copy(hid_hbm, hid, sem)
    fetch2 = pltpu.make_async_copy(mixed_hbm, mixed, sem2)

    @pl.when(step == 0)
    def _():
        fetch.start()
        fetch2.start()
        total = None
        for k in range(per):
            block = slice(k * rows, (k + 1) * rows)
            for j, piece in enumerate((c0, c1, c2, c3)):
                stage[j] = piece[k]
            image = Image(lay, meta, k)
            unpack(lay, stage, image, cot)
            wide = live_column(lay, image) * cot[...]
            gr[block, :] = wide.astype(BF16)
            grt[:, block] = wide.T.astype(BF16)
            total = jnp.sum(wide, 0, keepdims=True) + (0.0 if total is None else total)
        dvec_ref[...] = jnp.zeros_like(dvec_ref)
        dvec_ref[3:4] = total
        red[...] = jnp.zeros_like(red)
        gn[...] = jnp.zeros_like(gn)

    def share_fc2(sums):
        own2, send2 = dw[-2:]
        n = sums.shape[0] // 32
        for dp in range(8):
            for y in range(2):
                at = (dp * 4 + y * 2) * n
                place = place_of(FC2_ORDER, dp, y)
                own2[place], send2[place] = keep_and_send(
                    rank_ref[0] % 2, sums[at : at + n], sums[at + n : at + 2 * n]
                )

    @pl.when(step < last)
    def _():
        total = None
        for k in range(per):
            block = slice(k * rows, (k + 1) * rows)
            expanded = dot(n2_ref[block, :], w1_ref[...]) + b1_ref[...]
            cdf = 0.5 * (1.0 + lax.erf(expanded * 0.7071067811865476))
            slope = cdf + expanded * (jnp.exp(-0.5 * expanded * expanded) * 0.3989422804014327)
            act[block, :] = (expanded * cdf).astype(BF16)
            grad_active = dot_nt(gr[block, :], w2_ref[...])
            grad_exp = (grad_active * slope).astype(BF16)
            gexp[block, :] = grad_exp
            total = jnp.sum(grad_exp.astype(F32), 0, keepdims=True) + (0.0 if total is None else total)
            red[block, :] += dot(act[block, :], w2_ref[...])
            gn[block, :] += dot_nt(gexp[block, :], w1_ref[...])
        db1_ref[...] = total
        sums1 = dot_tn(gexp[...], n2_ref[...])
        sums2 = dot(grt[...], act[...])
        if fast:
            own1, send1 = dw[:2]
            n = CHUNK // 8
            for i in range(2):
                for y in range(2):
                    at = (i * 4 + y * 2) * n
                    place = place_of(FC1_ORDER, i, y)
                    own1[place], send1[place] = keep_and_send(
                        rank_ref[0] % 2, sums1[at : at + n], sums1[at + n : at + 2 * n]
                    )
            share_fc2(sums2)
        else:
            dw[0][...] = sums1.astype(BF16)
            dw[1][...] = sums2.astype(BF16)

    @pl.when(step == last)
    def _():
        fetch.wait()
        fetch2.wait()
        for k in range(per):
            block = slice(k * rows, (k + 1) * rows)
            live = live_column(lay, Image(lay, meta, k))
            hidden = hid[k]
            red[block, :] = hidden + live * (red[block, :] + row_of(b2_ref))
            xhat, rstd = normalise(hidden)
            grad = gn[block, :]
            dvec_ref[0:1] += jnp.sum(grad * xhat, 0, keepdims=True)
            dvec_ref[1:2] += jnp.sum(grad, 0, keepdims=True)
            row = norm_backward(grad, row_of(n2g), xhat, rstd)
            attended = (live * (gr[block, :].astype(F32) + row)).astype(BF16)
            ga_ref[block, :] = attended
            dvec_ref[2:3] += jnp.sum(attended.astype(F32), 0, keepdims=True)
        for k in range(per):
            repack(lay, red, k * rows, Image(lay, meta, k), back)
            for j, out_ref in enumerate(out_refs):
                out_ref[k] = back[j]
        sums = dot_tn(ga_ref[...], mixed[...])
        if fast:
            share_fc2(sums)
        else:
            dw[1][...] = sums.astype(BF16)


def call_feed(lay, per, fast, meta, hidden, cot, n2, w1, b1, w2, n2g, b2, mixed):
    width, inner = w1.shape
    rows = per * lay.rows
    steps = inner // CHUNK

    def hold(i):
        return jnp.minimum(i, steps - 1)

    shapes = [shaped((per, lay.piece, width), BF16)] * lay.ranks + [
        shaped((rows, width), BF16),
        shaped((1, inner), F32),
        shaped((8, width), F32),
    ]
    specs = [whole((per, lay.piece, width))] * lay.ranks + [
        whole((rows, width)),
        pl.BlockSpec((1, CHUNK), lambda i: (0, hold(i))),
        whole((8, width)),
    ]
    if fast:
        def where(i):
            i = hold(i)
            at = {"x": 0, "y": 0, "z0": i % 2, "z1": i // 2}
            return tuple(at[name] for name in FC1_ORDER) + (0, 0)

        block = tuple(2 if name in ("x", "y") else 1 for name in FC1_ORDER) + (inner // 32, width)
        shapes += [shaped((2, 2, 2, 2, inner // 32, width), BF16)] * 2
        specs += [pl.BlockSpec(block, where)] * 2
        n = width // 32
        shapes += [shaped((2, 2, 2, 2, n, inner + width), BF16)] * 2
        specs += [pl.BlockSpec((2, 2, 2, 2, n, CHUNK), lambda i: (0, 0, 0, 0, 0, i))] * 2
    else:
        shapes += [shaped((inner, width), BF16), shaped((width, inner + width), BF16)]
        specs += [pl.BlockSpec((CHUNK, width), lambda i: (hold(i), 0)), pl.BlockSpec((width, CHUNK), lambda i: (0, i))]
    once = pl.Buffered(1)
    return pl.pallas_call(
        functools.partial(feed_forward, lay, per, fast),
        grid=(steps + 1,),
        in_specs=[
            SMEM,
            SMEM,
            SMEM,
            HBM,
            *[pl.BlockSpec(c.shape, lambda i: (0, 0, 0), pipeline_mode=once) for c in cot],
            pl.BlockSpec(n2.shape, lambda i: (0, 0), pipeline_mode=once),
            pl.BlockSpec((width, CHUNK), lambda i: (0, hold(i))),
            pl.BlockSpec((1, CHUNK), lambda i: (0, hold(i))),
            pl.BlockSpec((CHUNK, width), lambda i: (hold(i), 0)),
            whole(n2g.shape),
            whole(b2.shape),
            HBM,
        ],
        out_specs=specs,
        out_shape=shapes,
        scratch_shapes=[
            pltpu.VMEM((lay.ranks, lay.slots, width), BF16),
            pltpu.VMEM((lay.ranks, lay.piece, width), BF16),
            pltpu.VMEM((lay.rows, width), F32),
            pltpu.VMEM((rows, width), BF16),
            pltpu.VMEM((width, rows), BF16),
            pltpu.VMEM((rows + lay.spare, width), F32),
            pltpu.VMEM((rows, width), F32),
            pltpu.VMEM((rows, CHUNK), BF16),
            pltpu.VMEM((rows, CHUNK), BF16),
            pltpu.VMEM((per, lay.rows, width), F32),
            pltpu.VMEM((rows, width), BF16),
            pltpu.SemaphoreType.DMA,
            pltpu.SemaphoreType.DMA,
        ],
        compiler_params=params(),
        cost_estimate=cost(12 * rows * width * inner, 30e6, 2 * rows * inner),
    )(*meta, hidden, *cot, n2, w1, b1, w2, n2g, b2, mixed)


def late_sums(per, fast, rank_ref, gp_ref, normed_ref, dvec_ref, db1_ref, *refs):
    _, _, rows, width = gp_ref.shape
    dvecs = refs[:per]
    step = pl.program_id(0)
    sums = dot_tn(gp_ref[...].reshape(per * rows, width), normed_ref[...])
    if not fast:
        refs[per][...] = sums.astype(BF16)
        return
    own_refs, send_refs, held = refs[per : per + 2], refs[per + 2 : per + 4], refs[-1]
    held[pl.ds(pl.multiple_of(step * width, width), width), :] = sums

    @pl.when(step == pl.num_programs(0) - 1)
    def _():
        vec = dvecs[0][...]
        for more in dvecs[1:]:
            vec = vec + more[...]
        parts = [vec[i : i + 1] for i in range(4)]
        parts += [dvec_ref[2:3], dvec_ref[0:1], dvec_ref[1:2], dvec_ref[3:4]]
        packed = spread(parts, db1_ref[...])
        each = 3 * width // 32
        for dp in range(8):
            for y in range(2):
                d = dp * 4 + y * 2
                first = [held[e * each : e * each + LATE_CUT, :] for e in (d, d + 1)]
                second = [
                    with_vectors(held[e * each + LATE_CUT : (e + 1) * each, :], packed, e, width)
                    for e in (d, d + 1)
                ]
                for i, pair in enumerate((first, second)):
                    place = place_of(LATE_ORDERS[i], dp, y)
                    own_refs[i][place], send_refs[i][place] = keep_and_send(rank_ref[0] % 2, *pair)


def call_late_sums(fast, rank, gp, normed, dvec, db1, dvecs):
    per, _, rows, width = gp.shape
    if fast:
        heights = (LATE_CUT, 3 * width // 32 - LATE_CUT + 8)
        shapes = [shaped((2, 2, 2, 2, n, width), BF16) for n in heights] * 2
        specs = [whole(s.shape) for s in shapes]
        scratch = [pltpu.VMEM((3 * width, width), F32)]
    else:
        shapes = [shaped((3 * width, width), BF16)]
        specs = [pl.BlockSpec((width, width), lambda i: (i, 0))]
        scratch = []
    return pl.pallas_call(
        functools.partial(late_sums, per, fast),
        grid=(3,),
        in_specs=[SMEM, pl.BlockSpec((per, 1, rows, width), lambda i: (0, i, 0, 0)), whole(normed.shape)]
        + [whole(dvec.shape), whole(db1.shape)]
        + [whole(d.shape) for d in dvecs],
        out_specs=specs,
        out_shape=shapes,
        scratch_shapes=scratch,
        compiler_params=params(),
        cost_estimate=cost(6 * per * rows * width * width, 10e6),
    )(rank, gp, normed, dvec, db1, *dvecs)


def attention_backward(
    lay, k, linked, rank_ref, split_ref, tag_ref, ga_ref, qkv_ref, prob_ref, x_ref, n1g, wo_ref, wq, wk, wv, *refs
):
    gp_ref, *ig_refs, dvec_ref, gn, res, back = refs[linked:]
    rows = lay.rows
    group = pl.program_id(0)
    grad_mixed = dot_nt(ga_ref[0], wo_ref[...]).astype(BF16)
    masks = half_masks()

    @pl.when(group == 0)
    def _():
        dvec_ref[...] = jnp.zeros_like(dvec_ref)
        gn[...] = jnp.zeros_like(gn)

    for p in range(GROUP // 128):
        lanes = slice(p * 128, (p + 1) * 128)
        q = qkv_ref[0, 0, 0:rows, lanes]
        key = qkv_ref[0, 1, :, lanes]
        v = qkv_ref[0, 2, :, lanes]
        gm = grad_mixed[:, lanes]
        both = dot_nt(gm, jnp.concatenate([v * masks[0], v * masks[1]], 0))
        ds, probs = [], []
        for h in (0, 1):
            prob = prob_ref[0, 2 * p + h]
            weights = prob.astype(F32)
            gw = both[:, h * lay.keys : (h + 1) * lay.keys]
            delta = jnp.sum(weights * gw, -1, keepdims=True)
            ds.append((weights * (gw - delta)).astype(BF16))
            probs.append(prob)
        dq = dot(jnp.concatenate(ds, 1), jnp.concatenate([key * masks[0], key * masks[1]], 0))
        dk = dot_tn(jnp.concatenate(ds, 0), jnp.concatenate([q * masks[0], q * masks[1]], 0))
        dv = dot_tn(jnp.concatenate(probs, 0), jnp.concatenate([gm * masks[0], gm * masks[1]], 0))
        dq, dk, dv = (dq * 0.125).astype(BF16), dk[:rows].astype(BF16), dv[:rows].astype(BF16)
        gp_ref[0, 0, :, lanes] = dq
        gp_ref[0, 1, :, lanes] = dk
        gp_ref[0, 2, :, lanes] = dv
        at = pl.multiple_of(group * GROUP + p * 128, 128)
        dvec_ref[2:3, pl.ds(at, 128)] = jnp.sum(dq.astype(F32), 0, keepdims=True)
        dvec_ref[3:4, pl.ds(at, 128)] = jnp.sum(dv.astype(F32), 0, keepdims=True)
    gn[...] += sum(dot_nt(gp_ref[0, j], w[...]) for j, w in enumerate((wq, wk, wv)))

    @pl.when(group == pl.num_programs(0) - 1)
    def _():
        grad = gn[...]
        xhat, rstd = normalise(x_ref[0].astype(F32))
        dvec_ref[0:1] = jnp.sum(grad * xhat, 0, keepdims=True)
        dvec_ref[1:2] = jnp.sum(grad, 0, keepdims=True)
        res[0:rows] = ga_ref[0].astype(F32) + norm_backward(grad, row_of(n1g), xhat, rstd)
        repack(lay, res, 0, Image(lay, (rank_ref, split_ref, tag_ref), k), back)
        for j, ig_ref in enumerate(ig_refs):
            ig_ref[0] = back[j]


def call_backward(lay, k, per, meta, ga, qkv, prob, x, n1g, out_weight, qkv_weight, chain):
    rows, keys = lay.rows, lay.keys
    width = out_weight.shape[0]
    groups = width // GROUP
    alone = k == per - 1
    one = pl.BlockSpec((1, rows, width), lambda g: (k, 0, 0))
    args = [*meta, ga, qkv, prob, x, n1g, out_weight, qkv_weight, qkv_weight, qkv_weight]
    specs = [
        SMEM,
        SMEM,
        SMEM,
        one,
        pl.BlockSpec((1, 3, keys, GROUP), lambda g: (k, 0, 0, g)),
        pl.BlockSpec((1, HEADS // groups, rows, keys), lambda g: (k, g, 0, 0)),
        one,
        whole(n1g.shape),
        pl.BlockSpec((GROUP, width), lambda g: (g, 0)),
    ] + [pl.BlockSpec((width, GROUP), functools.partial(lambda j, g: (0, j * groups + g), j)) for j in range(3)]
    aliases = {}
    if chain is not None:
        count = 1 if alone else len(chain)
        aliases = {len(args) + i: i for i in range(count)}
        args += chain[:count]
        specs += [HBM] * count
    return pl.pallas_call(
        functools.partial(attention_backward, lay, k, len(args) - 12),
        grid=(groups,),
        in_specs=specs,
        out_specs=[
            pl.BlockSpec((1, 3, rows, GROUP), lambda g: (k, 0, 0, g)),
            *[pl.BlockSpec((1, lay.piece, width), lambda g: (0 if alone else k, 0, 0))] * lay.ranks,
            whole((8, width)),
        ],
        out_shape=[
            shaped((per, 3, rows, width), BF16),
            *[shaped((1 if alone else per - 1, lay.piece, width), BF16)] * lay.ranks,
            shaped((8, width), F32),
        ],
        scratch_shapes=[
            pltpu.VMEM((rows, width), F32),
            pltpu.VMEM((rows + lay.spare, width), F32),
            pltpu.VMEM((lay.ranks, lay.piece, width), BF16),
        ],
        input_output_aliases=aliases,
        compiler_params=params(),
        cost_estimate=cost(10e9, 10e6),
    )(*args)


def assemble(lay, rank_ref, split_ref, tag_ref, *refs):
    *got, passed_ref, out_ref = refs
    images, slots, width = out_ref.shape
    row = lax.broadcasted_iota(jnp.int32, (slots, width), 0)
    rank = rank_ref[0]
    first = 0
    for b in range(0, len(got), lay.ranks):
        for j, piece in enumerate(got[b : b + lay.ranks]):
            for k in range(piece.shape[0]):
                number = (rank ^ j) * lay.per + first + k
                image = jnp.minimum(number, images - 1)
                live = jnp.where(tag_ref[image] < lay.groups, split_ref[image, rank] * GRID, 0)

                @pl.when(number < images)
                def _():
                    worked = piece[k][:slots].astype(F32)
                    kept = passed_ref[image].astype(F32)
                    out_ref[image] = jnp.where(row < live, worked, kept).astype(BF16)

        first += got[b].shape[0]


def call_assemble(lay, meta, got, passed):
    args = [*meta, *got, passed]
    return pl.pallas_call(
        functools.partial(assemble, lay),
        in_specs=[SMEM] * 3 + [VMEM] * len(args[3:]),
        out_specs=VMEM,
        out_shape=shaped(passed.shape, BF16),
        compiler_params=params(SMALL_LIMIT),
        cost_estimate=cost(0, 5e6),
    )(*args)


class Part:
    def __init__(self, own, send, order, at=None):
        self.own, self.send, self.order = own, send, ["core", *order]
        self.got = self.sent = None
        self.at = at


def exchange(parts):
    for p in parts:
        if p.send is None:
            continue
        axis, weight = BITS[p.order[0]]
        size = lax.axis_size(axis)
        p.got = lax.ppermute(p.send, axis, [(i, i ^ weight) for i in range(size)])
        p.sent, p.send = p.send, None


def add_and_split(counts, mine_ref, *refs):
    n = len(counts)
    for i in range(n):
        own, got, keep, send = refs[2 * i], refs[2 * i + 1], refs[2 * n + 2 * i], refs[2 * n + 2 * i + 1]
        mine = mine_ref[i]
        keep[...] = (own[mine].astype(F32) + got[mine].astype(F32)).astype(BF16)
        send[...] = (own[1 - mine].astype(F32) + got[1 - mine].astype(F32)).astype(BF16)


def combine(parts, before=()):
    parts = [p for p in parts if p.got is not None]
    last = [p for p in parts if len(p.order) == 1]
    for p in last:
        p.own = p.own.astype(F32) + p.got.astype(F32)
        p.got = p.send = None
        p.order = []
    parts = [p for p in parts if p.order]
    if not parts:
        return ()
    tied, _ = lax.optimization_barrier(([(p.own, p.got) for p in parts], before))
    for p, (p.own, p.got) in zip(parts, tied):
        pass
    views = []
    for p in parts:
        shape = p.own.shape
        flat = (2, 2 ** (len(p.order) - 2), *shape[-2:])
        if p.at is not None:
            flat = (shape[0], *flat)
        views.append((p.own.reshape(flat), p.got.reshape(flat)))
    size = sum(4 * v[0].size for v in views)
    steps = min(4 if size > 9e6 else 1, *(v[0].shape[-3] for v in views))
    ins, outs, shapes, args, mine = [], [], [], [], []
    for p, (own, got) in zip(parts, views):
        many, n, width = own.shape[-3:]
        block = (2, many // steps, n, width)
        if steps == 1:
            ins += [VMEM] * 2
            outs += [VMEM] * 2
            shapes += [shaped((many, n, width), BF16)] * 2
        elif p.at is None:
            ins += [pl.BlockSpec(block, lambda i: (0, i, 0, 0))] * 2
        else:
            ins += [pl.BlockSpec((None, *block), functools.partial(lambda a, i: (a, 0, i, 0, 0), p.at))] * 2
        if steps > 1:
            outs += [pl.BlockSpec(block[1:], lambda i: (i, 0, 0))] * 2
            shapes += [shaped((many, n, width), BF16)] * 2
        args += [own, got]
        axis, weight = BITS[p.order[1]]
        mine.append((lax.axis_index(axis) // weight) % 2)
    moved = sum(3 * a.size for a in args)
    res = pl.pallas_call(
        functools.partial(add_and_split, [None] * len(parts)),
        **({"grid": (steps,)} if steps > 1 else {}),
        in_specs=[SMEM] + ins,
        out_specs=outs,
        out_shape=shapes,
        compiler_params=params() if steps > 1 else params(SMALL_LIMIT),
        cost_estimate=cost(0, moved),
    )(jnp.stack(mine), *args)
    for i, p in enumerate(parts):
        shape = (*[2] * (len(p.order) - 2), *p.own.shape[-2:])
        p.at = None
        p.own, p.send = res[2 * i].reshape(shape), res[2 * i + 1].reshape(shape)
        p.got = None
        p.order.pop(0)
    return res[0]


def add_and_fan(heights, z_ref, *refs):
    ins, outs = refs[: 2 * len(heights)], refs[2 * len(heights) :]
    at = 0
    for i, n in enumerate(heights):
        own, got = ins[2 * i], ins[2 * i + 1]
        for j, out in enumerate(outs):
            place = (z_ref[0] % 2) ^ (j % 2), (z_ref[0] // 2) ^ (j // 2)
            total = own[place].astype(F32) + got[place].astype(F32)
            out[at : at + n, :] = total.astype(out.dtype)
        at += n


def fan(parts, before):
    tied, _ = lax.optimization_barrier(([(p.own, p.got) for p in parts], before))
    args = [a for pair in tied for a in pair]
    heights = [p.own.shape[2] for p in parts]
    width = args[0].shape[-1]
    z = lax.axis_index("dp") // 2
    shape = (sum(heights), width)
    own, *sends = pl.pallas_call(
        functools.partial(add_and_fan, heights),
        in_specs=[SMEM] + [VMEM] * len(args),
        out_specs=[VMEM] * 4,
        out_shape=[shaped(shape, F32)] + [shaped(shape, BF16)] * 3,
        compiler_params=params(SMALL_LIMIT),
        cost_estimate=cost(0, 1e6),
    )(z[None], *args)
    size = lax.axis_size("dp")
    got = [lax.ppermute(v, "dp", [(i, i ^ (2 * j)) for i in range(size)]) for j, v in zip((1, 2, 3), sends)]
    return own, sends, got


def wait(values, parts):
    live = [p for p in parts if p.got is not None]
    values, gots = lax.optimization_barrier((values, [p.got for p in live]))
    for p, g in zip(live, gots):
        p.got = g
    return values


def after(values, parts):
    return lax.optimization_barrier((values, [p.sent for p in parts if p.sent is not None]))[0]


def small_sum(value, n_dp, n_seq):
    for axis, size in (("seq", n_seq), ("dp", n_dp)):
        dim = 1 if axis == "seq" else 0
        weight = 1
        place = lax.axis_index(axis)
        while weight < size:
            shape = value.shape
            cut = value.reshape(*shape[:dim], shape[dim] // 2, 2, *shape[dim + 1 :])
            mine = (place // weight) % 2
            other = lax.dynamic_index_in_dim(cut, 1 - mine, dim + 1, keepdims=False)
            own = lax.dynamic_index_in_dim(cut, mine, dim + 1, keepdims=False)
            value = own + lax.ppermute(other, axis, [(i, i ^ weight) for i in range(size)])
            weight *= 2
    return value.reshape(-1)


def per_device(
    tokens,
    key_mask,
    row_split,
    group_tags,
    norm1_gain,
    norm1_shift,
    qkv_weight,
    query_bias,
    value_bias,
    out_weight,
    out_bias,
    norm2_gain,
    norm2_shift,
    fc1_weight,
    fc1_bias,
    fc2_weight,
    fc2_bias,
    out_cotangent,
):
    images, slots, width = tokens.shape
    n_seq = lax.axis_size("seq")
    n_dp = lax.axis_size("dp")
    devices = n_dp * n_seq
    rank = lax.axis_index("seq")
    lay = Rows(n_seq, slots, images, n_dp)
    per, rows = lay.per, lay.rows
    meta = rank[None], row_split, group_tags
    all_rows = per * rows
    fast = (n_dp, n_seq) == (8, 4)

    def swap(value, j):
        return lax.ppermute(value, "seq", [(i, i ^ j) for i in range(n_seq)])

    def rows_of(array, owner, k):
        return lax.dynamic_slice_in_dim(array, jnp.minimum(owner * per + k, images - 1), 1, 0)

    def cut_for(array, which):
        got = []
        for j in range(n_seq):
            mine = [rows_of(array, rank ^ j, k) for k in which]
            got.append(mine[0] if len(mine) == 1 else jnp.concatenate(mine, 0))
        return got

    def bring(mine):
        return [mine[0]] + [swap(mine[j], j) for j in range(1, n_seq)]

    vecs = (norm1_gain, norm1_shift, out_bias, norm2_gain, norm2_shift, query_bias, value_bias)

    first, rest = cut_for(tokens, [0]), cut_for(tokens, list(range(1, per)))
    cot = cut_for(out_cotangent, list(range(per)))
    first = bring(first)
    first, rest = lax.optimization_barrier((first, rest))
    chain = call_forward(lay, 0, 1, meta, first, key_mask, vecs, qkv_weight, out_weight, None)
    rest = bring(rest)
    chain, rest, cot = lax.optimization_barrier((chain, rest, cot))
    chain = call_forward(lay, 1, per - 1, meta, rest, key_mask, vecs, qkv_weight, out_weight, chain)
    hidden, x_all, normed_all, mixed_all, n2, qkv, prob = chain
    n2 = n2.reshape(all_rows, width)

    cot = bring(cot)
    res = call_feed(
        lay,
        per,
        fast,
        meta,
        hidden,
        cot,
        n2,
        fc1_weight,
        fc1_bias.astype(F32)[None],
        fc2_weight,
        norm2_gain,
        fc2_bias,
        mixed_all.reshape(all_rows, width),
    )
    out_pieces, (ga, db1, dvec2, *dw) = list(res[:n_seq]), res[n_seq:]

    fc = late = []
    if fast:
        fc = [Part(*dw[:2], FC1_ORDER), Part(*dw[2:], FC2_ORDER)]
    out_got = [swap(out_pieces[j], j) for j in range(2, n_seq)]
    exchange(fc)
    ga = ga.reshape(per, rows, width)

    chain = None
    dvecs, ig, ig_got = [], [], []
    for k in range(per):
        *chain, dvec = call_backward(
            lay, k, per, meta, ga, qkv, prob, x_all, norm1_gain, out_weight, qkv_weight, chain
        )
        dvecs.append(dvec)
        if k == 0:
            chain, out_got[0] = lax.optimization_barrier((chain, out_got[0]))
        if k == 1:
            chain, out_got, out_pieces = lax.optimization_barrier((chain, out_got, out_pieces))
            out_got = [out_pieces[0], swap(out_pieces[1], 1), *out_got]
        if k == 2:
            chain, ig_got[0] = lax.optimization_barrier((chain, ig_got[0]))
        if k >= per - 2:
            ig.append(chain[1:3])
            ig_got.append([swap(chain[1 + j], j) for j in range(2, n_seq)])
        if k != 1:
            chain = wait(chain, fc)
            combine(fc)
            exchange(fc)
            ga, chain = after((ga, chain), fc)
    gp = chain[0]
    dwl = call_late_sums(fast, meta[0], gp, normed_all.reshape(all_rows, width), dvec2, db1, dvecs)
    if fast:
        dwl, ig_got[1] = wait((dwl, ig_got[1]), fc)
        late = [Part(dwl[i], dwl[2 + i], order) for i, order in enumerate(LATE_ORDERS)]
        exchange(late)
        token = combine(fc, dwl)
        exchange(fc)
        token = combine(late, token)
        exchange(late)
        out_got, ig, _ = lax.optimization_barrier((out_got, ig, token))
    output = call_assemble(lay, meta, out_got, tokens)
    if fast:
        token = combine(late, output)
        exchange(late)
        token = combine(fc, token)
        exchange(fc)
        ig = after(ig, late)
    ig_got = [g for near, far in zip(ig, ig_got) for g in (near[0], swap(near[1], 1), *far)]
    if fast:
        own, sends, got = fan(late, token)
        ig_got, _ = lax.optimization_barrier((ig_got, sends))
    input_grad = call_assemble(lay, meta, ig_got, out_cotangent)
    if fast:
        input_grad, fc[0].got, fc[1].got = lax.optimization_barrier((input_grad, fc[0].got, fc[1].got))
        combine(fc)
        inner = fc1_weight.shape[1]
        done = fc[0].own.T, fc[1].own[:, :inner].T, fc[1].own[:, inner:].T
        done, got = lax.optimization_barrier((done, got))
        late_sum = own + sum(g.astype(F32) for g in got)

    part = width // devices
    inner = fc1_weight.shape[1]
    if fast:
        qkv_sum, small = late_sum[: 3 * part], late_sum[3 * part]
        small_late, small_early = small[: 4 * part], small[4 * part :]
    else:
        *done, qkv_sum = [
            lax.psum_scatter(v.astype(F32), ("dp", "seq"), scatter_dimension=0, tiled=True)
            for v in (dw[0], dw[1][:, :inner], dw[1][:, inner:], dwl[0])
        ]
        done = [v.T for v in done]
        dvec1 = sum(dvecs)

        def by_device(v):
            return v.reshape(n_dp, n_seq, v.shape[0] // devices)

        early = (dvec2[2], dvec2[0], dvec2[1], dvec2[3], db1[0])
        small_early = small_sum(jnp.concatenate([by_device(v) for v in early], -1), n_dp, n_seq)
        small_late = small_sum(jnp.concatenate([by_device(dvec1[i]) for i in range(4)], -1), n_dp, n_seq)
    vec = [small_late[i * part : (i + 1) * part] for i in range(4)]
    vec += [small_early[i * part : (i + 1) * part] for i in range(4)]
    vec.append(small_early[4 * part : 4 * part + fc1_bias.shape[0] // devices])
    return (
        output,
        input_grad,
        vec[0],
        vec[1],
        qkv_sum.T,
        vec[2],
        vec[3],
        done[2],
        vec[4],
        vec[5],
        vec[6],
        done[0],
        vec[8],
        done[1],
        vec[7],
    )


def solution(mesh):
    rows = P("dp", "seq", None)
    split = P(("dp", "seq"))
    columns = P(None, ("dp", "seq"))
    return jax.shard_map(
        per_device,
        mesh=mesh,
        in_specs=(rows, P("dp", None), P("dp", None), P("dp")) + (P(),) * 13 + (rows,),
        out_specs=(
            rows,
            rows,
            split,
            split,
            columns,
            split,
            split,
            columns,
            split,
            split,
            split,
            columns,
            split,
            columns,
            split,
        ),
        check_vma=False,
    )
```

```python
import functools

import jax
import jax.numpy as jnp
from jax import lax
from jax.experimental import pallas as pl
from jax.experimental.pallas import tpu as pltpu
from jax.sharding import PartitionSpec as P

HEADS = 12
GRID = 18
EPS = 1e-06
NEG = -1e30
F32 = jnp.float32
BF16 = jnp.bfloat16
VMEM_LIMIT = 60 * 1024 * 1024
CHUNK = 768
GROUP = 256
LANES = 384

BITS = {"core": ("seq", 1), "y": ("seq", 2), "x": ("dp", 1), "z0": ("dp", 2), "z1": ("dp", 4)}
FC1_ORDER = ("x", "z0", "z1", "y")
FC2_ORDER = ("z0", "x", "y", "z1")
LATE_ORDERS = (("x", "y", "z0", "z1"), ("y", "x", "z0", "z1"))
LATE_CUT = 40
SMEM = pl.BlockSpec(memory_space=pltpu.SMEM)
VMEM = pl.BlockSpec(memory_space=pltpu.VMEM)
SMALL_LIMIT = 8 * 1024 * 1024
HBM = pl.BlockSpec(memory_space=pl.ANY)


def round_up(n, to):
    return -(-n // to) * to


class Rows:
    def __init__(self, ranks, slots, images, groups):
        self.images, self.groups = images, groups
        self.per = -(-images // ranks)
        base, extra = GRID // ranks, GRID % ranks
        self.lens = [min(slots, (base + 1) * GRID)] * extra + [base * GRID] * (ranks - extra)
        self.extra = extra
        self.ranks = ranks
        self.slots = slots
        self.offs = []
        at = 0
        for n in self.lens:
            self.offs.append(at)
            at += round_up(n, 8)
        self.rows = round_up(at, 16)
        self.keys = round_up(self.rows, 128)
        self.piece = round_up(slots, 16)
        end = max(o + round_up(n, 16) for o, n in zip(self.offs, self.lens))
        self.spare = max(round_up(end, 8) - self.rows, 0)

    def is_row(self, index):
        hit = None
        for off, n in zip(self.offs, self.lens):
            one = (index >= off) & (index < off + n)
            hit = one if hit is None else hit | one
        return hit


def dot(a, b):
    return lax.dot_general(a, b, (((1,), (0,)), ((), ())), preferred_element_type=F32)


def dot_nt(a, b):
    return lax.dot_general(a, b, (((1,), (1,)), ((), ())), preferred_element_type=F32)


def dot_tn(a, b):
    return lax.dot_general(a, b, (((0,), (0,)), ((), ())), preferred_element_type=F32)


def params(limit=VMEM_LIMIT):
    return pltpu.CompilerParams(vmem_limit_bytes=limit)


def cost(flops, moved, exps=0):
    return pl.CostEstimate(flops=int(flops) // 16, bytes_accessed=int(moved) // 16, transcendentals=int(exps) // 16)


def whole(shape):
    return pl.BlockSpec(shape, lambda *i: (0,) * len(shape))


def shaped(shape, dtype):
    return jax.ShapeDtypeStruct(shape, dtype)


class Image:
    def __init__(self, lay, meta, k):
        rank_ref, split_ref, tag_ref = meta
        rank = rank_ref[0]
        number = rank * lay.per + k
        self.index = jnp.minimum(number, lay.images - 1)
        base = GRID // lay.ranks
        longs, shorts = jnp.int32(0), jnp.int32(lay.extra)
        self.sources = [jnp.int32(0)] * lay.ranks
        for r in range(lay.ranks):
            is_long = split_ref[self.index, r] > base
            place = jnp.where(is_long, longs, shorts)
            longs = longs + jnp.where(is_long, 1, 0)
            shorts = shorts + jnp.where(is_long, 0, 1)
            self.sources = [jnp.where(place == i, r, s) for i, s in enumerate(self.sources)]
        self.pieces = [s ^ rank for s in self.sources]
        self.counts = jnp.where((tag_ref[self.index] < lay.groups) & (number < lay.images), 1, 0)


def unpack(lay, stage, image, to_ref):
    width = to_ref.shape[1]
    for i, (off, n) in enumerate(zip(lay.offs, lay.lens)):
        full = round_up(n, 8)
        if full > n:
            to_ref[off + full - 8 : off + full, :] = jnp.zeros((8, width), F32)
        piece = stage[image.pieces[i]].astype(F32)
        to_ref[off : off + n, :] = piece[:n]
    last = lay.offs[-1] + round_up(lay.lens[-1], 8)
    if lay.rows > last:
        to_ref[last : lay.rows, :] = jnp.zeros((lay.rows - last, width), F32)


def repack(lay, from_ref, start, image, stage):
    for i, (off, n) in enumerate(zip(lay.offs, lay.lens)):
        full = round_up(n, 16)
        stage[image.pieces[i], 0:full, :] = from_ref[start + off : start + off + full, :].astype(BF16)


def mask_of(lay, image, key_ref):
    slots = key_ref.shape[1]
    row = jnp.broadcast_to(key_ref[pl.ds(image.index, 1), :], (8, slots)).astype(F32)
    lane = lax.broadcasted_iota(jnp.int32, (slots, lay.keys), 1)
    want = jnp.full((slots, lay.keys), -1, jnp.int32)
    for i, (off, n) in enumerate(zip(lay.offs, lay.lens)):
        want = jnp.where((lane >= off) & (lane < off + n), lane + (image.sources[i] * lay.slots - off), want)
    pick = (lax.broadcasted_iota(jnp.int32, (slots, lay.keys), 0) == want).astype(F32).astype(BF16)
    valid = jnp.where(row > 0, 1.0, 0.0).astype(BF16)
    return jnp.where(dot(valid, pick)[0:1] > 0.5, 0.0, NEG)


def row_of(ref):
    return ref[...].astype(F32).reshape(1, -1)


def live_column(lay, image):
    index = lax.broadcasted_iota(jnp.int32, (lay.rows, 1), 0)
    return jnp.where(lay.is_row(index), image.counts, 0).astype(F32)


def normalise(x):
    mean = jnp.mean(x, -1, keepdims=True)
    centered = x - mean
    rstd = lax.rsqrt(jnp.mean(centered * centered, -1, keepdims=True) + EPS)
    return centered * rstd, rstd


def norm_backward(grad, gain, xhat, rstd):
    scaled = grad * gain
    row = scaled - jnp.mean(scaled, -1, keepdims=True)
    return rstd * (row - xhat * jnp.mean(scaled * xhat, -1, keepdims=True))


def half_masks():
    lane = lax.broadcasted_iota(jnp.int32, (1, 128), 1)
    return [(lane < 64).astype(BF16), (lane >= 64).astype(BF16)]


def keep_and_send(core, even, odd):
    mine = core == 0
    return jnp.where(mine, even, odd).astype(BF16), jnp.where(mine, odd, even).astype(BF16)


def parts_of(rows, each):
    n = rows.shape[1]
    place = lax.broadcasted_iota(jnp.int32, rows.shape, 0) % (n // each) * each
    lane = lax.broadcasted_iota(jnp.int32, rows.shape, 1)
    return jnp.where((lane >= place) & (lane < place + each), rows, 0.0).astype(BF16)


def picker(n, each):
    source = lax.broadcasted_iota(jnp.int32, (n, 128), 0)
    part = ((source.astype(F32) + 0.5) * (1.0 / each)).astype(jnp.int32)
    target = lax.broadcasted_iota(jnp.int32, (n, 128), 1)
    return (source - part * each == target).astype(F32).astype(BF16)


def spread(vectors, long):
    n, m = vectors[0].shape[1], long.shape[1]
    each, long_each = n // 32, m // 32
    rows = [parts_of(jnp.broadcast_to(v, (32, n)), each) for v in vectors]
    found = dot(jnp.concatenate(rows, 0), picker(n, each))
    many = m // n
    group = lax.broadcasted_iota(jnp.int32, (32, n), 0) // (32 // many)
    chosen = sum(jnp.where(group == i, long[:, i * n : (i + 1) * n], 0.0) for i in range(many))
    last = dot(parts_of(chosen, long_each), picker(n, long_each))
    blank = jnp.zeros((32, LANES - 128), F32)
    total = pltpu.roll(jnp.concatenate([last, blank], 1), each * len(vectors), 1)
    for i in range(len(vectors)):
        one = jnp.concatenate([found[i * 32 : (i + 1) * 32], blank], 1)
        total = total + (pltpu.roll(one, each * i, 1) if i else one)
    return total


def with_vectors(rows, packed, d, width):
    lanes = packed.shape[1]
    vec = jnp.broadcast_to(packed[d : d + 1, :], (8, lanes))
    return jnp.concatenate([rows, jnp.concatenate([vec, jnp.zeros((8, width - lanes), F32)], 1)], 0)


def place_of(order, dp, y):
    bits = {"x": dp % 2, "z0": dp // 2 % 2, "z1": dp // 4, "y": y}
    return tuple(bits[name] for name in order)


def attention_forward(
    lay, first, linked, rank_ref, split_ref, tag_ref, p0, p1, p2, p3, key_ref, n1g, n1s, ob, n2g, n2s, qb, vb, wq, wk, wv, wo, *refs
):
    outs = refs[7:] if linked else refs
    hid_ref, x_ref, normed_ref, mixed_ref, n2_ref, qkv_ref, prob_ref, stage, xs, bias, mask = outs
    rows, keys = lay.rows, lay.keys
    group = pl.program_id(1)
    image = Image(lay, (rank_ref, split_ref, tag_ref), first + pl.program_id(0))

    @pl.when(group == 0)
    def _():
        for j, piece in enumerate((p0, p1, p2, p3)):
            stage[j] = piece[0]
        unpack(lay, stage, image, xs)
        mask[...] = jnp.broadcast_to(mask_of(lay, image, key_ref), mask.shape)
        bias[0:1, :] = row_of(qb)
        bias[1:2, :] = jnp.zeros((1, bias.shape[1]), F32)
        bias[2:3, :] = row_of(vb)
        x = xs[...]
        x_ref[0] = x.astype(BF16)
        xhat, _ = normalise(x)
        normed_ref[0] = (xhat * row_of(n1g) + row_of(n1s)).astype(BF16)

    normed = normed_ref[0]
    qkv = []
    for j, weight in enumerate((wq, wk, wv)):
        part = dot(normed, weight[...]) + bias[j : j + 1, pl.ds(pl.multiple_of(group * GROUP, GROUP), GROUP)]
        if j == 0:
            part = part * 0.125
        part = part.astype(BF16)
        if j and keys > rows:
            part = jnp.concatenate([part, jnp.zeros((keys - rows, GROUP), BF16)], 0)
        qkv_ref[0, j, 0 : part.shape[0], :] = part
    if keys > rows:
        qkv_ref[0, 0, rows:keys, :] = jnp.zeros((keys - rows, GROUP), BF16)
    masks = half_masks()
    for p in range(GROUP // 128):
        lanes = slice(p * 128, (p + 1) * 128)
        q = qkv_ref[0, 0, 0:rows, lanes]
        k = qkv_ref[0, 1, :, lanes]
        v = qkv_ref[0, 2, :, lanes]
        both = dot_nt(q, jnp.concatenate([k * masks[0], k * masks[1]], 0))
        probs = []
        for h in (0, 1):
            s = both[:, h * keys : (h + 1) * keys] + mask[0:1, :]
            e = jnp.exp(s - jnp.max(s, -1, keepdims=True))
            prob = (e * (1.0 / jnp.sum(e, -1, keepdims=True))).astype(BF16)
            prob_ref[0, 2 * p + h] = prob
            probs.append(prob)
        total = dot(jnp.concatenate(probs, 1), jnp.concatenate([v * masks[0], v * masks[1]], 0))
        at = pl.multiple_of(group * GROUP + p * 128, 128)
        mixed_ref[0, :, pl.ds(at, 128)] = total.astype(BF16)

    @pl.when(group == pl.num_programs(1) - 1)
    def _():
        attended = dot(mixed_ref[0], wo[...]) + row_of(ob)
        hidden = xs[...] + live_column(lay, image) * attended
        hid_ref[0] = hidden
        xhat, _ = normalise(hidden)
        n2_ref[0] = (xhat * row_of(n2g) + row_of(n2s)).astype(BF16)


def call_forward(lay, first, count, meta, pieces, key_mask, vecs, qkv_weight, out_weight, chain):
    per, rows, keys = lay.per, lay.rows, lay.keys
    width = out_weight.shape[0]
    groups = width // GROUP
    shapes = [
        shaped((per, rows, width), F32),
        shaped((per, rows, width), BF16),
        shaped((per, rows, width), BF16),
        shaped((per, rows, width), BF16),
        shaped((per, rows, width), BF16),
        shaped((per, 3, keys, width), BF16),
        shaped((per, HEADS, rows, keys), BF16),
    ]
    args = [*meta, *pieces, key_mask, *vecs, qkv_weight, qkv_weight, qkv_weight, out_weight]
    specs = (
        [SMEM] * 3
        + [pl.BlockSpec((1, lay.slots, width), lambda i, g: (i, 0, 0))] * len(pieces)
        + [whole(v.shape) for v in (key_mask, *vecs)]
        + [pl.BlockSpec((width, GROUP), functools.partial(lambda j, i, g: (0, j * groups + g), j)) for j in range(3)]
        + [whole(out_weight.shape)]
    )
    aliases = {}
    if chain is not None:
        aliases = {len(args) + i: i for i in range(7)}
        args += chain
        specs += [HBM] * 7
    return list(
        pl.pallas_call(
            functools.partial(attention_forward, lay, first, chain is not None),
            grid=(count, groups),
            in_specs=specs,
            out_specs=[pl.BlockSpec((1, rows, width), lambda i, g: (first + i, 0, 0))] * 5
            + [
                pl.BlockSpec((1, 3, keys, GROUP), lambda i, g: (first + i, 0, 0, g)),
                pl.BlockSpec((1, HEADS // groups, rows, keys), lambda i, g: (first + i, g, 0, 0)),
            ],
            out_shape=shapes,
            scratch_shapes=[
                pltpu.VMEM((lay.ranks, lay.slots, width), BF16),
                pltpu.VMEM((rows, width), F32),
                pltpu.VMEM((8, width), F32),
                pltpu.VMEM((8, keys), F32),
            ],
            input_output_aliases=aliases,
            compiler_params=params(),
            cost_estimate=cost(8e9 * count, 12e6 * count, HEADS * rows * keys * count),
        )(*args)
    )


def feed_forward(
    lay, per, fast, rank_ref, split_ref, tag_ref, hid_hbm, c0, c1, c2, c3, n2_ref, w1_ref, b1_ref, w2_ref, n2g, b2_ref, mixed_hbm, *refs
):
    out_refs = refs[: lay.ranks]
    ga_ref, db1_ref, dvec_ref, *dw = refs[lay.ranks : -13]
    stage, back, cot, gr, grt, red, gn, act, gexp, hid, mixed, sem, sem2 = refs[-13:]
    step = pl.program_id(0)
    last = pl.num_programs(0) - 1
    rows = lay.rows
    meta = rank_ref, split_ref, tag_ref
    fetch = pltpu.make_async_copy(hid_hbm, hid, sem)
    fetch2 = pltpu.make_async_copy(mixed_hbm, mixed, sem2)

    @pl.when(step == 0)
    def _():
        fetch.start()
        fetch2.start()
        total = None
        for k in range(per):
            block = slice(k * rows, (k + 1) * rows)
            for j, piece in enumerate((c0, c1, c2, c3)):
                stage[j] = piece[k]
            image = Image(lay, meta, k)
            unpack(lay, stage, image, cot)
            wide = live_column(lay, image) * cot[...]
            gr[block, :] = wide.astype(BF16)
            grt[:, block] = wide.T.astype(BF16)
            total = jnp.sum(wide, 0, keepdims=True) + (0.0 if total is None else total)
        dvec_ref[...] = jnp.zeros_like(dvec_ref)
        dvec_ref[3:4] = total
        red[...] = jnp.zeros_like(red)
        gn[...] = jnp.zeros_like(gn)

    def share_fc2(sums):
        own2, send2 = dw[-2:]
        n = sums.shape[0] // 32
        for dp in range(8):
            for y in range(2):
                at = (dp * 4 + y * 2) * n
                place = place_of(FC2_ORDER, dp, y)
                own2[place], send2[place] = keep_and_send(
                    rank_ref[0] % 2, sums[at : at + n], sums[at + n : at + 2 * n]
                )

    @pl.when(step < last)
    def _():
        total = None
        for k in range(per):
            block = slice(k * rows, (k + 1) * rows)
            expanded = dot(n2_ref[block, :], w1_ref[...]) + b1_ref[...]
            cdf = 0.5 * (1.0 + lax.erf(expanded * 0.7071067811865476))
            slope = cdf + expanded * (jnp.exp(-0.5 * expanded * expanded) * 0.3989422804014327)
            act[block, :] = (expanded * cdf).astype(BF16)
            grad_active = dot_nt(gr[block, :], w2_ref[...])
            grad_exp = (grad_active * slope).astype(BF16)
            gexp[block, :] = grad_exp
            total = jnp.sum(grad_exp.astype(F32), 0, keepdims=True) + (0.0 if total is None else total)
            red[block, :] += dot(act[block, :], w2_ref[...])
            gn[block, :] += dot_nt(gexp[block, :], w1_ref[...])
        db1_ref[...] = total
        sums1 = dot_tn(gexp[...], n2_ref[...])
        sums2 = dot(grt[...], act[...])
        if fast:
            own1, send1 = dw[:2]
            n = CHUNK // 8
            for i in range(2):
                for y in range(2):
                    at = (i * 4 + y * 2) * n
                    place = place_of(FC1_ORDER, i, y)
                    own1[place], send1[place] = keep_and_send(
                        rank_ref[0] % 2, sums1[at : at + n], sums1[at + n : at + 2 * n]
                    )
            share_fc2(sums2)
        else:
            dw[0][...] = sums1.astype(BF16)
            dw[1][...] = sums2.astype(BF16)

    @pl.when(step == last)
    def _():
        fetch.wait()
        fetch2.wait()
        for k in range(per):
            block = slice(k * rows, (k + 1) * rows)
            live = live_column(lay, Image(lay, meta, k))
            hidden = hid[k]
            red[block, :] = hidden + live * (red[block, :] + row_of(b2_ref))
            xhat, rstd = normalise(hidden)
            grad = gn[block, :]
            dvec_ref[0:1] += jnp.sum(grad * xhat, 0, keepdims=True)
            dvec_ref[1:2] += jnp.sum(grad, 0, keepdims=True)
            row = norm_backward(grad, row_of(n2g), xhat, rstd)
            attended = (live * (gr[block, :].astype(F32) + row)).astype(BF16)
            ga_ref[block, :] = attended
            dvec_ref[2:3] += jnp.sum(attended.astype(F32), 0, keepdims=True)
        for k in range(per):
            repack(lay, red, k * rows, Image(lay, meta, k), back)
            for j, out_ref in enumerate(out_refs):
                out_ref[k] = back[j]
        sums = dot_tn(ga_ref[...], mixed[...])
        if fast:
            share_fc2(sums)
        else:
            dw[1][...] = sums.astype(BF16)


def call_feed(lay, per, fast, meta, hidden, cot, n2, w1, b1, w2, n2g, b2, mixed):
    width, inner = w1.shape
    rows = per * lay.rows
    steps = inner // CHUNK

    def hold(i):
        return jnp.minimum(i, steps - 1)

    shapes = [shaped((per, lay.piece, width), BF16)] * lay.ranks + [
        shaped((rows, width), BF16),
        shaped((1, inner), F32),
        shaped((8, width), F32),
    ]
    specs = [whole((per, lay.piece, width))] * lay.ranks + [
        whole((rows, width)),
        pl.BlockSpec((1, CHUNK), lambda i: (0, hold(i))),
        whole((8, width)),
    ]
    if fast:
        def where(i):
            i = hold(i)
            at = {"x": 0, "y": 0, "z0": i % 2, "z1": i // 2}
            return tuple(at[name] for name in FC1_ORDER) + (0, 0)

        block = tuple(2 if name in ("x", "y") else 1 for name in FC1_ORDER) + (inner // 32, width)
        shapes += [shaped((2, 2, 2, 2, inner // 32, width), BF16)] * 2
        specs += [pl.BlockSpec(block, where)] * 2
        n = width // 32
        shapes += [shaped((2, 2, 2, 2, n, inner + width), BF16)] * 2
        specs += [pl.BlockSpec((2, 2, 2, 2, n, CHUNK), lambda i: (0, 0, 0, 0, 0, i))] * 2
    else:
        shapes += [shaped((inner, width), BF16), shaped((width, inner + width), BF16)]
        specs += [pl.BlockSpec((CHUNK, width), lambda i: (hold(i), 0)), pl.BlockSpec((width, CHUNK), lambda i: (0, i))]
    once = pl.Buffered(1)
    return pl.pallas_call(
        functools.partial(feed_forward, lay, per, fast),
        grid=(steps + 1,),
        in_specs=[
            SMEM,
            SMEM,
            SMEM,
            HBM,
            *[pl.BlockSpec(c.shape, lambda i: (0, 0, 0), pipeline_mode=once) for c in cot],
            pl.BlockSpec(n2.shape, lambda i: (0, 0), pipeline_mode=once),
            pl.BlockSpec((width, CHUNK), lambda i: (0, hold(i))),
            pl.BlockSpec((1, CHUNK), lambda i: (0, hold(i))),
            pl.BlockSpec((CHUNK, width), lambda i: (hold(i), 0)),
            whole(n2g.shape),
            whole(b2.shape),
            HBM,
        ],
        out_specs=specs,
        out_shape=shapes,
        scratch_shapes=[
            pltpu.VMEM((lay.ranks, lay.slots, width), BF16),
            pltpu.VMEM((lay.ranks, lay.piece, width), BF16),
            pltpu.VMEM((lay.rows, width), F32),
            pltpu.VMEM((rows, width), BF16),
            pltpu.VMEM((width, rows), BF16),
            pltpu.VMEM((rows + lay.spare, width), F32),
            pltpu.VMEM((rows, width), F32),
            pltpu.VMEM((rows, CHUNK), BF16),
            pltpu.VMEM((rows, CHUNK), BF16),
            pltpu.VMEM((per, lay.rows, width), F32),
            pltpu.VMEM((rows, width), BF16),
            pltpu.SemaphoreType.DMA,
            pltpu.SemaphoreType.DMA,
        ],
        compiler_params=params(),
        cost_estimate=cost(12 * rows * width * inner, 30e6, 2 * rows * inner),
    )(*meta, hidden, *cot, n2, w1, b1, w2, n2g, b2, mixed)


def late_sums(per, fast, rank_ref, gp_ref, normed_ref, dvec_ref, db1_ref, *refs):
    _, _, rows, width = gp_ref.shape
    dvecs = refs[:per]
    step = pl.program_id(0)
    sums = dot_tn(gp_ref[...].reshape(per * rows, width), normed_ref[...])
    if not fast:
        refs[per][...] = sums.astype(BF16)
        return
    own_refs, send_refs, held = refs[per : per + 2], refs[per + 2 : per + 4], refs[-1]
    held[pl.ds(pl.multiple_of(step * width, width), width), :] = sums

    @pl.when(step == pl.num_programs(0) - 1)
    def _():
        vec = dvecs[0][...]
        for more in dvecs[1:]:
            vec = vec + more[...]
        parts = [vec[i : i + 1] for i in range(4)]
        parts += [dvec_ref[2:3], dvec_ref[0:1], dvec_ref[1:2], dvec_ref[3:4]]
        packed = spread(parts, db1_ref[...])
        each = 3 * width // 32
        for dp in range(8):
            for y in range(2):
                d = dp * 4 + y * 2
                first = [held[e * each : e * each + LATE_CUT, :] for e in (d, d + 1)]
                second = [
                    with_vectors(held[e * each + LATE_CUT : (e + 1) * each, :], packed, e, width)
                    for e in (d, d + 1)
                ]
                for i, pair in enumerate((first, second)):
                    place = place_of(LATE_ORDERS[i], dp, y)
                    own_refs[i][place], send_refs[i][place] = keep_and_send(rank_ref[0] % 2, *pair)


def call_late_sums(fast, rank, gp, normed, dvec, db1, dvecs):
    per, _, rows, width = gp.shape
    if fast:
        heights = (LATE_CUT, 3 * width // 32 - LATE_CUT + 8)
        shapes = [shaped((2, 2, 2, 2, n, width), BF16) for n in heights] * 2
        specs = [whole(s.shape) for s in shapes]
        scratch = [pltpu.VMEM((3 * width, width), F32)]
    else:
        shapes = [shaped((3 * width, width), BF16)]
        specs = [pl.BlockSpec((width, width), lambda i: (i, 0))]
        scratch = []
    return pl.pallas_call(
        functools.partial(late_sums, per, fast),
        grid=(3,),
        in_specs=[SMEM, pl.BlockSpec((per, 1, rows, width), lambda i: (0, i, 0, 0)), whole(normed.shape)]
        + [whole(dvec.shape), whole(db1.shape)]
        + [whole(d.shape) for d in dvecs],
        out_specs=specs,
        out_shape=shapes,
        scratch_shapes=scratch,
        compiler_params=params(),
        cost_estimate=cost(6 * per * rows * width * width, 10e6),
    )(rank, gp, normed, dvec, db1, *dvecs)


def attention_backward(
    lay, k, linked, rank_ref, split_ref, tag_ref, ga_ref, qkv_ref, prob_ref, x_ref, n1g, wo_ref, wq, wk, wv, *refs
):
    gp_ref, *ig_refs, dvec_ref, gn, res, back = refs[linked:]
    rows = lay.rows
    group = pl.program_id(0)
    grad_mixed = dot_nt(ga_ref[0], wo_ref[...]).astype(BF16)
    masks = half_masks()

    @pl.when(group == 0)
    def _():
        dvec_ref[...] = jnp.zeros_like(dvec_ref)
        gn[...] = jnp.zeros_like(gn)

    for p in range(GROUP // 128):
        lanes = slice(p * 128, (p + 1) * 128)
        q = qkv_ref[0, 0, 0:rows, lanes]
        key = qkv_ref[0, 1, :, lanes]
        v = qkv_ref[0, 2, :, lanes]
        gm = grad_mixed[:, lanes]
        both = dot_nt(gm, jnp.concatenate([v * masks[0], v * masks[1]], 0))
        ds, probs = [], []
        for h in (0, 1):
            prob = prob_ref[0, 2 * p + h]
            weights = prob.astype(F32)
            gw = both[:, h * lay.keys : (h + 1) * lay.keys]
            delta = jnp.sum(weights * gw, -1, keepdims=True)
            ds.append((weights * (gw - delta)).astype(BF16))
            probs.append(prob)
        dq = dot(jnp.concatenate(ds, 1), jnp.concatenate([key * masks[0], key * masks[1]], 0))
        dk = dot_tn(jnp.concatenate([q * masks[0], q * masks[1]], 0), jnp.concatenate(ds, 0)).T
        dv = dot_tn(jnp.concatenate([gm * masks[0], gm * masks[1]], 0), jnp.concatenate(probs, 0)).T
        dq, dk, dv = (dq * 0.125).astype(BF16), dk[:rows].astype(BF16), dv[:rows].astype(BF16)
        gp_ref[0, 0, :, lanes] = dq
        gp_ref[0, 1, :, lanes] = dk
        gp_ref[0, 2, :, lanes] = dv
        at = pl.multiple_of(group * GROUP + p * 128, 128)
        dvec_ref[2:3, pl.ds(at, 128)] = jnp.sum(dq.astype(F32), 0, keepdims=True)
        dvec_ref[3:4, pl.ds(at, 128)] = jnp.sum(dv.astype(F32), 0, keepdims=True)
    gn[...] += sum(dot_nt(gp_ref[0, j], w[...]) for j, w in enumerate((wq, wk, wv)))

    @pl.when(group == pl.num_programs(0) - 1)
    def _():
        grad = gn[...]
        xhat, rstd = normalise(x_ref[0].astype(F32))
        dvec_ref[0:1] = jnp.sum(grad * xhat, 0, keepdims=True)
        dvec_ref[1:2] = jnp.sum(grad, 0, keepdims=True)
        res[0:rows] = ga_ref[0].astype(F32) + norm_backward(grad, row_of(n1g), xhat, rstd)
        repack(lay, res, 0, Image(lay, (rank_ref, split_ref, tag_ref), k), back)
        for j, ig_ref in enumerate(ig_refs):
            ig_ref[0] = back[j]


def call_backward(lay, k, per, meta, ga, qkv, prob, x, n1g, out_weight, qkv_weight, chain):
    rows, keys = lay.rows, lay.keys
    width = out_weight.shape[0]
    groups = width // GROUP
    alone = k == per - 1
    one = pl.BlockSpec((1, rows, width), lambda g: (k, 0, 0))
    args = [*meta, ga, qkv, prob, x, n1g, out_weight, qkv_weight, qkv_weight, qkv_weight]
    specs = [
        SMEM,
        SMEM,
        SMEM,
        one,
        pl.BlockSpec((1, 3, keys, GROUP), lambda g: (k, 0, 0, g)),
        pl.BlockSpec((1, HEADS // groups, rows, keys), lambda g: (k, g, 0, 0)),
        one,
        whole(n1g.shape),
        pl.BlockSpec((GROUP, width), lambda g: (g, 0)),
    ] + [pl.BlockSpec((width, GROUP), functools.partial(lambda j, g: (0, j * groups + g), j)) for j in range(3)]
    aliases = {}
    if chain is not None:
        count = 1 if alone else len(chain)
        aliases = {len(args) + i: i for i in range(count)}
        args += chain[:count]
        specs += [HBM] * count
    return pl.pallas_call(
        functools.partial(attention_backward, lay, k, len(args) - 12),
        grid=(groups,),
        in_specs=specs,
        out_specs=[
            pl.BlockSpec((1, 3, rows, GROUP), lambda g: (k, 0, 0, g)),
            *[pl.BlockSpec((1, lay.piece, width), lambda g: (0 if alone else k, 0, 0))] * lay.ranks,
            whole((8, width)),
        ],
        out_shape=[
            shaped((per, 3, rows, width), BF16),
            *[shaped((1 if alone else per - 1, lay.piece, width), BF16)] * lay.ranks,
            shaped((8, width), F32),
        ],
        scratch_shapes=[
            pltpu.VMEM((rows, width), F32),
            pltpu.VMEM((rows + lay.spare, width), F32),
            pltpu.VMEM((lay.ranks, lay.piece, width), BF16),
        ],
        input_output_aliases=aliases,
        compiler_params=params(),
        cost_estimate=cost(10e9, 10e6),
    )(*args)


def assemble(lay, rank_ref, split_ref, tag_ref, *refs):
    *got, passed_ref, out_ref = refs
    images, slots, width = out_ref.shape
    row = lax.broadcasted_iota(jnp.int32, (slots, width), 0)
    rank = rank_ref[0]
    first = 0
    for b in range(0, len(got), lay.ranks):
        for j, piece in enumerate(got[b : b + lay.ranks]):
            for k in range(piece.shape[0]):
                number = (rank ^ j) * lay.per + first + k
                image = jnp.minimum(number, images - 1)
                live = jnp.where(tag_ref[image] < lay.groups, split_ref[image, rank] * GRID, 0)

                @pl.when(number < images)
                def _():
                    worked = piece[k][:slots].astype(F32)
                    kept = passed_ref[image].astype(F32)
                    out_ref[image] = jnp.where(row < live, worked, kept).astype(BF16)

        first += got[b].shape[0]


def call_assemble(lay, meta, got, passed):
    args = [*meta, *got, passed]
    return pl.pallas_call(
        functools.partial(assemble, lay),
        in_specs=[SMEM] * 3 + [VMEM] * len(args[3:]),
        out_specs=VMEM,
        out_shape=shaped(passed.shape, BF16),
        compiler_params=params(SMALL_LIMIT),
        cost_estimate=cost(0, 5e6),
    )(*args)


class Part:
    def __init__(self, own, send, order, at=None):
        self.own, self.send, self.order = own, send, ["core", *order]
        self.got = self.sent = None
        self.at = at
        self.pending = None


def exchange(parts):
    for p in parts:
        if p.send is None:
            continue
        axis, weight = BITS[p.order[0]]
        size = lax.axis_size(axis)
        p.got = lax.ppermute(p.send, axis, [(i, i ^ weight) for i in range(size)])
        p.sent, p.send = p.send, None


def add_and_split(counts, mine_ref, *refs):
    n = len(counts)
    for i in range(n):
        own, got, keep, send = refs[2 * i], refs[2 * i + 1], refs[2 * n + 2 * i], refs[2 * n + 2 * i + 1]
        mine = mine_ref[i]
        keep[...] = (own[mine].astype(F32) + got[mine].astype(F32)).astype(BF16)
        send[...] = (own[1 - mine].astype(F32) + got[1 - mine].astype(F32)).astype(BF16)


def bit_of(name):
    axis, weight = BITS[name]
    return (lax.axis_index(axis) // weight) % 2


def add_sent(mine_ref, *refs):
    n = len(refs) // 3
    for i in range(n):
        refs[2 * n + i][...] = (refs[2 * i][...].astype(F32) + refs[2 * i + 1][...].astype(F32)).astype(BF16)


def send_first(parts, steps=2):
    args, ins, outs, shapes = [], [], [], []
    mine = jnp.stack([bit_of(p.order[1]) for p in parts])
    for i, p in enumerate(parts):
        n, width = p.own.shape[-2:]
        many = 2 ** (len(p.order) - 2)
        pair = [v.reshape(2, many, n, width) for v in (p.own, p.got)]
        args += pair
        place = functools.partial(lambda part, step, mine: (1 - mine[part], step, 0, 0), i)
        ins += [pl.BlockSpec((None, many // steps, n, width), place)] * 2
        outs.append(pl.BlockSpec((many // steps, n, width), lambda step, mine: (step, 0, 0)))
        shapes.append(shaped((many, n, width), BF16))
        p.pending = pair
    sends = pl.pallas_call(
        add_sent,
        grid_spec=pltpu.PrefetchScalarGridSpec(
            num_scalar_prefetch=1, grid=(steps,), in_specs=ins, out_specs=outs
        ),
        out_shape=shapes,
        compiler_params=params(),
        cost_estimate=cost(0, 10e6),
    )(mine, *args)
    for p, send in zip(parts, sends):
        p.order.pop(0)
        p.send = send.reshape(*[2] * (len(p.order) - 1), *send.shape[-2:])
        p.own = p.got = None


def add_three(n, bits_ref, *refs):
    for i in range(n):
        terms, keep, send = refs[3 * i : 3 * i + 3], refs[3 * n + 2 * i], refs[3 * n + 2 * i + 1]
        mine = bits_ref[n + i]
        keep[...] = sum(t[mine].astype(F32) for t in terms).astype(BF16)
        send[...] = sum(t[1 - mine].astype(F32) for t in terms).astype(BF16)


def combine_pending(parts, before, steps=2):
    tied, _ = lax.optimization_barrier(([(p.pending, p.got) for p in parts], before))
    bits = jnp.stack([bit_of(p.order[0]) for p in parts] + [bit_of(p.order[1]) for p in parts])
    args, ins, outs, shapes = [], [], [], []
    for i, (p, (pair, got)) in enumerate(zip(parts, tied)):
        n, width = pair[0].shape[-2:]
        many = pair[0].shape[1] // 2
        args += [v.reshape(2, 2, many, n, width) for v in pair] + [got.reshape(2, many, n, width)]
        place = functools.partial(lambda part, step, bits: (bits[part], 0, step, 0, 0), i)
        ins += [pl.BlockSpec((None, 2, many // steps, n, width), place)] * 2
        ins.append(pl.BlockSpec((2, many // steps, n, width), lambda step, bits: (0, step, 0, 0)))
        outs += [pl.BlockSpec((many // steps, n, width), lambda step, bits: (step, 0, 0))] * 2
        shapes += [shaped((many, n, width), BF16)] * 2
    res = pl.pallas_call(
        functools.partial(add_three, len(parts)),
        grid_spec=pltpu.PrefetchScalarGridSpec(
            num_scalar_prefetch=1, grid=(steps,), in_specs=ins, out_specs=outs
        ),
        out_shape=shapes,
        compiler_params=params(),
        cost_estimate=cost(0, 10e6),
    )(bits, *args)
    for i, p in enumerate(parts):
        p.order.pop(0)
        lead = [2] * (len(p.order) - 1)
        p.own, p.send = [v.reshape(*lead, *v.shape[-2:]) for v in res[2 * i : 2 * i + 2]]
        p.got = p.pending = None
    return res[0]


def combine(parts, before=()):
    parts = [p for p in parts if p.got is not None]
    if parts and parts[0].pending:
        return combine_pending(parts, before)
    last = [p for p in parts if len(p.order) == 1]
    for p in last:
        p.own = p.own.astype(F32) + p.got.astype(F32)
        p.got = p.send = None
        p.order = []
    parts = [p for p in parts if p.order]
    if not parts:
        return ()
    tied, _ = lax.optimization_barrier(([(p.own, p.got) for p in parts], before))
    for p, (p.own, p.got) in zip(parts, tied):
        pass
    views = []
    for p in parts:
        shape = p.own.shape
        flat = (2, 2 ** (len(p.order) - 2), *shape[-2:])
        if p.at is not None:
            flat = (shape[0], *flat)
        views.append((p.own.reshape(flat), p.got.reshape(flat)))
    size = sum(4 * v[0].size for v in views)
    steps = min(4 if size > 9e6 else 1, *(v[0].shape[-3] for v in views))
    ins, outs, shapes, args, mine = [], [], [], [], []
    for p, (own, got) in zip(parts, views):
        many, n, width = own.shape[-3:]
        block = (2, many // steps, n, width)
        if steps == 1:
            ins += [VMEM] * 2
            outs += [VMEM] * 2
            shapes += [shaped((many, n, width), BF16)] * 2
        elif p.at is None:
            ins += [pl.BlockSpec(block, lambda i: (0, i, 0, 0))] * 2
        else:
            ins += [pl.BlockSpec((None, *block), functools.partial(lambda a, i: (a, 0, i, 0, 0), p.at))] * 2
        if steps > 1:
            outs += [pl.BlockSpec(block[1:], lambda i: (i, 0, 0))] * 2
            shapes += [shaped((many, n, width), BF16)] * 2
        args += [own, got]
        axis, weight = BITS[p.order[1]]
        mine.append((lax.axis_index(axis) // weight) % 2)
    moved = sum(3 * a.size for a in args)
    res = pl.pallas_call(
        functools.partial(add_and_split, [None] * len(parts)),
        **({"grid": (steps,)} if steps > 1 else {}),
        in_specs=[SMEM] + ins,
        out_specs=outs,
        out_shape=shapes,
        compiler_params=params() if steps > 1 else params(SMALL_LIMIT),
        cost_estimate=cost(0, moved),
    )(jnp.stack(mine), *args)
    for i, p in enumerate(parts):
        shape = (*[2] * (len(p.order) - 2), *p.own.shape[-2:])
        p.at = None
        p.own, p.send = res[2 * i].reshape(shape), res[2 * i + 1].reshape(shape)
        p.got = None
        p.order.pop(0)
    return res[0]


def add_and_fan(heights, z_ref, *refs):
    ins, outs = refs[: 2 * len(heights)], refs[2 * len(heights) :]
    at = 0
    for i, n in enumerate(heights):
        own, got = ins[2 * i], ins[2 * i + 1]
        for j, out in enumerate(outs):
            place = (z_ref[0] % 2) ^ (j % 2), (z_ref[0] // 2) ^ (j // 2)
            total = own[place].astype(F32) + got[place].astype(F32)
            out[at : at + n, :] = total.astype(out.dtype)
        at += n


def fan(parts, before):
    tied, _ = lax.optimization_barrier(([(p.own, p.got) for p in parts], before))
    args = [a for pair in tied for a in pair]
    heights = [p.own.shape[2] for p in parts]
    width = args[0].shape[-1]
    z = lax.axis_index("dp") // 2
    shape = (sum(heights), width)
    own, *sends = pl.pallas_call(
        functools.partial(add_and_fan, heights),
        in_specs=[SMEM] + [VMEM] * len(args),
        out_specs=[VMEM] * 4,
        out_shape=[shaped(shape, F32)] + [shaped(shape, BF16)] * 3,
        compiler_params=params(SMALL_LIMIT),
        cost_estimate=cost(0, 1e6),
    )(z[None], *args)
    size = lax.axis_size("dp")
    got = [lax.ppermute(v, "dp", [(i, i ^ (2 * j)) for i in range(size)]) for j, v in zip((1, 2, 3), sends)]
    return own, sends, got


def wait(values, parts):
    live = [p for p in parts if p.got is not None]
    values, gots = lax.optimization_barrier((values, [p.got for p in live]))
    for p, g in zip(live, gots):
        p.got = g
    return values


def after(values, parts):
    return lax.optimization_barrier((values, [p.sent for p in parts if p.sent is not None]))[0]


def small_sum(value, n_dp, n_seq):
    for axis, size in (("seq", n_seq), ("dp", n_dp)):
        dim = 1 if axis == "seq" else 0
        weight = 1
        place = lax.axis_index(axis)
        while weight < size:
            shape = value.shape
            cut = value.reshape(*shape[:dim], shape[dim] // 2, 2, *shape[dim + 1 :])
            mine = (place // weight) % 2
            other = lax.dynamic_index_in_dim(cut, 1 - mine, dim + 1, keepdims=False)
            own = lax.dynamic_index_in_dim(cut, mine, dim + 1, keepdims=False)
            value = own + lax.ppermute(other, axis, [(i, i ^ weight) for i in range(size)])
            weight *= 2
    return value.reshape(-1)


def per_device(
    tokens,
    key_mask,
    row_split,
    group_tags,
    norm1_gain,
    norm1_shift,
    qkv_weight,
    query_bias,
    value_bias,
    out_weight,
    out_bias,
    norm2_gain,
    norm2_shift,
    fc1_weight,
    fc1_bias,
    fc2_weight,
    fc2_bias,
    out_cotangent,
):
    images, slots, width = tokens.shape
    n_seq = lax.axis_size("seq")
    n_dp = lax.axis_size("dp")
    devices = n_dp * n_seq
    rank = lax.axis_index("seq")
    lay = Rows(n_seq, slots, images, n_dp)
    per, rows = lay.per, lay.rows
    meta = rank[None], row_split, group_tags
    all_rows = per * rows
    fast = (n_dp, n_seq) == (8, 4)

    def swap(value, j):
        return lax.ppermute(value, "seq", [(i, i ^ j) for i in range(n_seq)])

    def rows_of(array, owner, k):
        return lax.dynamic_slice_in_dim(array, jnp.minimum(owner * per + k, images - 1), 1, 0)

    def cut_for(array, which):
        got = []
        for j in range(n_seq):
            mine = [rows_of(array, rank ^ j, k) for k in which]
            got.append(mine[0] if len(mine) == 1 else jnp.concatenate(mine, 0))
        return got

    def bring(mine):
        return [mine[0]] + [swap(mine[j], j) for j in range(1, n_seq)]

    vecs = (norm1_gain, norm1_shift, out_bias, norm2_gain, norm2_shift, query_bias, value_bias)

    first, rest = cut_for(tokens, [0]), cut_for(tokens, list(range(1, per)))
    cot = cut_for(out_cotangent, list(range(per)))
    first = bring(first)
    first, rest = lax.optimization_barrier((first, rest))
    chain = call_forward(lay, 0, 1, meta, first, key_mask, vecs, qkv_weight, out_weight, None)
    rest = bring(rest)
    chain, rest, cot = lax.optimization_barrier((chain, rest, cot))
    chain = call_forward(lay, 1, per - 1, meta, rest, key_mask, vecs, qkv_weight, out_weight, chain)
    hidden, x_all, normed_all, mixed_all, n2, qkv, prob = chain
    n2 = n2.reshape(all_rows, width)

    cot = bring(cot)
    res = call_feed(
        lay,
        per,
        fast,
        meta,
        hidden,
        cot,
        n2,
        fc1_weight,
        fc1_bias.astype(F32)[None],
        fc2_weight,
        norm2_gain,
        fc2_bias,
        mixed_all.reshape(all_rows, width),
    )
    out_pieces, (ga, db1, dvec2, *dw) = list(res[:n_seq]), res[n_seq:]

    fc = late = []
    if fast:
        fc = [Part(*dw[:2], FC1_ORDER), Part(*dw[2:], FC2_ORDER)]
    out_got = [swap(out_pieces[j], j) for j in range(2, n_seq)]
    exchange(fc)
    ga = ga.reshape(per, rows, width)

    chain = None
    dvecs, ig, ig_got = [], [], []
    for k in range(per):
        *chain, dvec = call_backward(
            lay, k, per, meta, ga, qkv, prob, x_all, norm1_gain, out_weight, qkv_weight, chain
        )
        dvecs.append(dvec)
        if k == 0:
            chain, out_got[0] = lax.optimization_barrier((chain, out_got[0]))
        if k == 1:
            chain, out_got, out_pieces = lax.optimization_barrier((chain, out_got, out_pieces))
            out_got = [out_pieces[0], swap(out_pieces[1], 1), *out_got]
        if k == 2:
            chain, ig_got[0] = lax.optimization_barrier((chain, ig_got[0]))
        if k >= per - 2:
            ig.append(chain[1:3])
            ig_got.append([swap(chain[1 + j], j) for j in range(2, n_seq)])
        if k != 1:
            chain = wait(chain, fc)
            if fast and k == 0:
                send_first(fc)
            else:
                combine(fc)
            exchange(fc)
            ga, chain = after((ga, chain), fc)
    gp = chain[0]
    dwl = call_late_sums(fast, meta[0], gp, normed_all.reshape(all_rows, width), dvec2, db1, dvecs)
    if fast:
        dwl, ig_got[1] = wait((dwl, ig_got[1]), fc)
        late = [Part(dwl[i], dwl[2 + i], order) for i, order in enumerate(LATE_ORDERS)]
        exchange(late)
        token = combine(fc, dwl)
        exchange(fc)
        token = combine(late, token)
        exchange(late)
        out_got, ig, _ = lax.optimization_barrier((out_got, ig, token))
    output = call_assemble(lay, meta, out_got, tokens)
    if fast:
        token = combine(late, output)
        exchange(late)
        token = combine(fc, token)
        exchange(fc)
        ig = after(ig, late)
    ig_got = [g for near, far in zip(ig, ig_got) for g in (near[0], swap(near[1], 1), *far)]
    if fast:
        own, sends, got = fan(late, token)
        ig_got, _ = lax.optimization_barrier((ig_got, sends))
    input_grad = call_assemble(lay, meta, ig_got, out_cotangent)
    if fast:
        input_grad, fc[0].got, fc[1].got = lax.optimization_barrier((input_grad, fc[0].got, fc[1].got))
        combine(fc)
        inner = fc1_weight.shape[1]
        done = fc[0].own.T, fc[1].own[:, :inner].T, fc[1].own[:, inner:].T
        done, got = lax.optimization_barrier((done, got))
        late_sum = own + sum(g.astype(F32) for g in got)

    part = width // devices
    inner = fc1_weight.shape[1]
    if fast:
        qkv_sum, small = late_sum[: 3 * part], late_sum[3 * part]
        small_late, small_early = small[: 4 * part], small[4 * part :]
    else:
        *done, qkv_sum = [
            lax.psum_scatter(v.astype(F32), ("dp", "seq"), scatter_dimension=0, tiled=True)
            for v in (dw[0], dw[1][:, :inner], dw[1][:, inner:], dwl[0])
        ]
        done = [v.T for v in done]
        dvec1 = sum(dvecs)

        def by_device(v):
            return v.reshape(n_dp, n_seq, v.shape[0] // devices)

        early = (dvec2[2], dvec2[0], dvec2[1], dvec2[3], db1[0])
        small_early = small_sum(jnp.concatenate([by_device(v) for v in early], -1), n_dp, n_seq)
        small_late = small_sum(jnp.concatenate([by_device(dvec1[i]) for i in range(4)], -1), n_dp, n_seq)
    vec = [small_late[i * part : (i + 1) * part] for i in range(4)]
    vec += [small_early[i * part : (i + 1) * part] for i in range(4)]
    vec.append(small_early[4 * part : 4 * part + fc1_bias.shape[0] // devices])
    return (
        output,
        input_grad,
        vec[0],
        vec[1],
        qkv_sum.T,
        vec[2],
        vec[3],
        done[2],
        vec[4],
        vec[5],
        vec[6],
        done[0],
        vec[8],
        done[1],
        vec[7],
    )


def solution(mesh):
    rows = P("dp", "seq", None)
    split = P(("dp", "seq"))
    columns = P(None, ("dp", "seq"))
    return jax.shard_map(
        per_device,
        mesh=mesh,
        in_specs=(rows, P("dp", None), P("dp", None), P("dp")) + (P(),) * 13 + (rows,),
        out_specs=(
            rows,
            rows,
            split,
            split,
            columns,
            split,
            split,
            columns,
            split,
            split,
            split,
            columns,
            split,
            columns,
            split,
        ),
        check_vma=False,
    )
```

```python
import functools

import jax
import jax.numpy as jnp
from jax import lax
from jax.experimental import pallas as pl
from jax.experimental.pallas import tpu as pltpu
from jax.sharding import PartitionSpec as P

HEADS = 12
GRID = 18
EPS = 1e-06
NEG = -1e30
F32 = jnp.float32
BF16 = jnp.bfloat16
VMEM_LIMIT = 60 * 1024 * 1024
CHUNK = 768
GROUP = 256
LANES = 384

BITS = {"core": ("seq", 1), "y": ("seq", 2), "x": ("dp", 1), "z0": ("dp", 2), "z1": ("dp", 4)}
FC1_ORDER = ("x", "z0", "z1", "y")
FC2_ORDER = ("z0", "x", "y", "z1")
LATE_ORDERS = (("x", "y", "z0", "z1"), ("y", "x", "z0", "z1"))
LATE_CUT = 48
SMEM = pl.BlockSpec(memory_space=pltpu.SMEM)
VMEM = pl.BlockSpec(memory_space=pltpu.VMEM)
SMALL_LIMIT = 8 * 1024 * 1024
HBM = pl.BlockSpec(memory_space=pl.ANY)


def round_up(n, to):
    return -(-n // to) * to


class Rows:
    def __init__(self, ranks, slots, images, groups):
        self.images, self.groups = images, groups
        self.per = -(-images // ranks)
        base, extra = GRID // ranks, GRID % ranks
        self.lens = [min(slots, (base + 1) * GRID)] * extra + [base * GRID] * (ranks - extra)
        self.extra = extra
        self.ranks = ranks
        self.slots = slots
        self.offs = []
        at = 0
        for n in self.lens:
            self.offs.append(at)
            at += round_up(n, 8)
        self.rows = round_up(at, 16)
        self.keys = round_up(self.rows, 128)
        self.piece = round_up(slots, 16)
        end = max(o + round_up(n, 16) for o, n in zip(self.offs, self.lens))
        self.spare = max(round_up(end, 8) - self.rows, 0)

    def is_row(self, index):
        hit = None
        for off, n in zip(self.offs, self.lens):
            one = (index >= off) & (index < off + n)
            hit = one if hit is None else hit | one
        return hit


def dot(a, b):
    return lax.dot_general(a, b, (((1,), (0,)), ((), ())), preferred_element_type=F32)


def dot_nt(a, b):
    return lax.dot_general(a, b, (((1,), (1,)), ((), ())), preferred_element_type=F32)


def dot_tn(a, b):
    return lax.dot_general(a, b, (((0,), (0,)), ((), ())), preferred_element_type=F32)


def params(limit=VMEM_LIMIT):
    return pltpu.CompilerParams(vmem_limit_bytes=limit)


def cost(flops, moved, exps=0):
    return pl.CostEstimate(flops=int(flops) // 16, bytes_accessed=int(moved) // 16, transcendentals=int(exps) // 16)


def whole(shape):
    return pl.BlockSpec(shape, lambda *i: (0,) * len(shape))


def shaped(shape, dtype):
    return jax.ShapeDtypeStruct(shape, dtype)


class Image:
    def __init__(self, lay, meta, k):
        rank_ref, split_ref, tag_ref = meta
        rank = rank_ref[0]
        self.index = jnp.minimum(rank * lay.per, lay.images - lay.per) + k
        base = GRID // lay.ranks
        longs, shorts = jnp.int32(0), jnp.int32(lay.extra)
        self.sources = [jnp.int32(0)] * lay.ranks
        for r in range(lay.ranks):
            is_long = split_ref[self.index, r] > base
            place = jnp.where(is_long, longs, shorts)
            longs = longs + jnp.where(is_long, 1, 0)
            shorts = shorts + jnp.where(is_long, 0, 1)
            self.sources = [jnp.where(place == i, r, s) for i, s in enumerate(self.sources)]
        self.pieces = [s ^ rank for s in self.sources]
        self.counts = jnp.where((tag_ref[self.index] < lay.groups) & (self.index >= rank * lay.per), 1, 0)


def unpack(lay, stage, image, to_ref):
    width = to_ref.shape[1]
    for i, (off, n) in enumerate(zip(lay.offs, lay.lens)):
        full = round_up(n, 8)
        if full > n:
            to_ref[off + full - 8 : off + full, :] = jnp.zeros((8, width), F32)
        piece = stage[image.pieces[i]].astype(F32)
        to_ref[off : off + n, :] = piece[:n]
    last = lay.offs[-1] + round_up(lay.lens[-1], 8)
    if lay.rows > last:
        to_ref[last : lay.rows, :] = jnp.zeros((lay.rows - last, width), F32)


def repack(lay, from_ref, start, image, stage):
    for i, (off, n) in enumerate(zip(lay.offs, lay.lens)):
        full = round_up(n, 16)
        stage[image.pieces[i], 0:full, :] = from_ref[start + off : start + off + full, :].astype(BF16)


def mask_of(lay, image, key_ref):
    slots = key_ref.shape[1]
    row = jnp.broadcast_to(key_ref[pl.ds(image.index, 1), :], (8, slots)).astype(F32)
    lane = lax.broadcasted_iota(jnp.int32, (slots, lay.keys), 1)
    want = jnp.full((slots, lay.keys), -1, jnp.int32)
    for i, (off, n) in enumerate(zip(lay.offs, lay.lens)):
        want = jnp.where((lane >= off) & (lane < off + n), lane + (image.sources[i] * lay.slots - off), want)
    pick = (lax.broadcasted_iota(jnp.int32, (slots, lay.keys), 0) == want).astype(F32).astype(BF16)
    valid = jnp.where(row > 0, 1.0, 0.0).astype(BF16)
    return jnp.where(dot(valid, pick)[0:1] > 0.5, 0.0, NEG)


def row_of(ref):
    return ref[...].astype(F32).reshape(1, -1)


def live_column(lay, image):
    index = lax.broadcasted_iota(jnp.int32, (lay.rows, 1), 0)
    return jnp.where(lay.is_row(index), image.counts, 0).astype(F32)


def normalise(x):
    mean = jnp.mean(x, -1, keepdims=True)
    centered = x - mean
    rstd = lax.rsqrt(jnp.mean(centered * centered, -1, keepdims=True) + EPS)
    return centered * rstd, rstd


def norm_backward(grad, gain, xhat, rstd):
    scaled = grad * gain
    row = scaled - jnp.mean(scaled, -1, keepdims=True)
    return rstd * (row - xhat * jnp.mean(scaled * xhat, -1, keepdims=True))


def half_masks():
    lane = lax.broadcasted_iota(jnp.int32, (1, 128), 1)
    return [(lane < 64).astype(BF16), (lane >= 64).astype(BF16)]


def keep_and_send(core, even, odd):
    mine = core == 0
    return jnp.where(mine, even, odd).astype(BF16), jnp.where(mine, odd, even).astype(BF16)


def parts_of(rows, each):
    n = rows.shape[1]
    place = lax.broadcasted_iota(jnp.int32, rows.shape, 0) % (n // each) * each
    lane = lax.broadcasted_iota(jnp.int32, rows.shape, 1)
    return jnp.where((lane >= place) & (lane < place + each), rows, 0.0).astype(BF16)


def picker(n, each):
    source = lax.broadcasted_iota(jnp.int32, (n, 128), 0)
    part = ((source.astype(F32) + 0.5) * (1.0 / each)).astype(jnp.int32)
    target = lax.broadcasted_iota(jnp.int32, (n, 128), 1)
    return (source - part * each == target).astype(F32).astype(BF16)


def spread(vectors, long):
    n, m = vectors[0].shape[1], long.shape[1]
    each, long_each = n // 32, m // 32
    rows = [parts_of(jnp.broadcast_to(v, (32, n)), each) for v in vectors]
    found = dot(jnp.concatenate(rows, 0), picker(n, each))
    many = m // n
    group = lax.broadcasted_iota(jnp.int32, (32, n), 0) // (32 // many)
    chosen = sum(jnp.where(group == i, long[:, i * n : (i + 1) * n], 0.0) for i in range(many))
    last = dot(parts_of(chosen, long_each), picker(n, long_each))
    blank = jnp.zeros((32, LANES - 128), F32)
    total = pltpu.roll(jnp.concatenate([last, blank], 1), each * len(vectors), 1)
    for i in range(len(vectors)):
        one = jnp.concatenate([found[i * 32 : (i + 1) * 32], blank], 1)
        total = total + (pltpu.roll(one, each * i, 1) if i else one)
    return total


def with_vectors(rows, packed, d, width):
    lanes = packed.shape[1]
    vec = jnp.broadcast_to(packed[d : d + 1, :], (8, lanes))
    return jnp.concatenate([rows, jnp.concatenate([vec, jnp.zeros((8, width - lanes), F32)], 1)], 0)


def place_of(order, dp, y):
    bits = {"x": dp % 2, "z0": dp // 2 % 2, "z1": dp // 4, "y": y}
    return tuple(bits[name] for name in order)


def attention_forward(
    lay, first, linked, rank_ref, split_ref, tag_ref, p0, p1, p2, p3, key_ref, n1g, n1s, ob, n2g, n2s, qb, vb, wq, wk, wv, wo, *refs
):
    outs = refs[7:] if linked else refs
    hid_ref, x_ref, normed_ref, mixed_ref, n2_ref, qkv_ref, prob_ref, stage, xs, bias, mask = outs
    rows, keys = lay.rows, lay.keys
    group = pl.program_id(1)
    image = Image(lay, (rank_ref, split_ref, tag_ref), first + pl.program_id(0))

    @pl.when(group == 0)
    def _():
        for j, piece in enumerate((p0, p1, p2, p3)):
            stage[j] = piece[0]
        unpack(lay, stage, image, xs)
        mask[...] = jnp.broadcast_to(mask_of(lay, image, key_ref), mask.shape)
        bias[0:1, :] = row_of(qb)
        bias[1:2, :] = jnp.zeros((1, bias.shape[1]), F32)
        bias[2:3, :] = row_of(vb)
        x = xs[...]
        x_ref[0] = x.astype(BF16)
        xhat, _ = normalise(x)
        normed_ref[0] = (xhat * row_of(n1g) + row_of(n1s)).astype(BF16)

    normed = normed_ref[0]
    qkv = []
    for j, weight in enumerate((wq, wk, wv)):
        part = dot(normed, weight[...]) + bias[j : j + 1, pl.ds(pl.multiple_of(group * GROUP, GROUP), GROUP)]
        if j == 0:
            part = part * 0.125
        part = part.astype(BF16)
        if j and keys > rows:
            part = jnp.concatenate([part, jnp.zeros((keys - rows, GROUP), BF16)], 0)
        qkv_ref[0, j, 0 : part.shape[0], :] = part
    if keys > rows:
        qkv_ref[0, 0, rows:keys, :] = jnp.zeros((keys - rows, GROUP), BF16)
    masks = half_masks()
    for p in range(GROUP // 128):
        lanes = slice(p * 128, (p + 1) * 128)
        q = qkv_ref[0, 0, 0:rows, lanes]
        k = qkv_ref[0, 1, :, lanes]
        v = qkv_ref[0, 2, :, lanes]
        both = dot_nt(q, jnp.concatenate([k * masks[0], k * masks[1]], 0))
        probs = []
        for h in (0, 1):
            s = both[:, h * keys : (h + 1) * keys] + mask[0:1, :]
            e = jnp.exp(s - jnp.max(s, -1, keepdims=True))
            prob = (e * (1.0 / jnp.sum(e, -1, keepdims=True))).astype(BF16)
            prob_ref[0, 2 * p + h] = prob
            probs.append(prob)
        total = dot(jnp.concatenate(probs, 1), jnp.concatenate([v * masks[0], v * masks[1]], 0))
        at = pl.multiple_of(group * GROUP + p * 128, 128)
        mixed_ref[0, :, pl.ds(at, 128)] = total.astype(BF16)

    @pl.when(group == pl.num_programs(1) - 1)
    def _():
        attended = dot(mixed_ref[0], wo[...]) + row_of(ob)
        hidden = xs[...] + live_column(lay, image) * attended
        hid_ref[0] = hidden
        xhat, _ = normalise(hidden)
        n2_ref[0] = (xhat * row_of(n2g) + row_of(n2s)).astype(BF16)


def call_forward(lay, first, count, meta, pieces, key_mask, vecs, qkv_weight, out_weight, chain):
    per, rows, keys = lay.per, lay.rows, lay.keys
    width = out_weight.shape[0]
    groups = width // GROUP
    shapes = [
        shaped((per, rows, width), F32),
        shaped((per, rows, width), BF16),
        shaped((per, rows, width), BF16),
        shaped((per, rows, width), BF16),
        shaped((per, rows, width), BF16),
        shaped((per, 3, keys, width), BF16),
        shaped((per, HEADS, rows, keys), BF16),
    ]
    args = [*meta, *pieces, key_mask, *vecs, qkv_weight, qkv_weight, qkv_weight, out_weight]
    specs = (
        [SMEM] * 3
        + [pl.BlockSpec((1, lay.slots, width), lambda i, g: (i, 0, 0))] * len(pieces)
        + [whole(v.shape) for v in (key_mask, *vecs)]
        + [pl.BlockSpec((width, GROUP), functools.partial(lambda j, i, g: (0, j * groups + g), j)) for j in range(3)]
        + [whole(out_weight.shape)]
    )
    aliases = {}
    if chain is not None:
        aliases = {len(args) + i: i for i in range(7)}
        args += chain
        specs += [HBM] * 7
    return list(
        pl.pallas_call(
            functools.partial(attention_forward, lay, first, chain is not None),
            grid=(count, groups),
            in_specs=specs,
            out_specs=[pl.BlockSpec((1, rows, width), lambda i, g: (first + i, 0, 0))] * 5
            + [
                pl.BlockSpec((1, 3, keys, GROUP), lambda i, g: (first + i, 0, 0, g)),
                pl.BlockSpec((1, HEADS // groups, rows, keys), lambda i, g: (first + i, g, 0, 0)),
            ],
            out_shape=shapes,
            scratch_shapes=[
                pltpu.VMEM((lay.ranks, lay.slots, width), BF16),
                pltpu.VMEM((rows, width), F32),
                pltpu.VMEM((8, width), F32),
                pltpu.VMEM((8, keys), F32),
            ],
            input_output_aliases=aliases,
            compiler_params=params(),
            cost_estimate=cost(8e9 * count, 12e6 * count, HEADS * rows * keys * count),
        )(*args)
    )


def feed_forward(
    lay, per, fast, rank_ref, split_ref, tag_ref, hid_hbm, c0, c1, c2, c3, n2_ref, w1_ref, b1_ref, w2_ref, n2g, b2_ref, mixed_hbm, *refs
):
    out_refs = refs[: lay.ranks]
    ga_ref, db1_ref, dvec_ref, *dw = refs[lay.ranks : -13]
    stage, back, cot, gr, grt, red, gn, act, gexp, hid, mixed, sem, sem2 = refs[-13:]
    step = pl.program_id(0)
    last = pl.num_programs(0) - 1
    rows = lay.rows
    meta = rank_ref, split_ref, tag_ref
    fetch = pltpu.make_async_copy(hid_hbm, hid, sem)
    fetch2 = pltpu.make_async_copy(mixed_hbm, mixed, sem2)

    @pl.when(step == 0)
    def _():
        fetch.start()
        fetch2.start()
        total = None
        for k in range(per):
            block = slice(k * rows, (k + 1) * rows)
            for j, piece in enumerate((c0, c1, c2, c3)):
                stage[j] = piece[k]
            image = Image(lay, meta, k)
            unpack(lay, stage, image, cot)
            wide = live_column(lay, image) * cot[...]
            gr[block, :] = wide.astype(BF16)
            grt[:, block] = wide.T.astype(BF16)
            total = jnp.sum(wide, 0, keepdims=True) + (0.0 if total is None else total)
        dvec_ref[...] = jnp.zeros_like(dvec_ref)
        dvec_ref[3:4] = total
        red[...] = jnp.zeros_like(red)
        gn[...] = jnp.zeros_like(gn)

    def share_fc2(sums):
        own2, send2 = dw[-2:]
        n = sums.shape[0] // 32
        for dp in range(8):
            for y in range(2):
                at = (dp * 4 + y * 2) * n
                place = place_of(FC2_ORDER, dp, y)
                own2[place], send2[place] = keep_and_send(
                    rank_ref[0] % 2, sums[at : at + n], sums[at + n : at + 2 * n]
                )

    @pl.when(step < last)
    def _():
        total = None
        for k in range(per):
            block = slice(k * rows, (k + 1) * rows)
            grads = []
            for c in range(0, CHUNK, 256):
                lanes = slice(c, c + 256)
                expanded = dot(n2_ref[block, :], w1_ref[:, lanes]) + b1_ref[:, lanes]
                grad_active = dot_nt(gr[block, :], w2_ref[lanes, :])
                cdf = 0.5 * (1.0 + lax.erf(expanded * 0.7071067811865476))
                slope = cdf + expanded * (jnp.exp(-0.5 * expanded * expanded) * 0.3989422804014327)
                act[block, lanes] = (expanded * cdf).astype(BF16)
                grad_exp = (grad_active * slope).astype(BF16)
                gexp[block, lanes] = grad_exp
                grads.append(jnp.sum(grad_exp.astype(F32), 0, keepdims=True))
            grads = jnp.concatenate(grads, 1)
            total = grads + (0.0 if total is None else total)
            red[block, :] += dot(act[block, :], w2_ref[...])
            gn[block, :] += dot_nt(gexp[block, :], w1_ref[...])
        db1_ref[...] = total
        sums1 = dot_tn(gexp[...], n2_ref[...])
        sums2 = dot(grt[...], act[...])
        if fast:
            own1, send1 = dw[:2]
            n = CHUNK // 8
            for i in range(2):
                for y in range(2):
                    at = (i * 4 + y * 2) * n
                    place = place_of(FC1_ORDER, i, y)
                    own1[place], send1[place] = keep_and_send(
                        rank_ref[0] % 2, sums1[at : at + n], sums1[at + n : at + 2 * n]
                    )
            share_fc2(sums2)
        else:
            dw[0][...] = sums1.astype(BF16)
            dw[1][...] = sums2.astype(BF16)

    @pl.when(step == last)
    def _():
        fetch.wait()
        fetch2.wait()
        for k in range(per):
            block = slice(k * rows, (k + 1) * rows)
            live = live_column(lay, Image(lay, meta, k))
            hidden = hid[k]
            red[block, :] = hidden + live * (red[block, :] + row_of(b2_ref))
            xhat, rstd = normalise(hidden)
            grad = gn[block, :]
            dvec_ref[0:1] += jnp.sum(grad * xhat, 0, keepdims=True)
            dvec_ref[1:2] += jnp.sum(grad, 0, keepdims=True)
            row = norm_backward(grad, row_of(n2g), xhat, rstd)
            attended = (live * (gr[block, :].astype(F32) + row)).astype(BF16)
            ga_ref[block, :] = attended
            dvec_ref[2:3] += jnp.sum(attended.astype(F32), 0, keepdims=True)
        for k in range(per):
            repack(lay, red, k * rows, Image(lay, meta, k), back)
            for j, out_ref in enumerate(out_refs):
                out_ref[k] = back[j]
        sums = dot_tn(ga_ref[...], mixed[...])
        if fast:
            share_fc2(sums)
        else:
            dw[1][...] = sums.astype(BF16)


def call_feed(lay, per, fast, meta, hidden, cot, n2, w1, b1, w2, n2g, b2, mixed):
    width, inner = w1.shape
    rows = per * lay.rows
    steps = inner // CHUNK

    def hold(i):
        return jnp.minimum(i, steps - 1)

    shapes = [shaped((per, lay.piece, width), BF16)] * lay.ranks + [
        shaped((rows, width), BF16),
        shaped((1, inner), F32),
        shaped((8, width), F32),
    ]
    specs = [whole((per, lay.piece, width))] * lay.ranks + [
        whole((rows, width)),
        pl.BlockSpec((1, CHUNK), lambda i: (0, hold(i))),
        whole((8, width)),
    ]
    if fast:
        def where(i):
            i = hold(i)
            at = {"x": 0, "y": 0, "z0": i % 2, "z1": i // 2}
            return tuple(at[name] for name in FC1_ORDER) + (0, 0)

        block = tuple(2 if name in ("x", "y") else 1 for name in FC1_ORDER) + (inner // 32, width)
        shapes += [shaped((2, 2, 2, 2, inner // 32, width), BF16)] * 2
        specs += [pl.BlockSpec(block, where)] * 2
        n = width // 32
        shapes += [shaped((2, 2, 2, 2, n, inner + width), BF16)] * 2
        specs += [pl.BlockSpec((2, 2, 2, 2, n, CHUNK), lambda i: (0, 0, 0, 0, 0, i))] * 2
    else:
        shapes += [shaped((inner, width), BF16), shaped((width, inner + width), BF16)]
        specs += [pl.BlockSpec((CHUNK, width), lambda i: (hold(i), 0)), pl.BlockSpec((width, CHUNK), lambda i: (0, i))]
    once = pl.Buffered(1)
    return pl.pallas_call(
        functools.partial(feed_forward, lay, per, fast),
        grid=(steps + 1,),
        in_specs=[
            SMEM,
            SMEM,
            SMEM,
            HBM,
            *[pl.BlockSpec(c.shape, lambda i: (0, 0, 0), pipeline_mode=once) for c in cot],
            pl.BlockSpec(n2.shape, lambda i: (0, 0), pipeline_mode=once),
            pl.BlockSpec((width, CHUNK), lambda i: (0, hold(i))),
            pl.BlockSpec((1, CHUNK), lambda i: (0, hold(i))),
            pl.BlockSpec((CHUNK, width), lambda i: (hold(i), 0)),
            whole(n2g.shape),
            whole(b2.shape),
            HBM,
        ],
        out_specs=specs,
        out_shape=shapes,
        scratch_shapes=[
            pltpu.VMEM((lay.ranks, lay.slots, width), BF16),
            pltpu.VMEM((lay.ranks, lay.piece, width), BF16),
            pltpu.VMEM((lay.rows, width), F32),
            pltpu.VMEM((rows, width), BF16),
            pltpu.VMEM((width, rows), BF16),
            pltpu.VMEM((rows + lay.spare, width), F32),
            pltpu.VMEM((rows, width), F32),
            pltpu.VMEM((rows, CHUNK), BF16),
            pltpu.VMEM((rows, CHUNK), BF16),
            pltpu.VMEM((per, lay.rows, width), F32),
            pltpu.VMEM((rows, width), BF16),
            pltpu.SemaphoreType.DMA,
            pltpu.SemaphoreType.DMA,
        ],
        compiler_params=params(),
        cost_estimate=cost(12 * rows * width * inner, 30e6, 2 * rows * inner),
    )(*meta, hidden, *cot, n2, w1, b1, w2, n2g, b2, mixed)


def late_sums(per, fast, rank_ref, gp_ref, normed_ref, dvec_ref, db1_ref, *refs):
    _, _, rows, width = gp_ref.shape
    dvecs = refs[:per]
    step = pl.program_id(0)
    sums = dot_tn(gp_ref[...].reshape(per * rows, width), normed_ref[...])
    if not fast:
        refs[per][...] = sums.astype(BF16)
        return
    own_refs, send_refs, held = refs[per : per + 2], refs[per + 2 : per + 4], refs[-1]
    held[pl.ds(pl.multiple_of(step * width, width), width), :] = sums

    @pl.when(step == pl.num_programs(0) - 1)
    def _():
        vec = dvecs[0][...]
        for more in dvecs[1:]:
            vec = vec + more[...]
        parts = [vec[i : i + 1] for i in range(4)]
        parts += [dvec_ref[2:3], dvec_ref[0:1], dvec_ref[1:2], dvec_ref[3:4]]
        packed = spread(parts, db1_ref[...])
        each = 3 * width // 32
        for dp in range(8):
            for y in range(2):
                d = dp * 4 + y * 2
                first = [held[e * each : e * each + LATE_CUT, :] for e in (d, d + 1)]
                second = [
                    with_vectors(held[e * each + LATE_CUT : (e + 1) * each, :], packed, e, width)
                    for e in (d, d + 1)
                ]
                for i, pair in enumerate((first, second)):
                    place = place_of(LATE_ORDERS[i], dp, y)
                    own_refs[i][place], send_refs[i][place] = keep_and_send(rank_ref[0] % 2, *pair)


def call_late_sums(fast, rank, gp, normed, dvec, db1, dvecs):
    per, _, rows, width = gp.shape
    if fast:
        heights = (LATE_CUT, 3 * width // 32 - LATE_CUT + 8)
        shapes = [shaped((2, 2, 2, 2, n, width), BF16) for n in heights] * 2
        specs = [whole(s.shape) for s in shapes]
        scratch = [pltpu.VMEM((3 * width, width), F32)]
    else:
        shapes = [shaped((3 * width, width), BF16)]
        specs = [pl.BlockSpec((width, width), lambda i: (i, 0))]
        scratch = []
    return pl.pallas_call(
        functools.partial(late_sums, per, fast),
        grid=(3,),
        in_specs=[SMEM, pl.BlockSpec((per, 1, rows, width), lambda i: (0, i, 0, 0)), whole(normed.shape)]
        + [whole(dvec.shape), whole(db1.shape)]
        + [whole(d.shape) for d in dvecs],
        out_specs=specs,
        out_shape=shapes,
        scratch_shapes=scratch,
        compiler_params=params(),
        cost_estimate=cost(6 * per * rows * width * width, 10e6),
    )(rank, gp, normed, dvec, db1, *dvecs)


def attention_backward(
    lay, k, linked, rank_ref, split_ref, tag_ref, ga_ref, qkv_ref, prob_ref, x_ref, n1g, wo_ref, wq, wk, wv, *refs
):
    gp_ref, *ig_refs, dvec_ref, gn, res, back = refs[linked:]
    rows = lay.rows
    group = pl.program_id(0)
    grad_mixed = dot_nt(ga_ref[0], wo_ref[...]).astype(BF16)
    masks = half_masks()

    @pl.when(group == 0)
    def _():
        dvec_ref[...] = jnp.zeros_like(dvec_ref)
        gn[...] = jnp.zeros_like(gn)

    for p in range(GROUP // 128):
        lanes = slice(p * 128, (p + 1) * 128)
        q = qkv_ref[0, 0, 0:rows, lanes]
        key = qkv_ref[0, 1, :, lanes]
        v = qkv_ref[0, 2, :, lanes]
        gm = grad_mixed[:, lanes]
        both = dot_nt(gm, jnp.concatenate([v * masks[0], v * masks[1]], 0))
        ds, probs = [], []
        for h in (0, 1):
            prob = prob_ref[0, 2 * p + h]
            weights = prob.astype(F32)
            gw = both[:, h * lay.keys : (h + 1) * lay.keys]
            delta = jnp.sum(weights * gw, -1, keepdims=True)
            ds.append((weights * (gw - delta)).astype(BF16))
            probs.append(prob)
        dq = dot(jnp.concatenate(ds, 1), jnp.concatenate([key * masks[0], key * masks[1]], 0))
        dk = dot_tn(jnp.concatenate([q * masks[0], q * masks[1]], 0), jnp.concatenate(ds, 0)).T
        dv = dot_tn(jnp.concatenate([gm * masks[0], gm * masks[1]], 0), jnp.concatenate(probs, 0)).T
        dq, dk, dv = (dq * 0.125).astype(BF16), dk[:rows].astype(BF16), dv[:rows].astype(BF16)
        gp_ref[0, 0, :, lanes] = dq
        gp_ref[0, 1, :, lanes] = dk
        gp_ref[0, 2, :, lanes] = dv
        at = pl.multiple_of(group * GROUP + p * 128, 128)
        dvec_ref[2:3, pl.ds(at, 128)] = jnp.sum(dq.astype(F32), 0, keepdims=True)
        dvec_ref[3:4, pl.ds(at, 128)] = jnp.sum(dv.astype(F32), 0, keepdims=True)
    gn[...] += sum(dot_nt(gp_ref[0, j], w[...]) for j, w in enumerate((wq, wk, wv)))

    @pl.when(group == pl.num_programs(0) - 1)
    def _():
        grad = gn[...]
        xhat, rstd = normalise(x_ref[0].astype(F32))
        dvec_ref[0:1] = jnp.sum(grad * xhat, 0, keepdims=True)
        dvec_ref[1:2] = jnp.sum(grad, 0, keepdims=True)
        res[0:rows] = ga_ref[0].astype(F32) + norm_backward(grad, row_of(n1g), xhat, rstd)
        repack(lay, res, 0, Image(lay, (rank_ref, split_ref, tag_ref), k), back)
        for j, ig_ref in enumerate(ig_refs):
            ig_ref[0] = back[j]


def call_backward(lay, k, per, meta, ga, qkv, prob, x, n1g, out_weight, qkv_weight, chain):
    rows, keys = lay.rows, lay.keys
    width = out_weight.shape[0]
    groups = width // GROUP
    alone = k == per - 1
    one = pl.BlockSpec((1, rows, width), lambda g: (k, 0, 0))
    args = [*meta, ga, qkv, prob, x, n1g, out_weight, qkv_weight, qkv_weight, qkv_weight]
    specs = [
        SMEM,
        SMEM,
        SMEM,
        one,
        pl.BlockSpec((1, 3, keys, GROUP), lambda g: (k, 0, 0, g)),
        pl.BlockSpec((1, HEADS // groups, rows, keys), lambda g: (k, g, 0, 0)),
        one,
        whole(n1g.shape),
        pl.BlockSpec((GROUP, width), lambda g: (g, 0)),
    ] + [pl.BlockSpec((width, GROUP), functools.partial(lambda j, g: (0, j * groups + g), j)) for j in range(3)]
    aliases = {}
    if chain is not None:
        count = 1 if alone else len(chain)
        aliases = {len(args) + i: i for i in range(count)}
        args += chain[:count]
        specs += [HBM] * count
    return pl.pallas_call(
        functools.partial(attention_backward, lay, k, len(args) - 12),
        grid=(groups,),
        in_specs=specs,
        out_specs=[
            pl.BlockSpec((1, 3, rows, GROUP), lambda g: (k, 0, 0, g)),
            *[pl.BlockSpec((1, lay.piece, width), lambda g: (0 if alone else k, 0, 0))] * lay.ranks,
            whole((8, width)),
        ],
        out_shape=[
            shaped((per, 3, rows, width), BF16),
            *[shaped((1 if alone else per - 1, lay.piece, width), BF16)] * lay.ranks,
            shaped((8, width), F32),
        ],
        scratch_shapes=[
            pltpu.VMEM((rows, width), F32),
            pltpu.VMEM((rows + lay.spare, width), F32),
            pltpu.VMEM((lay.ranks, lay.piece, width), BF16),
        ],
        input_output_aliases=aliases,
        compiler_params=params(),
        cost_estimate=cost(10e9, 10e6),
    )(*args)


def assemble(lay, rank_ref, split_ref, tag_ref, *refs):
    *got, passed_ref, out_ref = refs
    images, slots, width = out_ref.shape
    row = lax.broadcasted_iota(jnp.int32, (slots, width), 0)
    rank = rank_ref[0]
    first = 0
    for b in range(0, len(got), lay.ranks):
        for j, piece in enumerate(got[b : b + lay.ranks]):
            for k in range(piece.shape[0]):
                owner = rank ^ j
                image = jnp.minimum(owner * lay.per, images - lay.per) + first + k
                live = jnp.where(tag_ref[image] < lay.groups, split_ref[image, rank] * GRID, 0)

                @pl.when(image >= owner * lay.per)
                def _():
                    worked = piece[k][:slots].astype(F32)
                    kept = passed_ref[image].astype(F32)
                    out_ref[image] = jnp.where(row < live, worked, kept).astype(BF16)

        first += got[b].shape[0]


def call_assemble(lay, meta, got, passed):
    args = [*meta, *got, passed]
    return pl.pallas_call(
        functools.partial(assemble, lay),
        in_specs=[SMEM] * 3 + [VMEM] * len(args[3:]),
        out_specs=VMEM,
        out_shape=shaped(passed.shape, BF16),
        compiler_params=params(SMALL_LIMIT),
        cost_estimate=cost(0, 5e6),
    )(*args)


class Part:
    def __init__(self, own, send, order, at=None):
        self.own, self.send, self.order = own, send, ["core", *order]
        self.got = self.sent = None
        self.at = at
        self.pending = None


def exchange(parts):
    for p in parts:
        if p.send is None:
            continue
        axis, weight = BITS[p.order[0]]
        size = lax.axis_size(axis)
        p.got = lax.ppermute(p.send, axis, [(i, i ^ weight) for i in range(size)])
        p.sent, p.send = p.send, None


def add_and_split(counts, mine_ref, *refs):
    n = len(counts)
    for i in range(n):
        own, got, keep, send = refs[2 * i], refs[2 * i + 1], refs[2 * n + 2 * i], refs[2 * n + 2 * i + 1]
        mine = mine_ref[i]
        keep[...] = (own[mine].astype(F32) + got[mine].astype(F32)).astype(BF16)
        send[...] = (own[1 - mine].astype(F32) + got[1 - mine].astype(F32)).astype(BF16)


def bit_of(name):
    axis, weight = BITS[name]
    return (lax.axis_index(axis) // weight) % 2


def add_sent(mine_ref, *refs):
    n = len(refs) // 3
    for i in range(n):
        refs[2 * n + i][...] = (refs[2 * i][...].astype(F32) + refs[2 * i + 1][...].astype(F32)).astype(BF16)


def send_first(parts, steps=2):
    args, ins, outs, shapes = [], [], [], []
    mine = jnp.stack([bit_of(p.order[1]) for p in parts])
    for i, p in enumerate(parts):
        n, width = p.own.shape[-2:]
        many = 2 ** (len(p.order) - 2)
        pair = [v.reshape(2, many, n, width) for v in (p.own, p.got)]
        args += pair
        place = functools.partial(lambda part, step, mine: (1 - mine[part], step, 0, 0), i)
        ins += [pl.BlockSpec((None, many // steps, n, width), place)] * 2
        outs.append(pl.BlockSpec((many // steps, n, width), lambda step, mine: (step, 0, 0)))
        shapes.append(shaped((many, n, width), BF16))
        p.pending = pair
    sends = pl.pallas_call(
        add_sent,
        grid_spec=pltpu.PrefetchScalarGridSpec(
            num_scalar_prefetch=1, grid=(steps,), in_specs=ins, out_specs=outs
        ),
        out_shape=shapes,
        compiler_params=params(),
        cost_estimate=cost(0, 10e6),
    )(mine, *args)
    for p, send in zip(parts, sends):
        p.order.pop(0)
        p.send = send.reshape(*[2] * (len(p.order) - 1), *send.shape[-2:])
        p.own = p.got = None


def add_three(n, bits_ref, *refs):
    for i in range(n):
        terms, keep, send = refs[3 * i : 3 * i + 3], refs[3 * n + 2 * i], refs[3 * n + 2 * i + 1]
        mine = bits_ref[n + i]
        keep[...] = sum(t[mine].astype(F32) for t in terms).astype(BF16)
        send[...] = sum(t[1 - mine].astype(F32) for t in terms).astype(BF16)


def combine_pending(parts, before, steps=2):
    tied, _ = lax.optimization_barrier(([(p.pending, p.got) for p in parts], before))
    bits = jnp.stack([bit_of(p.order[0]) for p in parts] + [bit_of(p.order[1]) for p in parts])
    args, ins, outs, shapes = [], [], [], []
    for i, (p, (pair, got)) in enumerate(zip(parts, tied)):
        n, width = pair[0].shape[-2:]
        many = pair[0].shape[1] // 2
        args += [v.reshape(2, 2, many, n, width) for v in pair] + [got.reshape(2, many, n, width)]
        place = functools.partial(lambda part, step, bits: (bits[part], 0, step, 0, 0), i)
        ins += [pl.BlockSpec((None, 2, many // steps, n, width), place)] * 2
        ins.append(pl.BlockSpec((2, many // steps, n, width), lambda step, bits: (0, step, 0, 0)))
        outs += [pl.BlockSpec((many // steps, n, width), lambda step, bits: (step, 0, 0))] * 2
        shapes += [shaped((many, n, width), BF16)] * 2
    res = pl.pallas_call(
        functools.partial(add_three, len(parts)),
        grid_spec=pltpu.PrefetchScalarGridSpec(
            num_scalar_prefetch=1, grid=(steps,), in_specs=ins, out_specs=outs
        ),
        out_shape=shapes,
        compiler_params=params(),
        cost_estimate=cost(0, 10e6),
    )(bits, *args)
    for i, p in enumerate(parts):
        p.order.pop(0)
        lead = [2] * (len(p.order) - 1)
        p.own, p.send = [v.reshape(*lead, *v.shape[-2:]) for v in res[2 * i : 2 * i + 2]]
        p.got = p.pending = None
    return res[0]


def combine(parts, before=()):
    parts = [p for p in parts if p.got is not None]
    if parts and parts[0].pending:
        return combine_pending(parts, before)
    last = [p for p in parts if len(p.order) == 1]
    for p in last:
        p.own = p.own.astype(F32) + p.got.astype(F32)
        p.got = p.send = None
        p.order = []
    parts = [p for p in parts if p.order]
    if not parts:
        return ()
    tied, _ = lax.optimization_barrier(([(p.own, p.got) for p in parts], before))
    for p, (p.own, p.got) in zip(parts, tied):
        pass
    views = []
    for p in parts:
        shape = p.own.shape
        flat = (2, 2 ** (len(p.order) - 2), *shape[-2:])
        if p.at is not None:
            flat = (shape[0], *flat)
        views.append((p.own.reshape(flat), p.got.reshape(flat)))
    size = sum(4 * v[0].size for v in views)
    steps = min(4 if size > 9e6 else 1, *(v[0].shape[-3] for v in views))
    ins, outs, shapes, args, mine = [], [], [], [], []
    for p, (own, got) in zip(parts, views):
        many, n, width = own.shape[-3:]
        block = (2, many // steps, n, width)
        if steps == 1:
            ins += [VMEM] * 2
            outs += [VMEM] * 2
            shapes += [shaped((many, n, width), BF16)] * 2
        elif p.at is None:
            ins += [pl.BlockSpec(block, lambda i: (0, i, 0, 0))] * 2
        else:
            ins += [pl.BlockSpec((None, *block), functools.partial(lambda a, i: (a, 0, i, 0, 0), p.at))] * 2
        if steps > 1:
            outs += [pl.BlockSpec(block[1:], lambda i: (i, 0, 0))] * 2
            shapes += [shaped((many, n, width), BF16)] * 2
        args += [own, got]
        axis, weight = BITS[p.order[1]]
        mine.append((lax.axis_index(axis) // weight) % 2)
    moved = sum(3 * a.size for a in args)
    res = pl.pallas_call(
        functools.partial(add_and_split, [None] * len(parts)),
        **({"grid": (steps,)} if steps > 1 else {}),
        in_specs=[SMEM] + ins,
        out_specs=outs,
        out_shape=shapes,
        compiler_params=params() if steps > 1 else params(SMALL_LIMIT),
        cost_estimate=cost(0, moved),
    )(jnp.stack(mine), *args)
    for i, p in enumerate(parts):
        shape = (*[2] * (len(p.order) - 2), *p.own.shape[-2:])
        p.at = None
        p.own, p.send = res[2 * i].reshape(shape), res[2 * i + 1].reshape(shape)
        p.got = None
        p.order.pop(0)
    return res[0]


def add_and_fan(heights, z_ref, *refs):
    ins, outs = refs[: 2 * len(heights)], refs[2 * len(heights) :]
    at = 0
    for i, n in enumerate(heights):
        own, got = ins[2 * i], ins[2 * i + 1]
        for j, out in enumerate(outs):
            place = (z_ref[0] % 2) ^ (j % 2), (z_ref[0] // 2) ^ (j // 2)
            total = own[place].astype(F32) + got[place].astype(F32)
            out[at : at + n, :] = total.astype(out.dtype)
        at += n


def fan(parts, before):
    tied, _ = lax.optimization_barrier(([(p.own, p.got) for p in parts], before))
    args = [a for pair in tied for a in pair]
    heights = [p.own.shape[2] for p in parts]
    width = args[0].shape[-1]
    z = lax.axis_index("dp") // 2
    shape = (sum(heights), width)
    own, *sends = pl.pallas_call(
        functools.partial(add_and_fan, heights),
        in_specs=[SMEM] + [VMEM] * len(args),
        out_specs=[VMEM] * 4,
        out_shape=[shaped(shape, F32)] + [shaped(shape, BF16)] * 3,
        compiler_params=params(SMALL_LIMIT),
        cost_estimate=cost(0, 1e6),
    )(z[None], *args)
    size = lax.axis_size("dp")
    got = [lax.ppermute(v, "dp", [(i, i ^ (2 * j)) for i in range(size)]) for j, v in zip((1, 2, 3), sends)]
    return own, sends, got


def wait(values, parts):
    live = [p for p in parts if p.got is not None]
    values, gots = lax.optimization_barrier((values, [p.got for p in live]))
    for p, g in zip(live, gots):
        p.got = g
    return values


def after(values, parts):
    return lax.optimization_barrier((values, [p.sent for p in parts if p.sent is not None]))[0]


def small_sum(value, n_dp, n_seq):
    for axis, size in (("seq", n_seq), ("dp", n_dp)):
        dim = 1 if axis == "seq" else 0
        weight = 1
        place = lax.axis_index(axis)
        while weight < size:
            shape = value.shape
            cut = value.reshape(*shape[:dim], shape[dim] // 2, 2, *shape[dim + 1 :])
            mine = (place // weight) % 2
            other = lax.dynamic_index_in_dim(cut, 1 - mine, dim + 1, keepdims=False)
            own = lax.dynamic_index_in_dim(cut, mine, dim + 1, keepdims=False)
            value = own + lax.ppermute(other, axis, [(i, i ^ weight) for i in range(size)])
            weight *= 2
    return value.reshape(-1)


def per_device(
    tokens,
    key_mask,
    row_split,
    group_tags,
    norm1_gain,
    norm1_shift,
    qkv_weight,
    query_bias,
    value_bias,
    out_weight,
    out_bias,
    norm2_gain,
    norm2_shift,
    fc1_weight,
    fc1_bias,
    fc2_weight,
    fc2_bias,
    out_cotangent,
):
    images, slots, width = tokens.shape
    n_seq = lax.axis_size("seq")
    n_dp = lax.axis_size("dp")
    devices = n_dp * n_seq
    rank = lax.axis_index("seq")
    lay = Rows(n_seq, slots, images, n_dp)
    per, rows = lay.per, lay.rows
    meta = rank[None], row_split, group_tags
    all_rows = per * rows
    fast = (n_dp, n_seq) == (8, 4)

    def swap(value, j):
        return lax.ppermute(value, "seq", [(i, i ^ j) for i in range(n_seq)])

    def cut_for(array, k, count):
        starts = [jnp.minimum((rank ^ j) * per, images - per) + k for j in range(n_seq)]
        return [lax.dynamic_slice_in_dim(array, at, count, 0) for at in starts]

    def bring(mine):
        return [mine[0]] + [swap(mine[j], j) for j in range(1, n_seq)]

    vecs = (norm1_gain, norm1_shift, out_bias, norm2_gain, norm2_shift, query_bias, value_bias)

    first, rest = cut_for(tokens, 0, 1), cut_for(tokens, 1, per - 1)
    cot = cut_for(out_cotangent, 0, per)
    first = bring(first)
    first, rest = lax.optimization_barrier((first, rest))
    chain = call_forward(lay, 0, 1, meta, first, key_mask, vecs, qkv_weight, out_weight, None)
    rest = bring(rest)
    chain, rest, cot = lax.optimization_barrier((chain, rest, cot))
    chain = call_forward(lay, 1, per - 1, meta, rest, key_mask, vecs, qkv_weight, out_weight, chain)
    hidden, x_all, normed_all, mixed_all, n2, qkv, prob = chain
    n2 = n2.reshape(all_rows, width)

    cot = bring(cot)
    res = call_feed(
        lay,
        per,
        fast,
        meta,
        hidden,
        cot,
        n2,
        fc1_weight,
        fc1_bias.astype(F32)[None],
        fc2_weight,
        norm2_gain,
        fc2_bias,
        mixed_all.reshape(all_rows, width),
    )
    out_pieces, (ga, db1, dvec2, *dw) = list(res[:n_seq]), res[n_seq:]

    fc = late = []
    if fast:
        fc = [Part(*dw[:2], FC1_ORDER), Part(*dw[2:], FC2_ORDER)]
    out_got = [swap(out_pieces[j], j) for j in range(2, n_seq)]
    exchange(fc)
    ga = ga.reshape(per, rows, width)

    chain = None
    dvecs, ig, ig_got = [], [], []
    for k in range(per):
        *chain, dvec = call_backward(
            lay, k, per, meta, ga, qkv, prob, x_all, norm1_gain, out_weight, qkv_weight, chain
        )
        dvecs.append(dvec)
        if k == 0:
            chain, out_got[0] = lax.optimization_barrier((chain, out_got[0]))
        if k == 1:
            chain, out_got, out_pieces = lax.optimization_barrier((chain, out_got, out_pieces))
            out_got = [out_pieces[0], swap(out_pieces[1], 1), *out_got]
        if k == 2:
            chain, ig_got[0] = lax.optimization_barrier((chain, ig_got[0]))
        if k >= per - 2:
            ig.append(chain[1:3])
            ig_got.append([swap(chain[1 + j], j) for j in range(2, n_seq)])
        if k != 1:
            chain = wait(chain, fc)
            if fast and k == 0:
                send_first(fc)
            else:
                combine(fc)
            exchange(fc)
            ga, chain = after((ga, chain), fc)
    gp = chain[0]
    dwl = call_late_sums(fast, meta[0], gp, normed_all.reshape(all_rows, width), dvec2, db1, dvecs)
    if fast:
        dwl, ig_got[1] = wait((dwl, ig_got[1]), fc)
        late = [Part(dwl[i], dwl[2 + i], order) for i, order in enumerate(LATE_ORDERS)]
        exchange(late)
        token = combine(fc, dwl)
        exchange(fc)
        token = combine(late, token)
        exchange(late)
        out_got, ig, _ = lax.optimization_barrier((out_got, ig, token))
    output = call_assemble(lay, meta, out_got, tokens)
    if fast:
        token = combine(late, output)
        exchange(late)
        token = combine(fc, token)
        exchange(fc)
        ig = after(ig, late)
    ig_got = [g for near, far in zip(ig, ig_got) for g in (near[0], swap(near[1], 1), *far)]
    if fast:
        own, sends, got = fan(late, token)
        ig_got, _ = lax.optimization_barrier((ig_got, sends))
    input_grad = call_assemble(lay, meta, ig_got, out_cotangent)
    if fast:
        input_grad, fc[0].got, fc[1].got = lax.optimization_barrier((input_grad, fc[0].got, fc[1].got))
        combine(fc)
        inner = fc1_weight.shape[1]
        done = fc[0].own.T, fc[1].own[:, :inner].T, fc[1].own[:, inner:].T
        done, got = lax.optimization_barrier((done, got))
        late_sum = own + sum(g.astype(F32) for g in got)

    part = width // devices
    inner = fc1_weight.shape[1]
    if fast:
        qkv_sum, small = late_sum[: 3 * part], late_sum[3 * part]
        small_late, small_early = small[: 4 * part], small[4 * part :]
    else:
        *done, qkv_sum = [
            lax.psum_scatter(v.astype(F32), ("dp", "seq"), scatter_dimension=0, tiled=True)
            for v in (dw[0], dw[1][:, :inner], dw[1][:, inner:], dwl[0])
        ]
        done = [v.T for v in done]
        dvec1 = sum(dvecs)

        def by_device(v):
            return v.reshape(n_dp, n_seq, v.shape[0] // devices)

        early = (dvec2[2], dvec2[0], dvec2[1], dvec2[3], db1[0])
        small_early = small_sum(jnp.concatenate([by_device(v) for v in early], -1), n_dp, n_seq)
        small_late = small_sum(jnp.concatenate([by_device(dvec1[i]) for i in range(4)], -1), n_dp, n_seq)
    vec = [small_late[i * part : (i + 1) * part] for i in range(4)]
    vec += [small_early[i * part : (i + 1) * part] for i in range(4)]
    vec.append(small_early[4 * part : 4 * part + fc1_bias.shape[0] // devices])
    return (
        output,
        input_grad,
        vec[0],
        vec[1],
        qkv_sum.T,
        vec[2],
        vec[3],
        done[2],
        vec[4],
        vec[5],
        vec[6],
        done[0],
        vec[8],
        done[1],
        vec[7],
    )


def solution(mesh):
    rows = P("dp", "seq", None)
    split = P(("dp", "seq"))
    columns = P(None, ("dp", "seq"))
    return jax.shard_map(
        per_device,
        mesh=mesh,
        in_specs=(rows, P("dp", None), P("dp", None), P("dp")) + (P(),) * 13 + (rows,),
        out_specs=(
            rows,
            rows,
            split,
            split,
            columns,
            split,
            split,
            columns,
            split,
            split,
            split,
            columns,
            split,
            columns,
            split,
        ),
        check_vma=False,
    )
```

```python
import functools

import jax
import jax.numpy as jnp
from jax import lax
from jax.experimental import pallas as pl
from jax.experimental.pallas import tpu as pltpu
from jax.sharding import PartitionSpec as P

HEADS = 12
GRID = 18
EPS = 1e-06
NEG = -1e30
F32 = jnp.float32
BF16 = jnp.bfloat16
VMEM_LIMIT = 60 * 1024 * 1024
CHUNK = 768
GROUP = 384
LANES = 384

BITS = {"core": ("seq", 1), "y": ("seq", 2), "x": ("dp", 1), "z0": ("dp", 2), "z1": ("dp", 4)}
FC1_ORDER = ("x", "z0", "z1", "y")
FC2_ORDER = ("z0", "x", "y", "z1")
LATE_ORDERS = (("x", "y", "z0", "z1"), ("y", "x", "z0", "z1"))
LATE_CUT = 48
SMEM = pl.BlockSpec(memory_space=pltpu.SMEM)
VMEM = pl.BlockSpec(memory_space=pltpu.VMEM)
SMALL_LIMIT = 8 * 1024 * 1024
HBM = pl.BlockSpec(memory_space=pl.ANY)


def round_up(n, to):
    return -(-n // to) * to


class Rows:
    def __init__(self, ranks, slots, images, groups):
        self.images, self.groups = images, groups
        self.per = -(-images // ranks)
        base, extra = GRID // ranks, GRID % ranks
        self.lens = [min(slots, (base + 1) * GRID)] * extra + [base * GRID] * (ranks - extra)
        self.extra = extra
        self.ranks = ranks
        self.slots = slots
        self.offs = []
        at = 0
        for n in self.lens:
            self.offs.append(at)
            at += round_up(n, 8)
        self.rows = round_up(at, 16)
        self.keys = round_up(self.rows, 128)
        self.piece = round_up(slots, 16)
        end = max(o + round_up(n, 16) for o, n in zip(self.offs, self.lens))
        self.spare = max(round_up(end, 8) - self.rows, 0)

    def is_row(self, index):
        hit = None
        for off, n in zip(self.offs, self.lens):
            one = (index >= off) & (index < off + n)
            hit = one if hit is None else hit | one
        return hit


def dot(a, b):
    return lax.dot_general(a, b, (((1,), (0,)), ((), ())), preferred_element_type=F32)


def dot_nt(a, b):
    return lax.dot_general(a, b, (((1,), (1,)), ((), ())), preferred_element_type=F32)


def dot_tn(a, b):
    return lax.dot_general(a, b, (((0,), (0,)), ((), ())), preferred_element_type=F32)


def params(limit=VMEM_LIMIT):
    return pltpu.CompilerParams(vmem_limit_bytes=limit)


def cost(flops, moved, exps=0):
    return pl.CostEstimate(flops=int(flops) // 16, bytes_accessed=int(moved) // 16, transcendentals=int(exps) // 16)


def whole(shape):
    return pl.BlockSpec(shape, lambda *i: (0,) * len(shape))


def shaped(shape, dtype):
    return jax.ShapeDtypeStruct(shape, dtype)


class Image:
    def __init__(self, lay, meta, k):
        rank_ref, split_ref, tag_ref = meta
        rank = rank_ref[0]
        self.index = jnp.minimum(rank * lay.per, lay.images - lay.per) + k
        base = GRID // lay.ranks
        longs, shorts = jnp.int32(0), jnp.int32(lay.extra)
        self.sources = [jnp.int32(0)] * lay.ranks
        for r in range(lay.ranks):
            is_long = split_ref[self.index, r] > base
            place = jnp.where(is_long, longs, shorts)
            longs = longs + jnp.where(is_long, 1, 0)
            shorts = shorts + jnp.where(is_long, 0, 1)
            self.sources = [jnp.where(place == i, r, s) for i, s in enumerate(self.sources)]
        self.pieces = [s ^ rank for s in self.sources]
        self.counts = jnp.where((tag_ref[self.index] < lay.groups) & (self.index >= rank * lay.per), 1, 0)


def unpack(lay, stage, image, to_ref):
    width = to_ref.shape[1]
    for i, (off, n) in enumerate(zip(lay.offs, lay.lens)):
        full = round_up(n, 8)
        if full > n:
            to_ref[off + full - 8 : off + full, :] = jnp.zeros((8, width), F32)
        piece = stage[image.pieces[i]].astype(F32)
        to_ref[off : off + n, :] = piece[:n]
    last = lay.offs[-1] + round_up(lay.lens[-1], 8)
    if lay.rows > last:
        to_ref[last : lay.rows, :] = jnp.zeros((lay.rows - last, width), F32)


def repack(lay, from_ref, start, image, stage):
    for i, (off, n) in enumerate(zip(lay.offs, lay.lens)):
        full = round_up(n, 16)
        stage[image.pieces[i], 0:full, :] = from_ref[start + off : start + off + full, :].astype(BF16)


def mask_of(lay, image, key_ref):
    slots = key_ref.shape[1]
    row = jnp.broadcast_to(key_ref[pl.ds(image.index, 1), :], (8, slots)).astype(F32)
    lane = lax.broadcasted_iota(jnp.int32, (slots, lay.keys), 1)
    want = jnp.full((slots, lay.keys), -1, jnp.int32)
    for i, (off, n) in enumerate(zip(lay.offs, lay.lens)):
        want = jnp.where((lane >= off) & (lane < off + n), lane + (image.sources[i] * lay.slots - off), want)
    pick = (lax.broadcasted_iota(jnp.int32, (slots, lay.keys), 0) == want).astype(F32).astype(BF16)
    valid = jnp.where(row > 0, 1.0, 0.0).astype(BF16)
    return jnp.where(dot(valid, pick)[0:1] > 0.5, 0.0, NEG)


def row_of(ref):
    return ref[...].astype(F32).reshape(1, -1)


def live_column(lay, image):
    index = lax.broadcasted_iota(jnp.int32, (lay.rows, 1), 0)
    return jnp.where(lay.is_row(index), image.counts, 0).astype(F32)


def normalise(x):
    mean = jnp.mean(x, -1, keepdims=True)
    centered = x - mean
    rstd = lax.rsqrt(jnp.mean(centered * centered, -1, keepdims=True) + EPS)
    return centered * rstd, rstd


def norm_backward(grad, gain, xhat, rstd):
    scaled = grad * gain
    row = scaled - jnp.mean(scaled, -1, keepdims=True)
    return rstd * (row - xhat * jnp.mean(scaled * xhat, -1, keepdims=True))


def half_masks():
    lane = lax.broadcasted_iota(jnp.int32, (1, 128), 1)
    return [(lane < 64).astype(BF16), (lane >= 64).astype(BF16)]


def keep_and_send(core, even, odd):
    mine = core == 0
    return jnp.where(mine, even, odd).astype(BF16), jnp.where(mine, odd, even).astype(BF16)


def parts_of(rows, each):
    n = rows.shape[1]
    place = lax.broadcasted_iota(jnp.int32, rows.shape, 0) % (n // each) * each
    lane = lax.broadcasted_iota(jnp.int32, rows.shape, 1)
    return jnp.where((lane >= place) & (lane < place + each), rows, 0.0).astype(BF16)


def picker(n, each):
    source = lax.broadcasted_iota(jnp.int32, (n, 128), 0)
    part = ((source.astype(F32) + 0.5) * (1.0 / each)).astype(jnp.int32)
    target = lax.broadcasted_iota(jnp.int32, (n, 128), 1)
    return (source - part * each == target).astype(F32).astype(BF16)


def spread(vectors, long):
    n, m = vectors[0].shape[1], long.shape[1]
    each, long_each = n // 32, m // 32
    rows = [parts_of(jnp.broadcast_to(v, (32, n)), each) for v in vectors]
    found = dot(jnp.concatenate(rows, 0), picker(n, each))
    many = m // n
    group = lax.broadcasted_iota(jnp.int32, (32, n), 0) // (32 // many)
    chosen = sum(jnp.where(group == i, long[:, i * n : (i + 1) * n], 0.0) for i in range(many))
    last = dot(parts_of(chosen, long_each), picker(n, long_each))
    blank = jnp.zeros((32, LANES - 128), F32)
    total = pltpu.roll(jnp.concatenate([last, blank], 1), each * len(vectors), 1)
    for i in range(len(vectors)):
        one = jnp.concatenate([found[i * 32 : (i + 1) * 32], blank], 1)
        total = total + (pltpu.roll(one, each * i, 1) if i else one)
    return total


def with_vectors(rows, packed, d, width):
    lanes = packed.shape[1]
    vec = jnp.broadcast_to(packed[d : d + 1, :], (8, lanes))
    return jnp.concatenate([rows, jnp.concatenate([vec, jnp.zeros((8, width - lanes), F32)], 1)], 0)


def place_of(order, dp, y):
    bits = {"x": dp % 2, "z0": dp // 2 % 2, "z1": dp // 4, "y": y}
    return tuple(bits[name] for name in order)


def attention_forward(
    lay, first, linked, rank_ref, split_ref, tag_ref, p0, p1, p2, p3, key_ref, n1g, n1s, ob, n2g, n2s, qb, vb, wq, wk, wv, wo, *refs
):
    outs = refs[7:] if linked else refs
    hid_ref, x_ref, normed_ref, mixed_ref, n2_ref, qkv_ref, prob_ref, stage, xs, bias, mask = outs
    rows, keys = lay.rows, lay.keys
    group = pl.program_id(1)
    image = Image(lay, (rank_ref, split_ref, tag_ref), first + pl.program_id(0))

    @pl.when(group == 0)
    def _():
        for j, piece in enumerate((p0, p1, p2, p3)):
            stage[j] = piece[0]
        unpack(lay, stage, image, xs)
        mask[...] = jnp.broadcast_to(mask_of(lay, image, key_ref), mask.shape)
        bias[0:1, :] = row_of(qb)
        bias[1:2, :] = jnp.zeros((1, bias.shape[1]), F32)
        bias[2:3, :] = row_of(vb)
        x = xs[...]
        x_ref[0] = x.astype(BF16)
        xhat, _ = normalise(x)
        normed_ref[0] = (xhat * row_of(n1g) + row_of(n1s)).astype(BF16)

    normed = normed_ref[0]
    qkv = []
    for j, weight in enumerate((wq, wk, wv)):
        part = dot(normed, weight[...]) + bias[j : j + 1, pl.ds(pl.multiple_of(group * GROUP, GROUP), GROUP)]
        if j == 0:
            part = part * 0.125
        part = part.astype(BF16)
        if j and keys > rows:
            part = jnp.concatenate([part, jnp.zeros((keys - rows, GROUP), BF16)], 0)
        qkv_ref[0, j, 0 : part.shape[0], :] = part
    if keys > rows:
        qkv_ref[0, 0, rows:keys, :] = jnp.zeros((keys - rows, GROUP), BF16)
    masks = half_masks()
    for p in range(GROUP // 128):
        lanes = slice(p * 128, (p + 1) * 128)
        q = qkv_ref[0, 0, 0:rows, lanes]
        k = qkv_ref[0, 1, :, lanes]
        v = qkv_ref[0, 2, :, lanes]
        both = dot_nt(q, jnp.concatenate([k * masks[0], k * masks[1]], 0))
        probs = []
        for h in (0, 1):
            s = both[:, h * keys : (h + 1) * keys] + mask[0:1, :]
            e = jnp.exp(s - jnp.max(s, -1, keepdims=True))
            prob = (e * (1.0 / jnp.sum(e, -1, keepdims=True))).astype(BF16)
            prob_ref[0, 2 * p + h] = prob
            probs.append(prob)
        total = dot(jnp.concatenate(probs, 1), jnp.concatenate([v * masks[0], v * masks[1]], 0))
        at = pl.multiple_of(group * GROUP + p * 128, 128)
        mixed_ref[0, :, pl.ds(at, 128)] = total.astype(BF16)

    @pl.when(group == pl.num_programs(1) - 1)
    def _():
        attended = dot(mixed_ref[0], wo[...]) + row_of(ob)
        hidden = xs[...] + live_column(lay, image) * attended
        hid_ref[0] = hidden
        xhat, _ = normalise(hidden)
        n2_ref[0] = (xhat * row_of(n2g) + row_of(n2s)).astype(BF16)


def call_forward(lay, first, count, meta, pieces, key_mask, vecs, qkv_weight, out_weight, chain):
    per, rows, keys = lay.per, lay.rows, lay.keys
    width = out_weight.shape[0]
    groups = width // GROUP
    shapes = [
        shaped((per, rows, width), F32),
        shaped((per, rows, width), BF16),
        shaped((per, rows, width), BF16),
        shaped((per, rows, width), BF16),
        shaped((per, rows, width), BF16),
        shaped((per, 3, keys, width), BF16),
        shaped((per, HEADS, rows, keys), BF16),
    ]
    args = [*meta, *pieces, key_mask, *vecs, qkv_weight, qkv_weight, qkv_weight, out_weight]
    specs = (
        [SMEM] * 3
        + [pl.BlockSpec((1, lay.slots, width), lambda i, g: (i, 0, 0))] * len(pieces)
        + [whole(v.shape) for v in (key_mask, *vecs)]
        + [pl.BlockSpec((width, GROUP), functools.partial(lambda j, i, g: (0, j * groups + g), j)) for j in range(3)]
        + [whole(out_weight.shape)]
    )
    aliases = {}
    if chain is not None:
        aliases = {len(args) + i: i for i in range(7)}
        args += chain
        specs += [HBM] * 7
    return list(
        pl.pallas_call(
            functools.partial(attention_forward, lay, first, chain is not None),
            grid=(count, groups),
            in_specs=specs,
            out_specs=[pl.BlockSpec((1, rows, width), lambda i, g: (first + i, 0, 0))] * 5
            + [
                pl.BlockSpec((1, 3, keys, GROUP), lambda i, g: (first + i, 0, 0, g)),
                pl.BlockSpec((1, HEADS // groups, rows, keys), lambda i, g: (first + i, g, 0, 0)),
            ],
            out_shape=shapes,
            scratch_shapes=[
                pltpu.VMEM((lay.ranks, lay.slots, width), BF16),
                pltpu.VMEM((rows, width), F32),
                pltpu.VMEM((8, width), F32),
                pltpu.VMEM((8, keys), F32),
            ],
            input_output_aliases=aliases,
            compiler_params=params(),
            cost_estimate=cost(8e9 * count, 12e6 * count, HEADS * rows * keys * count),
        )(*args)
    )


def feed_forward(
    lay, per, fast, rank_ref, split_ref, tag_ref, hid_hbm, c0, c1, c2, c3, n2_ref, w1_ref, b1_ref, w2_ref, n2g, b2_ref, mixed_hbm, *refs
):
    out_refs = refs[: lay.ranks]
    ga_ref, db1_ref, dvec_ref, *dw = refs[lay.ranks : -13]
    stage, back, cot, gr, grt, red, gn, act, gexp, hid, mixed, sem, sem2 = refs[-13:]
    step = pl.program_id(0)
    last = pl.num_programs(0) - 1
    rows = lay.rows
    meta = rank_ref, split_ref, tag_ref
    fetch = pltpu.make_async_copy(hid_hbm, hid, sem)
    fetch2 = pltpu.make_async_copy(mixed_hbm, mixed, sem2)

    @pl.when(step == 0)
    def _():
        fetch.start()
        fetch2.start()
        total = None
        for k in range(per):
            block = slice(k * rows, (k + 1) * rows)
            for j, piece in enumerate((c0, c1, c2, c3)):
                stage[j] = piece[k]
            image = Image(lay, meta, k)
            unpack(lay, stage, image, cot)
            wide = live_column(lay, image) * cot[...]
            gr[block, :] = wide.astype(BF16)
            grt[:, block] = wide.T.astype(BF16)
            total = jnp.sum(wide, 0, keepdims=True) + (0.0 if total is None else total)
        dvec_ref[...] = jnp.zeros_like(dvec_ref)
        dvec_ref[3:4] = total
        red[...] = jnp.zeros_like(red)
        gn[...] = jnp.zeros_like(gn)

    def share_fc2(sums):
        own2, send2 = dw[-2:]
        n = sums.shape[0] // 32
        for dp in range(8):
            for y in range(2):
                at = (dp * 4 + y * 2) * n
                place = place_of(FC2_ORDER, dp, y)
                own2[place], send2[place] = keep_and_send(
                    rank_ref[0] % 2, sums[at : at + n], sums[at + n : at + 2 * n]
                )

    @pl.when(step < last)
    def _():
        total = None
        for k in range(per):
            block = slice(k * rows, (k + 1) * rows)
            grads = []
            for c in range(0, CHUNK, 256):
                lanes = slice(c, c + 256)
                expanded = dot(n2_ref[block, :], w1_ref[:, lanes]) + b1_ref[:, lanes]
                grad_active = dot_nt(gr[block, :], w2_ref[lanes, :])
                cdf = 0.5 * (1.0 + lax.erf(expanded * 0.7071067811865476))
                slope = cdf + expanded * (jnp.exp(-0.5 * expanded * expanded) * 0.3989422804014327)
                act[block, lanes] = (expanded * cdf).astype(BF16)
                grad_exp = (grad_active * slope).astype(BF16)
                gexp[block, lanes] = grad_exp
                grads.append(jnp.sum(grad_exp.astype(F32), 0, keepdims=True))
            grads = jnp.concatenate(grads, 1)
            total = grads + (0.0 if total is None else total)
            red[block, :] += dot(act[block, :], w2_ref[...])
            gn[block, :] += dot_nt(gexp[block, :], w1_ref[...])
        db1_ref[...] = total
        sums1 = dot_tn(gexp[...], n2_ref[...])
        sums2 = dot(grt[...], act[...])
        if fast:
            own1, send1 = dw[:2]
            n = CHUNK // 8
            for i in range(2):
                for y in range(2):
                    at = (i * 4 + y * 2) * n
                    place = place_of(FC1_ORDER, i, y)
                    own1[place], send1[place] = keep_and_send(
                        rank_ref[0] % 2, sums1[at : at + n], sums1[at + n : at + 2 * n]
                    )
            share_fc2(sums2)
        else:
            dw[0][...] = sums1.astype(BF16)
            dw[1][...] = sums2.astype(BF16)

    @pl.when(step == last)
    def _():
        fetch.wait()
        fetch2.wait()
        for k in range(per):
            block = slice(k * rows, (k + 1) * rows)
            live = live_column(lay, Image(lay, meta, k))
            hidden = hid[k]
            red[block, :] = hidden + live * (red[block, :] + row_of(b2_ref))
            xhat, rstd = normalise(hidden)
            grad = gn[block, :]
            dvec_ref[0:1] += jnp.sum(grad * xhat, 0, keepdims=True)
            dvec_ref[1:2] += jnp.sum(grad, 0, keepdims=True)
            row = norm_backward(grad, row_of(n2g), xhat, rstd)
            attended = (live * (gr[block, :].astype(F32) + row)).astype(BF16)
            ga_ref[block, :] = attended
            dvec_ref[2:3] += jnp.sum(attended.astype(F32), 0, keepdims=True)
        for k in range(per):
            repack(lay, red, k * rows, Image(lay, meta, k), back)
            for j, out_ref in enumerate(out_refs):
                out_ref[k] = back[j]
        sums = dot_tn(ga_ref[...], mixed[...])
        if fast:
            share_fc2(sums)
        else:
            dw[1][...] = sums.astype(BF16)


def call_feed(lay, per, fast, meta, hidden, cot, n2, w1, b1, w2, n2g, b2, mixed):
    width, inner = w1.shape
    rows = per * lay.rows
    steps = inner // CHUNK

    def hold(i):
        return jnp.minimum(i, steps - 1)

    shapes = [shaped((per, lay.piece, width), BF16)] * lay.ranks + [
        shaped((rows, width), BF16),
        shaped((1, inner), F32),
        shaped((8, width), F32),
    ]
    specs = [whole((per, lay.piece, width))] * lay.ranks + [
        whole((rows, width)),
        pl.BlockSpec((1, CHUNK), lambda i: (0, hold(i))),
        whole((8, width)),
    ]
    if fast:
        def where(i):
            i = hold(i)
            at = {"x": 0, "y": 0, "z0": i % 2, "z1": i // 2}
            return tuple(at[name] for name in FC1_ORDER) + (0, 0)

        block = tuple(2 if name in ("x", "y") else 1 for name in FC1_ORDER) + (inner // 32, width)
        shapes += [shaped((2, 2, 2, 2, inner // 32, width), BF16)] * 2
        specs += [pl.BlockSpec(block, where)] * 2
        n = width // 32
        shapes += [shaped((2, 2, 2, 2, n, inner + width), BF16)] * 2
        specs += [pl.BlockSpec((2, 2, 2, 2, n, CHUNK), lambda i: (0, 0, 0, 0, 0, i))] * 2
    else:
        shapes += [shaped((inner, width), BF16), shaped((width, inner + width), BF16)]
        specs += [pl.BlockSpec((CHUNK, width), lambda i: (hold(i), 0)), pl.BlockSpec((width, CHUNK), lambda i: (0, i))]
    once = pl.Buffered(1)
    return pl.pallas_call(
        functools.partial(feed_forward, lay, per, fast),
        grid=(steps + 1,),
        in_specs=[
            SMEM,
            SMEM,
            SMEM,
            HBM,
            *[pl.BlockSpec(c.shape, lambda i: (0, 0, 0), pipeline_mode=once) for c in cot],
            pl.BlockSpec(n2.shape, lambda i: (0, 0), pipeline_mode=once),
            pl.BlockSpec((width, CHUNK), lambda i: (0, hold(i))),
            pl.BlockSpec((1, CHUNK), lambda i: (0, hold(i))),
            pl.BlockSpec((CHUNK, width), lambda i: (hold(i), 0)),
            whole(n2g.shape),
            whole(b2.shape),
            HBM,
        ],
        out_specs=specs,
        out_shape=shapes,
        scratch_shapes=[
            pltpu.VMEM((lay.ranks, lay.slots, width), BF16),
            pltpu.VMEM((lay.ranks, lay.piece, width), BF16),
            pltpu.VMEM((lay.rows, width), F32),
            pltpu.VMEM((rows, width), BF16),
            pltpu.VMEM((width, rows), BF16),
            pltpu.VMEM((rows + lay.spare, width), F32),
            pltpu.VMEM((rows, width), F32),
            pltpu.VMEM((rows, CHUNK), BF16),
            pltpu.VMEM((rows, CHUNK), BF16),
            pltpu.VMEM((per, lay.rows, width), F32),
            pltpu.VMEM((rows, width), BF16),
            pltpu.SemaphoreType.DMA,
            pltpu.SemaphoreType.DMA,
        ],
        compiler_params=params(),
        cost_estimate=cost(12 * rows * width * inner, 30e6, 2 * rows * inner),
    )(*meta, hidden, *cot, n2, w1, b1, w2, n2g, b2, mixed)


def late_sums(per, fast, rank_ref, gp_ref, normed_ref, dvec_ref, db1_ref, *refs):
    _, _, rows, width = gp_ref.shape
    dvecs = refs[:per]
    step = pl.program_id(0)
    sums = dot_tn(gp_ref[...].reshape(per * rows, width), normed_ref[...])
    if not fast:
        refs[per][...] = sums.astype(BF16)
        return
    own_refs, send_refs, held = refs[per : per + 2], refs[per + 2 : per + 4], refs[-1]
    held[pl.ds(pl.multiple_of(step * width, width), width), :] = sums

    @pl.when(step == pl.num_programs(0) - 1)
    def _():
        vec = dvecs[0][...]
        for more in dvecs[1:]:
            vec = vec + more[...]
        parts = [vec[i : i + 1] for i in range(4)]
        parts += [dvec_ref[2:3], dvec_ref[0:1], dvec_ref[1:2], dvec_ref[3:4]]
        packed = spread(parts, db1_ref[...])
        each = 3 * width // 32
        for dp in range(8):
            for y in range(2):
                d = dp * 4 + y * 2
                first = [held[e * each : e * each + LATE_CUT, :] for e in (d, d + 1)]
                second = [
                    with_vectors(held[e * each + LATE_CUT : (e + 1) * each, :], packed, e, width)
                    for e in (d, d + 1)
                ]
                for i, pair in enumerate((first, second)):
                    place = place_of(LATE_ORDERS[i], dp, y)
                    own_refs[i][place], send_refs[i][place] = keep_and_send(rank_ref[0] % 2, *pair)


def call_late_sums(fast, rank, gp, normed, dvec, db1, dvecs):
    per, _, rows, width = gp.shape
    if fast:
        heights = (LATE_CUT, 3 * width // 32 - LATE_CUT + 8)
        shapes = [shaped((2, 2, 2, 2, n, width), BF16) for n in heights] * 2
        specs = [whole(s.shape) for s in shapes]
        scratch = [pltpu.VMEM((3 * width, width), F32)]
    else:
        shapes = [shaped((3 * width, width), BF16)]
        specs = [pl.BlockSpec((width, width), lambda i: (i, 0))]
        scratch = []
    return pl.pallas_call(
        functools.partial(late_sums, per, fast),
        grid=(3,),
        in_specs=[SMEM, pl.BlockSpec((per, 1, rows, width), lambda i: (0, i, 0, 0)), whole(normed.shape)]
        + [whole(dvec.shape), whole(db1.shape)]
        + [whole(d.shape) for d in dvecs],
        out_specs=specs,
        out_shape=shapes,
        scratch_shapes=scratch,
        compiler_params=params(),
        cost_estimate=cost(6 * per * rows * width * width, 10e6),
    )(rank, gp, normed, dvec, db1, *dvecs)


def attention_backward(
    lay, k, linked, rank_ref, split_ref, tag_ref, ga_ref, qkv_ref, prob_ref, x_ref, n1g, wo_ref, wq, wk, wv, *refs
):
    gp_ref, *ig_refs, dvec_ref, gn, res, back = refs[linked:]
    rows = lay.rows
    group = pl.program_id(0)
    grad_mixed = dot_nt(ga_ref[0], wo_ref[...]).astype(BF16)
    masks = half_masks()

    @pl.when(group == 0)
    def _():
        dvec_ref[...] = jnp.zeros_like(dvec_ref)
        gn[...] = jnp.zeros_like(gn)

    for p in range(GROUP // 128):
        lanes = slice(p * 128, (p + 1) * 128)
        q = qkv_ref[0, 0, 0:rows, lanes]
        key = qkv_ref[0, 1, :, lanes]
        v = qkv_ref[0, 2, :, lanes]
        gm = grad_mixed[:, lanes]
        both = dot_nt(gm, jnp.concatenate([v * masks[0], v * masks[1]], 0))
        ds, probs = [], []
        for h in (0, 1):
            prob = prob_ref[0, 2 * p + h]
            weights = prob.astype(F32)
            gw = both[:, h * lay.keys : (h + 1) * lay.keys]
            delta = jnp.sum(weights * gw, -1, keepdims=True)
            ds.append((weights * (gw - delta)).astype(BF16))
            probs.append(prob)
        dq = dot(jnp.concatenate(ds, 1), jnp.concatenate([key * masks[0], key * masks[1]], 0))
        dk = dot_tn(jnp.concatenate([q * masks[0], q * masks[1]], 0), jnp.concatenate(ds, 0)).T
        dv = dot_tn(jnp.concatenate([gm * masks[0], gm * masks[1]], 0), jnp.concatenate(probs, 0)).T
        dq, dk, dv = (dq * 0.125).astype(BF16), dk[:rows].astype(BF16), dv[:rows].astype(BF16)
        gp_ref[0, 0, :, lanes] = dq
        gp_ref[0, 1, :, lanes] = dk
        gp_ref[0, 2, :, lanes] = dv
        at = pl.multiple_of(group * GROUP + p * 128, 128)
        dvec_ref[2:3, pl.ds(at, 128)] = jnp.sum(dq.astype(F32), 0, keepdims=True)
        dvec_ref[3:4, pl.ds(at, 128)] = jnp.sum(dv.astype(F32), 0, keepdims=True)
    gn[...] += sum(dot_nt(gp_ref[0, j], w[...]) for j, w in enumerate((wq, wk, wv)))

    @pl.when(group == pl.num_programs(0) - 1)
    def _():
        grad = gn[...]
        xhat, rstd = normalise(x_ref[0].astype(F32))
        dvec_ref[0:1] = jnp.sum(grad * xhat, 0, keepdims=True)
        dvec_ref[1:2] = jnp.sum(grad, 0, keepdims=True)
        res[0:rows] = ga_ref[0].astype(F32) + norm_backward(grad, row_of(n1g), xhat, rstd)
        repack(lay, res, 0, Image(lay, (rank_ref, split_ref, tag_ref), k), back)
        for j, ig_ref in enumerate(ig_refs):
            ig_ref[0] = back[j]


def call_backward(lay, k, per, meta, ga, qkv, prob, x, n1g, out_weight, qkv_weight, chain):
    rows, keys = lay.rows, lay.keys
    width = out_weight.shape[0]
    groups = width // GROUP
    alone = k == per - 1
    one = pl.BlockSpec((1, rows, width), lambda g: (k, 0, 0))
    args = [*meta, ga, qkv, prob, x, n1g, out_weight, qkv_weight, qkv_weight, qkv_weight]
    specs = [
        SMEM,
        SMEM,
        SMEM,
        one,
        pl.BlockSpec((1, 3, keys, GROUP), lambda g: (k, 0, 0, g)),
        pl.BlockSpec((1, HEADS // groups, rows, keys), lambda g: (k, g, 0, 0)),
        one,
        whole(n1g.shape),
        pl.BlockSpec((GROUP, width), lambda g: (g, 0)),
    ] + [pl.BlockSpec((width, GROUP), functools.partial(lambda j, g: (0, j * groups + g), j)) for j in range(3)]
    aliases = {}
    if chain is not None:
        count = 1 if alone else len(chain)
        aliases = {len(args) + i: i for i in range(count)}
        args += chain[:count]
        specs += [HBM] * count
    return pl.pallas_call(
        functools.partial(attention_backward, lay, k, len(args) - 12),
        grid=(groups,),
        in_specs=specs,
        out_specs=[
            pl.BlockSpec((1, 3, rows, GROUP), lambda g: (k, 0, 0, g)),
            *[pl.BlockSpec((1, lay.piece, width), lambda g: (0 if alone else k, 0, 0))] * lay.ranks,
            whole((8, width)),
        ],
        out_shape=[
            shaped((per, 3, rows, width), BF16),
            *[shaped((1 if alone else per - 1, lay.piece, width), BF16)] * lay.ranks,
            shaped((8, width), F32),
        ],
        scratch_shapes=[
            pltpu.VMEM((rows, width), F32),
            pltpu.VMEM((rows + lay.spare, width), F32),
            pltpu.VMEM((lay.ranks, lay.piece, width), BF16),
        ],
        input_output_aliases=aliases,
        compiler_params=params(),
        cost_estimate=cost(10e9, 10e6),
    )(*args)


def assemble(lay, rank_ref, split_ref, tag_ref, *refs):
    *got, passed_ref, out_ref = refs
    images, slots, width = out_ref.shape
    row = lax.broadcasted_iota(jnp.int32, (slots, width), 0)
    rank = rank_ref[0]
    first = 0
    for b in range(0, len(got), lay.ranks):
        for j, piece in enumerate(got[b : b + lay.ranks]):
            for k in range(piece.shape[0]):
                owner = rank ^ j
                image = jnp.minimum(owner * lay.per, images - lay.per) + first + k
                live = jnp.where(tag_ref[image] < lay.groups, split_ref[image, rank] * GRID, 0)

                @pl.when(image >= owner * lay.per)
                def _():
                    worked = piece[k][:slots].astype(F32)
                    kept = passed_ref[image].astype(F32)
                    out_ref[image] = jnp.where(row < live, worked, kept).astype(BF16)

        first += got[b].shape[0]


def call_assemble(lay, meta, got, passed):
    args = [*meta, *got, passed]
    return pl.pallas_call(
        functools.partial(assemble, lay),
        in_specs=[SMEM] * 3 + [VMEM] * len(args[3:]),
        out_specs=VMEM,
        out_shape=shaped(passed.shape, BF16),
        compiler_params=params(SMALL_LIMIT),
        cost_estimate=cost(0, 5e6),
    )(*args)


class Part:
    def __init__(self, own, send, order, at=None):
        self.own, self.send, self.order = own, send, ["core", *order]
        self.got = self.sent = None
        self.at = at
        self.pending = None


def exchange(parts):
    for p in parts:
        if p.send is None:
            continue
        axis, weight = BITS[p.order[0]]
        size = lax.axis_size(axis)
        p.got = lax.ppermute(p.send, axis, [(i, i ^ weight) for i in range(size)])
        p.sent, p.send = p.send, None


def add_and_split(counts, mine_ref, *refs):
    n = len(counts)
    for i in range(n):
        own, got, keep, send = refs[2 * i], refs[2 * i + 1], refs[2 * n + 2 * i], refs[2 * n + 2 * i + 1]
        mine = mine_ref[i]
        keep[...] = (own[mine].astype(F32) + got[mine].astype(F32)).astype(BF16)
        send[...] = (own[1 - mine].astype(F32) + got[1 - mine].astype(F32)).astype(BF16)


def bit_of(name):
    axis, weight = BITS[name]
    return (lax.axis_index(axis) // weight) % 2


def add_sent(mine_ref, *refs):
    n = len(refs) // 3
    for i in range(n):
        refs[2 * n + i][...] = (refs[2 * i][...].astype(F32) + refs[2 * i + 1][...].astype(F32)).astype(BF16)


def send_first(parts, steps=2):
    args, ins, outs, shapes = [], [], [], []
    mine = jnp.stack([bit_of(p.order[1]) for p in parts])
    for i, p in enumerate(parts):
        n, width = p.own.shape[-2:]
        many = 2 ** (len(p.order) - 2)
        pair = [v.reshape(2, many, n, width) for v in (p.own, p.got)]
        args += pair
        place = functools.partial(lambda part, step, mine: (1 - mine[part], step, 0, 0), i)
        ins += [pl.BlockSpec((None, many // steps, n, width), place)] * 2
        outs.append(pl.BlockSpec((many // steps, n, width), lambda step, mine: (step, 0, 0)))
        shapes.append(shaped((many, n, width), BF16))
        p.pending = pair
    sends = pl.pallas_call(
        add_sent,
        grid_spec=pltpu.PrefetchScalarGridSpec(
            num_scalar_prefetch=1, grid=(steps,), in_specs=ins, out_specs=outs
        ),
        out_shape=shapes,
        compiler_params=params(),
        cost_estimate=cost(0, 10e6),
    )(mine, *args)
    for p, send in zip(parts, sends):
        p.order.pop(0)
        p.send = send.reshape(*[2] * (len(p.order) - 1), *send.shape[-2:])
        p.own = p.got = None


def add_three(n, bits_ref, *refs):
    for i in range(n):
        terms, keep, send = refs[3 * i : 3 * i + 3], refs[3 * n + 2 * i], refs[3 * n + 2 * i + 1]
        mine = bits_ref[n + i]
        keep[...] = sum(t[mine].astype(F32) for t in terms).astype(BF16)
        send[...] = sum(t[1 - mine].astype(F32) for t in terms).astype(BF16)


def combine_pending(parts, before, steps=2):
    tied, _ = lax.optimization_barrier(([(p.pending, p.got) for p in parts], before))
    bits = jnp.stack([bit_of(p.order[0]) for p in parts] + [bit_of(p.order[1]) for p in parts])
    args, ins, outs, shapes = [], [], [], []
    for i, (p, (pair, got)) in enumerate(zip(parts, tied)):
        n, width = pair[0].shape[-2:]
        many = pair[0].shape[1] // 2
        args += [v.reshape(2, 2, many, n, width) for v in pair] + [got.reshape(2, many, n, width)]
        place = functools.partial(lambda part, step, bits: (bits[part], 0, step, 0, 0), i)
        ins += [pl.BlockSpec((None, 2, many // steps, n, width), place)] * 2
        ins.append(pl.BlockSpec((2, many // steps, n, width), lambda step, bits: (0, step, 0, 0)))
        outs += [pl.BlockSpec((many // steps, n, width), lambda step, bits: (step, 0, 0))] * 2
        shapes += [shaped((many, n, width), BF16)] * 2
    res = pl.pallas_call(
        functools.partial(add_three, len(parts)),
        grid_spec=pltpu.PrefetchScalarGridSpec(
            num_scalar_prefetch=1, grid=(steps,), in_specs=ins, out_specs=outs
        ),
        out_shape=shapes,
        compiler_params=params(),
        cost_estimate=cost(0, 10e6),
    )(bits, *args)
    for i, p in enumerate(parts):
        p.order.pop(0)
        lead = [2] * (len(p.order) - 1)
        p.own, p.send = [v.reshape(*lead, *v.shape[-2:]) for v in res[2 * i : 2 * i + 2]]
        p.got = p.pending = None
    return res[0]


def combine(parts, before=()):
    parts = [p for p in parts if p.got is not None]
    if parts and parts[0].pending:
        return combine_pending(parts, before)
    last = [p for p in parts if len(p.order) == 1]
    for p in last:
        p.own = p.own.astype(F32) + p.got.astype(F32)
        p.got = p.send = None
        p.order = []
    parts = [p for p in parts if p.order]
    if not parts:
        return ()
    tied, _ = lax.optimization_barrier(([(p.own, p.got) for p in parts], before))
    for p, (p.own, p.got) in zip(parts, tied):
        pass
    views = []
    for p in parts:
        shape = p.own.shape
        flat = (2, 2 ** (len(p.order) - 2), *shape[-2:])
        if p.at is not None:
            flat = (shape[0], *flat)
        views.append((p.own.reshape(flat), p.got.reshape(flat)))
    size = sum(4 * v[0].size for v in views)
    steps = min(4 if size > 9e6 else 1, *(v[0].shape[-3] for v in views))
    ins, outs, shapes, args, mine = [], [], [], [], []
    for p, (own, got) in zip(parts, views):
        many, n, width = own.shape[-3:]
        block = (2, many // steps, n, width)
        if steps == 1:
            ins += [VMEM] * 2
            outs += [VMEM] * 2
            shapes += [shaped((many, n, width), BF16)] * 2
        elif p.at is None:
            ins += [pl.BlockSpec(block, lambda i: (0, i, 0, 0))] * 2
        else:
            ins += [pl.BlockSpec((None, *block), functools.partial(lambda a, i: (a, 0, i, 0, 0), p.at))] * 2
        if steps > 1:
            outs += [pl.BlockSpec(block[1:], lambda i: (i, 0, 0))] * 2
            shapes += [shaped((many, n, width), BF16)] * 2
        args += [own, got]
        axis, weight = BITS[p.order[1]]
        mine.append((lax.axis_index(axis) // weight) % 2)
    moved = sum(3 * a.size for a in args)
    res = pl.pallas_call(
        functools.partial(add_and_split, [None] * len(parts)),
        **({"grid": (steps,)} if steps > 1 else {}),
        in_specs=[SMEM] + ins,
        out_specs=outs,
        out_shape=shapes,
        compiler_params=params() if steps > 1 else params(SMALL_LIMIT),
        cost_estimate=cost(0, moved),
    )(jnp.stack(mine), *args)
    for i, p in enumerate(parts):
        shape = (*[2] * (len(p.order) - 2), *p.own.shape[-2:])
        p.at = None
        p.own, p.send = res[2 * i].reshape(shape), res[2 * i + 1].reshape(shape)
        p.got = None
        p.order.pop(0)
    return res[0]


def add_and_fan(heights, z_ref, *refs):
    ins, outs = refs[: 2 * len(heights)], refs[2 * len(heights) :]
    at = 0
    for i, n in enumerate(heights):
        own, got = ins[2 * i], ins[2 * i + 1]
        for j, out in enumerate(outs):
            place = (z_ref[0] % 2) ^ (j % 2), (z_ref[0] // 2) ^ (j // 2)
            total = own[place].astype(F32) + got[place].astype(F32)
            out[at : at + n, :] = total.astype(out.dtype)
        at += n


def fan(parts, before):
    tied, _ = lax.optimization_barrier(([(p.own, p.got) for p in parts], before))
    args = [a for pair in tied for a in pair]
    heights = [p.own.shape[2] for p in parts]
    width = args[0].shape[-1]
    z = lax.axis_index("dp") // 2
    shape = (sum(heights), width)
    own, *sends = pl.pallas_call(
        functools.partial(add_and_fan, heights),
        in_specs=[SMEM] + [VMEM] * len(args),
        out_specs=[VMEM] * 4,
        out_shape=[shaped(shape, F32)] + [shaped(shape, BF16)] * 3,
        compiler_params=params(SMALL_LIMIT),
        cost_estimate=cost(0, 1e6),
    )(z[None], *args)
    size = lax.axis_size("dp")
    got = [lax.ppermute(v, "dp", [(i, i ^ (2 * j)) for i in range(size)]) for j, v in zip((1, 2, 3), sends)]
    return own, sends, got


def wait(values, parts):
    live = [p for p in parts if p.got is not None]
    values, gots = lax.optimization_barrier((values, [p.got for p in live]))
    for p, g in zip(live, gots):
        p.got = g
    return values


def after(values, parts):
    return lax.optimization_barrier((values, [p.sent for p in parts if p.sent is not None]))[0]


def small_sum(value, n_dp, n_seq):
    for axis, size in (("seq", n_seq), ("dp", n_dp)):
        dim = 1 if axis == "seq" else 0
        weight = 1
        place = lax.axis_index(axis)
        while weight < size:
            shape = value.shape
            cut = value.reshape(*shape[:dim], shape[dim] // 2, 2, *shape[dim + 1 :])
            mine = (place // weight) % 2
            other = lax.dynamic_index_in_dim(cut, 1 - mine, dim + 1, keepdims=False)
            own = lax.dynamic_index_in_dim(cut, mine, dim + 1, keepdims=False)
            value = own + lax.ppermute(other, axis, [(i, i ^ weight) for i in range(size)])
            weight *= 2
    return value.reshape(-1)


def per_device(
    tokens,
    key_mask,
    row_split,
    group_tags,
    norm1_gain,
    norm1_shift,
    qkv_weight,
    query_bias,
    value_bias,
    out_weight,
    out_bias,
    norm2_gain,
    norm2_shift,
    fc1_weight,
    fc1_bias,
    fc2_weight,
    fc2_bias,
    out_cotangent,
):
    images, slots, width = tokens.shape
    n_seq = lax.axis_size("seq")
    n_dp = lax.axis_size("dp")
    devices = n_dp * n_seq
    rank = lax.axis_index("seq")
    lay = Rows(n_seq, slots, images, n_dp)
    per, rows = lay.per, lay.rows
    meta = rank[None], row_split, group_tags
    all_rows = per * rows
    fast = (n_dp, n_seq) == (8, 4)

    def swap(value, j):
        return lax.ppermute(value, "seq", [(i, i ^ j) for i in range(n_seq)])

    def cut_for(array, k, count):
        starts = [jnp.minimum((rank ^ j) * per, images - per) + k for j in range(n_seq)]
        return [lax.dynamic_slice_in_dim(array, at, count, 0) for at in starts]

    def bring(mine):
        return [mine[0]] + [swap(mine[j], j) for j in range(1, n_seq)]

    vecs = (norm1_gain, norm1_shift, out_bias, norm2_gain, norm2_shift, query_bias, value_bias)

    first, rest = cut_for(tokens, 0, 1), cut_for(tokens, 1, per - 1)
    cot = cut_for(out_cotangent, 0, per)
    first = bring(first)
    first, rest = lax.optimization_barrier((first, rest))
    chain = call_forward(lay, 0, 1, meta, first, key_mask, vecs, qkv_weight, out_weight, None)
    rest = bring(rest)
    chain, rest, cot = lax.optimization_barrier((chain, rest, cot))
    chain = call_forward(lay, 1, per - 1, meta, rest, key_mask, vecs, qkv_weight, out_weight, chain)
    hidden, x_all, normed_all, mixed_all, n2, qkv, prob = chain
    n2 = n2.reshape(all_rows, width)

    cot = bring(cot)
    res = call_feed(
        lay,
        per,
        fast,
        meta,
        hidden,
        cot,
        n2,
        fc1_weight,
        fc1_bias.astype(F32)[None],
        fc2_weight,
        norm2_gain,
        fc2_bias,
        mixed_all.reshape(all_rows, width),
    )
    out_pieces, (ga, db1, dvec2, *dw) = list(res[:n_seq]), res[n_seq:]

    fc = late = []
    if fast:
        fc = [Part(*dw[:2], FC1_ORDER), Part(*dw[2:], FC2_ORDER)]
    out_got = [swap(out_pieces[j], j) for j in range(2, n_seq)]
    exchange(fc)
    ga = ga.reshape(per, rows, width)

    chain = None
    dvecs, ig, ig_got = [], [], []
    for k in range(per):
        *chain, dvec = call_backward(
            lay, k, per, meta, ga, qkv, prob, x_all, norm1_gain, out_weight, qkv_weight, chain
        )
        dvecs.append(dvec)
        if k == 0:
            chain, out_got[0] = lax.optimization_barrier((chain, out_got[0]))
        if k == 1:
            chain, out_got, out_pieces = lax.optimization_barrier((chain, out_got, out_pieces))
            out_got = [out_pieces[0], swap(out_pieces[1], 1), *out_got]
        if k == 2:
            chain, ig_got[0] = lax.optimization_barrier((chain, ig_got[0]))
        if k >= per - 2:
            ig.append(chain[1:3])
            ig_got.append([swap(chain[1 + j], j) for j in range(2, n_seq)])
        if k != 1:
            chain = wait(chain, fc)
            if fast and k == 0:
                send_first(fc)
            else:
                combine(fc)
            exchange(fc)
            ga, chain = after((ga, chain), fc)
    gp = chain[0]
    dwl = call_late_sums(fast, meta[0], gp, normed_all.reshape(all_rows, width), dvec2, db1, dvecs)
    if fast:
        dwl, ig_got[1] = wait((dwl, ig_got[1]), fc)
        late = [Part(dwl[i], dwl[2 + i], order) for i, order in enumerate(LATE_ORDERS)]
        exchange(late)
        token = combine(fc, dwl)
        exchange(fc)
        token = combine(late, token)
        exchange(late)
        out_got, ig, _ = lax.optimization_barrier((out_got, ig, token))
    output = call_assemble(lay, meta, out_got, tokens)
    if fast:
        token = combine(late, output)
        exchange(late)
        token = combine(fc, token)
        exchange(fc)
        ig = after(ig, late)
    ig_got = [g for near, far in zip(ig, ig_got) for g in (near[0], swap(near[1], 1), *far)]
    if fast:
        own, sends, got = fan(late, token)
        ig_got, _ = lax.optimization_barrier((ig_got, sends))
    input_grad = call_assemble(lay, meta, ig_got, out_cotangent)
    if fast:
        input_grad, fc[0].got, fc[1].got = lax.optimization_barrier((input_grad, fc[0].got, fc[1].got))
        combine(fc)
        inner = fc1_weight.shape[1]
        done = fc[0].own.T, fc[1].own[:, :inner].T, fc[1].own[:, inner:].T
        done, got = lax.optimization_barrier((done, got))
        late_sum = own + sum(g.astype(F32) for g in got)

    part = width // devices
    inner = fc1_weight.shape[1]
    if fast:
        qkv_sum, small = late_sum[: 3 * part], late_sum[3 * part]
        small_late, small_early = small[: 4 * part], small[4 * part :]
    else:
        *done, qkv_sum = [
            lax.psum_scatter(v.astype(F32), ("dp", "seq"), scatter_dimension=0, tiled=True)
            for v in (dw[0], dw[1][:, :inner], dw[1][:, inner:], dwl[0])
        ]
        done = [v.T for v in done]
        dvec1 = sum(dvecs)

        def by_device(v):
            return v.reshape(n_dp, n_seq, v.shape[0] // devices)

        early = (dvec2[2], dvec2[0], dvec2[1], dvec2[3], db1[0])
        small_early = small_sum(jnp.concatenate([by_device(v) for v in early], -1), n_dp, n_seq)
        small_late = small_sum(jnp.concatenate([by_device(dvec1[i]) for i in range(4)], -1), n_dp, n_seq)
    vec = [small_late[i * part : (i + 1) * part] for i in range(4)]
    vec += [small_early[i * part : (i + 1) * part] for i in range(4)]
    vec.append(small_early[4 * part : 4 * part + fc1_bias.shape[0] // devices])
    return (
        output,
        input_grad,
        vec[0],
        vec[1],
        qkv_sum.T,
        vec[2],
        vec[3],
        done[2],
        vec[4],
        vec[5],
        vec[6],
        done[0],
        vec[8],
        done[1],
        vec[7],
    )


def solution(mesh):
    rows = P("dp", "seq", None)
    split = P(("dp", "seq"))
    columns = P(None, ("dp", "seq"))
    return jax.shard_map(
        per_device,
        mesh=mesh,
        in_specs=(rows, P("dp", None), P("dp", None), P("dp")) + (P(),) * 13 + (rows,),
        out_specs=(
            rows,
            rows,
            split,
            split,
            columns,
            split,
            split,
            columns,
            split,
            split,
            split,
            columns,
            split,
            columns,
            split,
        ),
        check_vma=False,
    )
```
